128 devices in a mesh: lat: 16 (over z, x), chan: 8 (over y, core).
Axes of the slice: x: 4, y: 4, z: 4, core: 2. Of those that a mesh axis runs over, the one named last changes fastest.
Arguments:
- probe_field: bfloat16 [2, 384, 384, 1024], P(None, 'lat', 'chan'), may hold values from -6 to 6
- gate_slope: bfloat16 [384, 768, 1024], P('lat', None, 'chan'), may hold values from -0.099609375 to 1.09375
- spectral_filter: float32 [384, 384], P(None, 'chan'), may hold values from -4 to 4
- weight_in: bfloat16 [384, 768], replicated, may hold values from -0.3125 to 0.3125
- weight_out: bfloat16 [768, 384], replicated, may hold values from -0.21875 to 0.21875
- weight_flux: bfloat16 [384, 4], replicated, may hold values from -0.3125 to 0.3125
- send_cells: int32 [128, 16, 128], P(('lat', 'chan')), may hold values from 0 to 3071
- recv_slots: int32 [128, 4, 2048], P(('lat', 'chan')), may hold values from 0 to 2047
- recv_weights: float32 [128, 4, 2048], P(('lat', 'chan')), may hold values from 0.1 to 0.5
- ocean_probe: bfloat16 [2, 200, 128, 2048], P(None, None, 'lat', 'chan'), may hold values from -6 to 6
- ocean_mask: int32 [128, 2048], P('lat', 'chan'), may hold values 0 or 1
- coupling: bfloat16 [4, 200], replicated, may hold values from -3 to 3
- base_fine: bfloat16 [200, 128, 2048], P(None, 'lat', 'chan'), may hold values from -5 to 5
- sigma_fine: float32 [128, 2048], P('lat', 'chan'), may hold values from 0.5 to 2
- slope_fine: bfloat16 [800, 128, 2048], P(None, 'lat', 'chan'), may hold values from -0.099609375 to 1.09375
- gain_fine: float32 [200], replicated, may hold values from 0.1 to 1.9
- kernel_fine: float32 [200, 49], replicated, may hold values from -0.875 to 0.875
- expand_fine: bfloat16 [200, 800], replicated, may hold values from -0.4375 to 0.4375
- shrink_fine: bfloat16 [800, 200], replicated, may hold values from -0.21875 to 0.21875
- down_proj: bfloat16 [200, 250], replicated, may hold values from -0.4375 to 0.4375
- base_coarse: bfloat16 [250, 64, 1024], P(None, 'lat', 'chan'), may hold values from -5 to 5
- sigma_coarse: float32 [64, 1024], P('lat', 'chan'), may hold values from 0.5 to 2
- slope_coarse: bfloat16 [1000, 64, 1024], P(None, 'lat', 'chan'), may hold values from -0.099609375 to 1.09375
- gain_coarse: float32 [250], replicated, may hold values from 0.1 to 1.9
- kernel_coarse: float32 [250, 49], replicated, may hold values from -0.875 to 0.875
- expand_coarse: bfloat16 [250, 1000], replicated, may hold values from -0.375 to 0.375
- shrink_coarse: bfloat16 [1000, 250], replicated, may hold values from -0.1875 to 0.1875
- up_proj: bfloat16 [250, 200], replicated, may hold values from -0.375 to 0.375
Outputs:
- atmos_out: bfloat16 [2, 384, 384, 1024], P(None, 'lat', 'chan')
- ocean_out: bfloat16 [2, 200, 128, 2048], P(None, None, 'lat', 'chan')
The draws below stay inside these ranges and needn't reach their ends.
Inputs may be any that keep to these rules, and one draw needn't show every extreme that they name: `send_cells`: local cell numbers of a flux tile of 24 by 128 cells. `recv_slots`: slot numbers into the 16 times 128 received cells.
All inputs are finite; a program needn't handle non-finite values. No bound on the sum of `ocean_mask` on one device may be relied on, other than what follows from the above.
Results may differ from the reference program's by a relative error of at most 0.023.
Values may be sent and summed in bfloat16 or wider, within the bound.
A program may use at most 192 MiB of HBM per device.

```python
import math
import jax
import jax.numpy as jnp
from jax import lax

PROBES = 2
NLAT = 384
NLON = 1024
C = 384
HID = 768
FLUX = 4
CAP = 128
KSRC = 4
OY = 8
OX = 256
OCH1 = 200
OCH2 = 250
LAT_DEV = 24
LON_DEV = 128
OYT = 128
OXT = 2048
OCELLS = 2048
N_LAT = 16
N_CHAN = 8


def plant(drawn, own_key, low, largest):
    longest = drawn.shape.index(max(drawn.shape))
    spots = []
    for shift in (0, 1):
        where = [jax.random.randint(jax.random.fold_in(own_key, axis), (), 0, length) for axis, length in enumerate(drawn.shape)]
        where[longest] = (where[longest] + shift) % drawn.shape[longest]
        spots.append(tuple(where))
    return drawn.at[spots[0]].set(low).at[spots[1]].set(largest)


def shard_levels(rng, shape, cuts, smallest, high):
    loudness = 1.0
    for dim, blocks in cuts:
        steps = jax.random.uniform(jax.random.fold_in(jax.random.fold_in(rng, 6), dim), (blocks,), jnp.float32, smallest / len(cuts), high / len(cuts))
        loudness = loudness * jnp.repeat(jnp.exp(steps), shape[dim] // blocks).reshape((-1,) + (1,) * (len(shape) - 1 - dim))
    return loudness


def scatter_about(rng, dims, scale, limit, split=(), kind=jnp.bfloat16):
    entries = scale * jax.random.normal(rng, dims, jnp.float32)
    if split:
        entries = entries * shard_levels(rng, dims, split, -0.22, 0.18)
    return jnp.clip(entries, -limit, limit).astype(kind)


def setup_inputs(seed: int = 0) -> dict:
    keys = jax.random.split(jax.random.key(seed), 29)
    return {
        "probe_field": scatter_about(keys[0], (PROBES, NLAT, C, NLON), 1.0, 6.0, ((1, 16), (2, 8))),
        "gate_slope": jnp.clip(-0.099609375 + 1.1933594 * jax.random.uniform(keys[1], (NLAT, HID, NLON), jnp.float32) ** shard_levels(keys[1], (NLAT, HID, NLON), ((0, 16), (2, 8)), -0.2, 0.2), -0.099609375, 1.09375).astype(jnp.bfloat16),
        "spectral_filter": scatter_about(keys[2], (NLAT, C), 1.0, 4.0, ((1, 8),), jnp.float32),
        "weight_in": scatter_about(keys[3], (C, HID), C ** -0.5, 0.3125),
        "weight_out": scatter_about(keys[4], (HID, C), HID ** -0.5, 0.21875),
        "weight_flux": scatter_about(keys[5], (C, FLUX), C ** -0.5, 0.3125),
        "send_cells": plant(jax.random.randint(keys[6], (N_LAT * N_CHAN, N_LAT, CAP), 0, LAT_DEV * LON_DEV), jax.random.fold_in(keys[6], 1), 0, (LAT_DEV * LON_DEV) - 1).astype(jnp.int32),
        "recv_slots": plant(jax.random.randint(keys[7], (N_LAT * N_CHAN, KSRC, OCELLS), 0, N_LAT * CAP), jax.random.fold_in(keys[7], 1), 0, (N_LAT * CAP) - 1).astype(jnp.int32),
        "recv_weights": jnp.clip(0.1 + 0.4 * jax.random.uniform(keys[8], (N_LAT * N_CHAN, KSRC, OCELLS), jnp.float32) ** shard_levels(keys[8], (N_LAT * N_CHAN, KSRC, OCELLS), ((0, 128),), -0.2, 0.2), 0.1, 0.5),
        "ocean_probe": scatter_about(keys[9], (PROBES, OCH1, OYT, OXT), 1.0, 6.0, ((2, 16), (3, 8))),
        "ocean_mask": plant((jax.random.randint(keys[10], (OYT, OXT), 0, 10) < 7).astype(jnp.int32), jax.random.fold_in(keys[10], 1), 0, 1),
        "coupling": scatter_about(keys[11], (FLUX, OCH1), FLUX ** -0.5, 3.0),
        "base_fine": scatter_about(keys[12], (OCH1, OYT, OXT), 1.0, 5.0, ((1, 16), (2, 8))),
        "sigma_fine": jnp.clip(jnp.exp(math.log(2.0) - 1.3862944 * jax.random.uniform(keys[13], (OYT, OXT), jnp.float32) ** shard_levels(keys[13], (OYT, OXT), ((0, 16), (1, 8)), -0.2, 0.2)), 0.5, 2.0),
        "slope_fine": jnp.clip(-0.099609375 + 1.1933594 * jax.random.uniform(keys[14], (4 * OCH1, OYT, OXT), jnp.float32) ** shard_levels(keys[14], (4 * OCH1, OYT, OXT), ((1, 16), (2, 8)), -0.2, 0.2), -0.099609375, 1.09375).astype(jnp.bfloat16),
        "gain_fine": jnp.clip(1.0 + 0.18 * jax.random.normal(keys[15], (OCH1,), jnp.float32), 0.1, 1.9),
        "kernel_fine": scatter_about(keys[16], (OCH1, 49), 49 ** -0.5, 0.875, (), jnp.float32),
        "expand_fine": scatter_about(keys[17], (OCH1, 4 * OCH1), OCH1 ** -0.5, 0.4375),
        "shrink_fine": scatter_about(keys[18], (4 * OCH1, OCH1), (4 * OCH1) ** -0.5, 0.21875),
        "down_proj": scatter_about(keys[19], (OCH1, OCH2), OCH1 ** -0.5, 0.4375),
        "base_coarse": scatter_about(keys[20], (OCH2, OYT // 2, OXT // 2), 1.0, 5.0, ((1, 16), (2, 8))),
        "sigma_coarse": jnp.clip(jnp.exp(math.log(2.0) - 1.3862944 * jax.random.uniform(keys[21], (OYT // 2, OXT // 2), jnp.float32) ** shard_levels(keys[21], (OYT // 2, OXT // 2), ((0, 16), (1, 8)), -0.2, 0.2)), 0.5, 2.0),
        "slope_coarse": jnp.clip(-0.099609375 + 1.1933594 * jax.random.uniform(keys[22], (4 * OCH2, OYT // 2, OXT // 2), jnp.float32) ** shard_levels(keys[22], (4 * OCH2, OYT // 2, OXT // 2), ((1, 16), (2, 8)), -0.2, 0.2), -0.099609375, 1.09375).astype(jnp.bfloat16),
        "gain_coarse": jnp.clip(1.0 + 0.18 * jax.random.normal(keys[23], (OCH2,), jnp.float32), 0.1, 1.9),
        "kernel_coarse": scatter_about(keys[24], (OCH2, 49), 49 ** -0.5, 0.875, (), jnp.float32),
        "expand_coarse": scatter_about(keys[25], (OCH2, 4 * OCH2), OCH2 ** -0.5, 0.375),
        "shrink_coarse": scatter_about(keys[26], (4 * OCH2, OCH2), (4 * OCH2) ** -0.5, 0.1875),
        "up_proj": scatter_about(keys[27], (OCH2, OCH1), OCH2 ** -0.5, 0.375),
    }


def fourier_tables(count):
    column = jnp.arange(count, dtype=jnp.int32)
    half = count // 2
    wave = jnp.where(column <= half, column, column - half)
    points = jnp.arange(count, dtype=jnp.int32)
    phase = (points[:, None] * wave[None, :]) % count
    angles = phase.astype(jnp.float32) * (2.0 * math.pi / count)
    basis = jnp.where((column <= half)[None, :], jnp.cos(angles), jnp.sin(angles))
    forward = (basis / count).astype(jnp.bfloat16)
    factor = jnp.where((column == 0) | (column == half), 1.0, 2.0).astype(jnp.float32)
    inverse = (basis.T * factor[:, None]).astype(jnp.bfloat16)
    return forward, inverse


def cosine_tables(count):
    degree = jnp.arange(count, dtype=jnp.int32)
    points = jnp.arange(count, dtype=jnp.int32)
    phase = (degree[None, :] * (2 * points[:, None] + 1)) % (4 * count)
    basis = jnp.cos(phase.astype(jnp.float32) * (math.pi / (2 * count)))
    forward = (basis / count).astype(jnp.bfloat16)
    factor = jnp.where(degree == 0, 1.0, 2.0).astype(jnp.float32)
    inverse = (basis.T * factor[:, None]).astype(jnp.bfloat16)
    return forward, inverse


def atmosphere_step(field, gate_slope, spectral_filter, weight_in, weight_out, weight_flux):
    fwd_lon, inv_lon = fourier_tables(NLON)
    fwd_lat, inv_lat = cosine_tables(NLAT)
    fourier = jnp.einsum('ncx,xk->nkc', field.astype(jnp.float32), fwd_lon.astype(jnp.float32)).astype(jnp.bfloat16)
    spectrum = jnp.einsum('nkc,nl->lkc', fourier.astype(jnp.float32), fwd_lat.astype(jnp.float32))
    filtered = (spectrum * spectral_filter[:, None, :]).astype(jnp.bfloat16)
    returned = jnp.einsum('lkc,ln->nkc', filtered.astype(jnp.float32), inv_lat.astype(jnp.float32)).astype(jnp.bfloat16)
    spatial = jnp.einsum('nkc,kx->ncx', returned.astype(jnp.float32), inv_lon.astype(jnp.float32))
    mixed = (field.astype(jnp.float32) + spatial).astype(jnp.bfloat16)

    def row_step(parts):
        mix_row, slope_row, field_row = parts
        hidden = jnp.dot(weight_in.T, mix_row, preferred_element_type=jnp.float32)
        gated = (slope_row.astype(jnp.float32) * hidden).astype(jnp.bfloat16)
        update = jnp.dot(weight_out.T, gated, preferred_element_type=jnp.float32).astype(jnp.bfloat16)
        result = field_row.astype(jnp.float32) + update.astype(jnp.float32)
        flux_row = jnp.dot(weight_flux.T.astype(jnp.float32), result, precision=lax.Precision.HIGHEST)
        return result.astype(jnp.bfloat16), flux_row.astype(jnp.bfloat16)

    output, flux = lax.map(row_step, (mixed, gate_slope, field))
    return output, jnp.transpose(flux, (1, 0, 2))


def route_fluxes(flux, send_cells, recv_slots, recv_weights):
    tiles = flux.reshape(PROBES, FLUX, N_LAT, LAT_DEV, N_CHAN, LON_DEV)
    tiles = tiles.transpose(2, 4, 0, 1, 3, 5).reshape(N_LAT * N_CHAN, PROBES, FLUX, LAT_DEV * LON_DEV)

    def pick(source, cells):
        return jnp.take(source, cells.reshape(-1), axis=2).reshape(PROBES, FLUX, N_LAT, CAP)

    sent = jax.vmap(pick)(tiles, send_cells).reshape(N_LAT, N_CHAN, PROBES, FLUX, N_LAT, CAP)
    received = sent.transpose(4, 1, 2, 3, 0, 5).reshape(N_LAT * N_CHAN, PROBES, FLUX, N_LAT * CAP)

    def combine(buffer, slot_ids, weights):
        taken = jnp.take(buffer, slot_ids.reshape(-1), axis=2).reshape(PROBES, FLUX, KSRC, OCELLS)
        return jnp.sum(taken.astype(jnp.float32) * weights[None, None], axis=2)

    ocean_flux = jax.vmap(combine)(received, recv_slots, recv_weights)
    ocean_flux = ocean_flux.reshape(N_LAT, N_CHAN, PROBES, FLUX, OY, OX).transpose(2, 3, 0, 4, 1, 5)
    return ocean_flux.reshape(PROBES, FLUX, OYT, OXT)


def depthwise(padded, kernel, rows, cols):
    total = jnp.zeros((padded.shape[0], padded.shape[1], rows, cols), jnp.float32)
    wide = padded.astype(jnp.float32)
    for offset in range(49):
        row_start = offset // 7
        col_start = offset % 7
        total = total + wide[:, :, row_start:row_start + rows, col_start:col_start + cols] * kernel[:, offset][None, :, None, None]
    return total


def level_tangent(field, base, sigma, slope, gain, kernel, expand, shrink, mask_values):
    rows = field.shape[2]
    cols = field.shape[3]
    padded = jnp.pad(field, ((0, 0), (0, 0), (3, 3), (3, 3)))
    spread = depthwise(padded, kernel, rows, cols)
    center = jnp.mean(spread, axis=1, keepdims=True)
    normed = base.astype(jnp.float32)[None]
    along = jnp.mean(normed * spread, axis=1, keepdims=True)
    tangent = (gain[None, :, None, None] * sigma[None, None] * (spread - center - normed * along)).astype(jnp.bfloat16)
    hidden = jnp.einsum('pqyx,qh->phyx', tangent.astype(jnp.float32), expand.astype(jnp.float32))
    gated = (slope.astype(jnp.float32)[None] * hidden).astype(jnp.bfloat16)
    output = jnp.einsum('phyx,hq->pqyx', gated.astype(jnp.float32), shrink.astype(jnp.float32))
    return ((field.astype(jnp.float32) + output) * mask_values).astype(jnp.bfloat16)


def reference(probe_field, gate_slope, spectral_filter, weight_in, weight_out, weight_flux, send_cells, recv_slots, recv_weights, ocean_probe, ocean_mask, coupling, base_fine, sigma_fine, slope_fine, gain_fine, kernel_fine, expand_fine, shrink_fine, down_proj, base_coarse, sigma_coarse, slope_coarse, gain_coarse, kernel_coarse, expand_coarse, shrink_coarse, up_proj):
    def probe_step(field):
        return atmosphere_step(field, gate_slope, spectral_filter, weight_in, weight_out, weight_flux)

    atmos_out, flux = lax.map(probe_step, probe_field)
    ocean_flux = route_fluxes(flux, send_cells, recv_slots, recv_weights)
    mask_values = ocean_mask.astype(jnp.float32)

    def ocean_step(pair):
        probe_one = pair[0][None]
        flux_one = pair[1][None]
        forcing = jnp.einsum('pfyx,fq->pqyx', flux_one, coupling.astype(jnp.float32), precision=lax.Precision.HIGHEST)
        start_field = ((probe_one.astype(jnp.float32) + forcing) * mask_values).astype(jnp.bfloat16)
        level_one = level_tangent(start_field, base_fine, sigma_fine, slope_fine, gain_fine, kernel_fine, expand_fine, shrink_fine, mask_values)
        shaped = level_one.astype(jnp.float32).reshape(1, OCH1, OYT // 2, 2, OXT // 2, 2)
        pooled = jnp.mean(shaped, axis=(3, 5))
        coarse_field = jnp.einsum('pqyx,qr->pryx', pooled, down_proj.astype(jnp.float32), precision=lax.Precision.HIGHEST).astype(jnp.bfloat16)
        level_two = level_tangent(coarse_field, base_coarse, sigma_coarse, slope_coarse, gain_coarse, kernel_coarse, expand_coarse, shrink_coarse, 1.0)
        raised = jnp.einsum('pryx,rq->pqyx', level_two.astype(jnp.float32), up_proj.astype(jnp.float32))
        upsampled = jnp.repeat(jnp.repeat(raised, 2, axis=2), 2, axis=3)
        return ((level_one.astype(jnp.float32) + upsampled) * mask_values).astype(jnp.bfloat16)[0]

    ocean_out = lax.map(ocean_step, (ocean_probe, ocean_flux))
    return atmos_out, ocean_out
```

```python
import functools
import math

import jax
import jax.numpy as jnp
from jax import lax
from jax.experimental import pallas as pl
from jax.experimental.pallas import tpu as pltpu
from jax.sharding import PartitionSpec as P

F32 = jnp.float32
BF16 = jnp.bfloat16
VMEM_LIMIT = 56 * 1024 * 1024


def params(**more):
    return pltpu.CompilerParams(vmem_limit_bytes=VMEM_LIMIT, **more)


def cost(flops, nbytes):
    return pl.CostEstimate(flops=int(flops), bytes_accessed=int(nbytes), transcendentals=0)


def mm(a, b):
    return jnp.dot(a, b, preferred_element_type=F32)


def whole(shape):
    zeros = (0,) * len(shape)
    return pl.BlockSpec(shape, lambda *_: zeros)


def fourier_tables(count):
    column = jnp.arange(count, dtype=jnp.int32)
    half = count // 2
    wave = jnp.where(column <= half, column, column - half)
    points = jnp.arange(count, dtype=jnp.int32)
    phase = points[:, None] * wave[None, :] % count
    angles = phase.astype(F32) * (2.0 * math.pi / count)
    basis = jnp.where((column <= half)[None, :], jnp.cos(angles), jnp.sin(angles))
    forward = (basis / count).astype(BF16)
    factor = jnp.where((column == 0) | (column == half), 1.0, 2.0).astype(F32)
    inverse = (basis.T * factor[:, None]).astype(BF16)
    return (forward, inverse)


def cosine_tables(count):
    degree = jnp.arange(count, dtype=jnp.int32)
    points = jnp.arange(count, dtype=jnp.int32)
    phase = degree[None, :] * (2 * points[:, None] + 1) % (4 * count)
    basis = jnp.cos(phase.astype(F32) * (math.pi / (2 * count)))
    forward = (basis / count).astype(BF16)
    factor = jnp.where(degree == 0, 1.0, 2.0).astype(F32)
    inverse = (basis.T * factor[:, None]).astype(BF16)
    return (forward, inverse)


def turn_kernel(in_ref, out_ref, wide):
    rows, chans, lanes = in_ref.shape
    wide[...] = in_ref[...].astype(F32).reshape(rows * chans, lanes)
    for c in range(chans):
        out_ref[c] = wide[pl.ds(c, rows, stride=chans), :].astype(BF16)


def turn_channels(field):
    rows, chans, lons = field.shape
    return pl.pallas_call(
        turn_kernel,
        grid=(lons // 128,),
        in_specs=[pl.BlockSpec((rows, chans, 128), lambda i: (0, 0, i))],
        out_specs=pl.BlockSpec((chans, rows, 128), lambda i: (0, 0, i)),
        out_shape=jax.ShapeDtypeStruct((chans, rows, lons), BF16),
        scratch_shapes=[pltpu.VMEM((rows * chans, 128), F32)],
        compiler_params=params(),
        cost_estimate=cost(0, 4 * field.size),
        name="turn_channels",
    )(field)


def probe_flux_kernel(probe_ref, weight_ref, out_ref):
    weight = weight_ref[...]
    rows = probe_ref.shape[1]
    for n in range(0, rows, 2):
        pair = [
            mm(weight, jnp.concatenate([probe_ref[0, m], probe_ref[1, m]], axis=0))
            for m in (n, n + 1)
        ]
        both = jnp.concatenate(pair, axis=0).astype(BF16)
        for j in range(out_ref.shape[0]):
            out_ref[j, n * 8 : n * 8 + 16, :] = both[:, j * 128 : (j + 1) * 128]


def probe_flux(probe, weight):
    probes, rows, chans, lons = probe.shape
    blocks = lons // 128
    step = 4
    return pl.pallas_call(
        probe_flux_kernel,
        grid=(rows // step,),
        in_specs=[
            pl.BlockSpec((probes, step, chans, lons), lambda i: (0, i, 0, 0)),
            whole(weight.shape),
        ],
        out_specs=pl.BlockSpec((blocks, step * 8, 128), lambda i: (0, i, 0)),
        out_shape=jax.ShapeDtypeStruct((blocks, rows * 8, 128), BF16),
        compiler_params=params(),
        cost_estimate=cost(2 * 8 * probe.size, 2 * probe.size),
        name="probe_flux",
    )(probe, weight)


def filter_kernel(in_ref, fwd_ref, inv_ref, filt_ref, diff_ref, out_ref, wide, back):
    bands, _, pair, lons = in_ref.shape
    rows = pair // 2
    blocks = out_ref.shape[1]

    def load(b, carry):
        piece = in_ref[b, 0].astype(F32)
        at = pl.ds(pl.multiple_of(b * rows, 8), rows)
        wide[at, 0:lons] = piece[0:rows]
        wide[at, lons : 2 * lons] = piece[rows:pair]
        return carry

    lax.fori_loop(0, bands, load, 0)
    fwd = fwd_ref[...]
    inv = inv_ref[...]
    filt = filt_ref[0]
    chunk = 512

    def lat_filter(t, carry):
        at = pl.ds(pl.multiple_of(t * chunk, chunk), chunk)
        value = wide[:, at]
        filtered = (mm(fwd, value.astype(BF16)) * filt).astype(BF16)
        returned = mm(inv, filtered)
        back[:, at] = returned.astype(BF16)
        wide[:, at] = value + returned
        return carry

    lax.fori_loop(0, 2 * lons // chunk, lat_filter, 0)
    for p in range(2):
        for t in range(lons // 256):
            at = slice(p * lons + t * 256, p * lons + (t + 1) * 256)
            wide[:, at] = wide[:, at] + mm(
                back[:, p * lons : (p + 1) * lons], diff_ref[:, t * 256 : (t + 1) * 256]
            )

    def store(b, carry):
        at = pl.ds(pl.multiple_of(b * rows, 8), rows)
        for j in range(blocks):
            cols = slice(j * 128, (j + 1) * 128)
            more = slice(lons + j * 128, lons + (j + 1) * 128)
            out_ref[b, j, 0] = jnp.concatenate([wide[at, cols], wide[at, more]], axis=0).astype(
                BF16
            )
        return carry

    lax.fori_loop(0, bands, store, 0)


def lat_filter(received, fwd, inv, filt, diff):
    bands, chans, pair, lons = received.shape
    lats = fwd.shape[0]
    blocks = lons // 128
    return pl.pallas_call(
        filter_kernel,
        grid=(chans,),
        in_specs=[
            pl.BlockSpec((bands, 1, pair, lons), lambda i: (0, i, 0, 0)),
            whole(fwd.shape),
            whole(inv.shape),
            pl.BlockSpec((1, lats, 1), lambda i: (i, 0, 0)),
            whole(diff.shape),
        ],
        out_specs=pl.BlockSpec((bands, blocks, 1, pair, 128), lambda i: (0, 0, i, 0, 0)),
        out_shape=jax.ShapeDtypeStruct((bands, blocks, chans, pair, 128), BF16),
        scratch_shapes=[pltpu.VMEM((lats, 2 * lons), F32), pltpu.VMEM((lats, 2 * lons), BF16)],
        compiler_params=params(),
        cost_estimate=cost(8.4e9, 4 * received.size),
        name="lat_filter",
    )(received, fwd, inv, filt, diff)


def point_kernel(
    mixed_ref, slope_ref, win_ref, wout_ref, pflux_ref, cells_ref, out_ref, picked_ref, wide, flux
):
    chans, pair, lanes = mixed_ref.shape
    rows = pair // 2
    step = pl.program_id(0)

    @pl.when(step == 0)
    def _():
        def load(i, carry):
            at = pl.ds(pl.multiple_of(i * 8, 8), 8)
            wide[pl.ds(pl.multiple_of(i * 8 * pair, 8), 8 * pair), :] = (
                mixed_ref[at].astype(F32).reshape(8 * pair, lanes)
            )
            return carry

        lax.fori_loop(0, chans // 8, load, 0)

    value = jnp.concatenate(
        [wide[pl.ds(step + p * rows, chans, stride=pair), :] for p in range(2)], axis=1
    ).astype(BF16)
    slope = slope_ref[0].astype(F32)
    hidden = mm(win_ref[...], value)
    gated = (jnp.concatenate([slope, slope], axis=1) * hidden).astype(BF16)
    update = mm(wout_ref[...], gated)
    width = out_ref.shape[3]
    for j in range(out_ref.shape[0]):
        for p in range(2):
            out_ref[j, p, 0] = update[
                j * width : (j + 1) * width, p * lanes : (p + 1) * lanes
            ].astype(BF16)
    terms = update[chans : chans + 8]
    which = lax.broadcasted_iota(jnp.int32, (8, lanes), 0)
    flux[pl.ds(pl.multiple_of(step * 8, 8), 8), :] = jnp.where(
        which < 4, terms[:, 0:lanes], terms[:, lanes : 2 * lanes]
    )

    @pl.when(step == rows - 1)
    def _():
        total = flux[...]
        for j in range(pflux_ref.shape[0]):
            total = total + pflux_ref[j].astype(F32)
        total = total.astype(BF16)
        place = lax.broadcasted_iota(jnp.int32, (lanes, lanes), 0)
        for r in range(cells_ref.shape[0]):
            cells = cells_ref[r : r + 1, :]
            row = cells // lanes
            hot = jnp.where(place == cells - row * lanes, 1.0, 0.0).astype(BF16)
            found = mm(total, hot)
            picked = jnp.zeros((8, lanes), F32)
            for n in range(rows):
                picked = picked + jnp.where(row == n, found[n * 8 : (n + 1) * 8], 0.0)
            picked_ref[r] = picked


def pointwise(mixed, slope, win, wout, pflux, cells):
    chans, pair, lanes = mixed.shape
    rows, hid, _ = slope.shape
    blocks = pflux.shape[0]
    width = chans // blocks
    return pl.pallas_call(
        point_kernel,
        grid=(rows,),
        in_specs=[
            whole(mixed.shape),
            pl.BlockSpec((1, hid, lanes), lambda i: (i, 0, 0)),
            whole(win.shape),
            whole(wout.shape),
            whole(pflux.shape),
            whole(cells.shape),
        ],
        out_specs=[
            pl.BlockSpec((blocks, 2, 1, width, lanes), lambda i: (0, 0, i, 0, 0)),
            whole((cells.shape[0], 8, lanes)),
        ],
        out_shape=[
            jax.ShapeDtypeStruct((blocks, 2, rows, width, lanes), BF16),
            jax.ShapeDtypeStruct((cells.shape[0], 8, lanes), F32),
        ],
        scratch_shapes=[
            pltpu.VMEM((chans * pair, lanes), F32),
            pltpu.VMEM((rows * 8, lanes), F32),
        ],
        compiler_params=params(),
        cost_estimate=cost(7.3e9, 4 * mixed.size + 2 * slope.size),
        name="pointwise",
    )(mixed, slope, win, wout, pflux, cells)


def add_kernel(probe_ref, update_ref, out_ref):
    for j in range(update_ref.shape[0]):
        cols = slice(j * 128, (j + 1) * 128)
        out_ref[:, :, cols] = (
            probe_ref[:, :, cols].astype(F32) + update_ref[j].astype(F32)
        ).astype(BF16)


def add_update(probe, update):
    rows, chans, lons = probe.shape
    blocks = update.shape[0]
    step = 6
    return pl.pallas_call(
        add_kernel,
        grid=(rows // step,),
        in_specs=[
            pl.BlockSpec((step, chans, lons), lambda i: (i, 0, 0)),
            pl.BlockSpec((blocks, step, chans, 128), lambda i: (0, i, 0, 0)),
        ],
        out_specs=pl.BlockSpec((step, chans, lons), lambda i: (i, 0, 0)),
        out_shape=jax.ShapeDtypeStruct(probe.shape, BF16),
        compiler_params=params(),
        cost_estimate=cost(probe.size, 6 * probe.size),
        name="add_update",
    )(probe, update)


def depth_kernel(in_ref, kernel_ref, out_ref, wide):
    high, _, chans, broad = in_ref.shape
    rows = high - 6
    cols = broad - 6
    tiles = -(-chans // 8)
    for y in range(high):
        wide[y, 0:chans, 0:broad] = in_ref[y, 0].astype(F32)

    def tile(i, carry):
        at = pl.ds(pl.multiple_of(i * 8, 8), 8)
        weights = kernel_ref[at, :]
        total = [jnp.zeros((8, cols), F32) for _ in range(rows)]
        for b in range(7):
            taps = [
                jnp.broadcast_to(weights[:, 7 * a + b : 7 * a + b + 1], (8, cols))
                for a in range(7)
            ]
            for y in range(high):
                moved = wide[y, at, b : b + cols]
                for a in range(7):
                    if 0 <= y - a < rows:
                        total[y - a] = total[y - a] + moved * taps[a]
        for y in range(rows):
            out_ref[y, at, :] = total[y]
        return carry

    lax.fori_loop(0, tiles, tile, 0)


def depthwise(padded, kernel):
    high, probes, chans, broad = padded.shape
    rows, cols = high - 6, broad - 6
    full = -(-chans // 8) * 8
    kernel = jnp.pad(kernel, ((0, full - chans), (0, 0)))
    return pl.pallas_call(
        depth_kernel,
        grid=(probes,),
        in_specs=[
            pl.BlockSpec((high, 1, chans, broad), lambda p: (0, p, 0, 0)),
            whole(kernel.shape),
        ],
        out_specs=pl.BlockSpec((rows, full, cols), lambda p: (0, 0, p)),
        out_shape=jax.ShapeDtypeStruct((rows, full, probes * cols), F32),
        scratch_shapes=[pltpu.VMEM((high, full, -(-broad // 128) * 128), F32)],
        compiler_params=params(),
        cost_estimate=cost(200 * rows * cols * chans * probes, 4 * padded.size),
        name="depthwise",
    )(padded, kernel)


def combine_kernel(pool_ref, slots_ref, weights_ref, mask_ref, out_ref):
    bands, fields, cap = pool_ref.shape
    pool = pool_ref[...].reshape(bands * fields, cap).astype(BF16)
    rows, cols = mask_ref.shape
    place = lax.broadcasted_iota(jnp.int32, (cap, cols), 0)
    for y in range(rows):
        at = slice(y * cols, (y + 1) * cols)
        total = jnp.zeros((fields, cols), F32)
        for k in range(slots_ref.shape[0]):
            slots = slots_ref[k : k + 1, at]
            weights = weights_ref[k : k + 1, at]
            band = slots // cap
            hot = jnp.where(place == slots - band * cap, 1.0, 0.0).astype(BF16)
            found = mm(pool, hot)
            for b in range(bands):
                total = total + found[b * fields : (b + 1) * fields] * jnp.where(
                    band == b, weights, 0.0
                )
        out_ref[y] = total * mask_ref[y : y + 1, :]


def combine(pool, slots, weights, mask):
    fields = pool.shape[1]
    rows, cols = mask.shape
    return pl.pallas_call(
        combine_kernel,
        in_specs=[whole(a.shape) for a in (pool, slots, weights, mask)],
        out_specs=whole((rows, fields, cols)),
        out_shape=jax.ShapeDtypeStruct((rows, fields, cols), F32),
        compiler_params=params(),
        name="combine",
    )(pool, slots, weights, mask)


def normed_step(spread, base, sigma, gain):
    chans = spread.shape[0]
    wide_base = jnp.concatenate([base, base], axis=1)
    center = jnp.sum(spread, axis=0, keepdims=True) * (1.0 / chans)
    along = jnp.sum(wide_base * spread, axis=0, keepdims=True) * (1.0 / chans)
    scale = jnp.concatenate([sigma, sigma], axis=1)
    return (gain * scale * (spread - center - wide_base * along)).astype(BF16)


def fine_kernel(
    spread_ref,
    probe_ref,
    flux_ref,
    left_ref,
    right_ref,
    mask_ref,
    sigma_ref,
    base_ref,
    slope_ref,
    gain_ref,
    mix_ref,
    couple_ref,
    expand_ref,
    shrink_ref,
    pool_ref,
    down_ref,
    one_ref,
    coarse_ref,
    columns,
    held,
):
    step = pl.program_id(0)
    high = flux_ref.shape[0]
    cols = flux_ref.shape[2]

    @pl.when(step == 0)
    def _():
        for y in range(high):
            row = jnp.concatenate([left_ref[y], flux_ref[y], right_ref[y]], axis=1)
            for b in range(7):
                columns[(y * 7 + b) * 8 : (y * 7 + b + 1) * 8, :] = row[:, 125 + b : 125 + b + cols]

    near = columns[pl.ds(pl.multiple_of(step * 56, 8), 392), :].astype(BF16)
    center = columns[pl.ds(pl.multiple_of((step + 3) * 56 + 24, 8), 8), :].astype(BF16)
    spread = spread_ref[0] + jnp.concatenate([mm(mix_ref[p], near) for p in range(2)], axis=1)
    forcing = jnp.concatenate([mm(couple_ref[p], center) for p in range(2)], axis=1)
    start = (probe_ref[0].astype(F32) + forcing).astype(BF16).astype(F32)
    at = pl.ds(step, 1)
    tangent = normed_step(spread, base_ref[0].astype(F32), sigma_ref[at, :], gain_ref[...])
    slope = slope_ref[0].astype(F32)
    hidden = mm(expand_ref[...], tangent)
    gated = (hidden * jnp.concatenate([slope, slope], axis=1)).astype(BF16)
    mask = mask_ref[at, :]
    one = ((start + mm(shrink_ref[...], gated)) * jnp.concatenate([mask, mask], axis=1)).astype(BF16)
    one_ref[0] = one
    pooled = mm(one, pool_ref[...])

    @pl.when(step % 2 == 0)
    def _():
        held[...] = pooled

    @pl.when(step % 2 == 1)
    def _():
        coarse = mm(down_ref[...], (held[...] + pooled).astype(BF16)).astype(BF16)
        half = coarse.shape[1] // 2
        coarse_ref[0, 0] = coarse[:, 0:half]
        coarse_ref[0, 1] = coarse[:, half : 2 * half]


def fine_level(spread, probe, flux, left, right, mask, sigma, base, slope, gain, mix, couple, expand, shrink, pool, down):
    rows, chans, wide = spread.shape
    cols = wide // 2
    coarse = down.shape[0]
    row = lambda i: (i, 0, 0)
    return pl.pallas_call(
        fine_kernel,
        grid=(rows,),
        in_specs=[
            pl.BlockSpec((1, chans, wide), row),
            pl.BlockSpec((1, chans, wide), row),
            whole(flux.shape),
            whole(left.shape),
            whole(right.shape),
            whole(mask.shape),
            whole(sigma.shape),
            pl.BlockSpec((1, chans, cols), row),
            pl.BlockSpec((1, slope.shape[1], cols), row),
            whole(gain.shape),
            whole(mix.shape),
            whole(couple.shape),
            whole(expand.shape),
            whole(shrink.shape),
            whole(pool.shape),
            whole(down.shape),
        ],
        out_specs=[
            pl.BlockSpec((1, chans, wide), row),
            pl.BlockSpec((1, 2, coarse, cols // 2), lambda i: (i // 2, 0, 0, 0)),
        ],
        out_shape=[
            jax.ShapeDtypeStruct((rows, chans, wide), BF16),
            jax.ShapeDtypeStruct((rows // 2, 2, coarse, cols // 2), BF16),
        ],
        scratch_shapes=[
            pltpu.VMEM((flux.shape[0] * 56, cols), F32),
            pltpu.VMEM((chans, cols), F32),
        ],
        compiler_params=params(),
        name="fine_level",
    )(spread, probe, flux, left, right, mask, sigma, base, slope, gain, mix, couple, expand, shrink, pool, down)


def coarse_kernel(
    spread_ref,
    field_ref,
    sigma_ref,
    base_ref,
    slope_ref,
    gain_ref,
    expand_ref,
    shrink_ref,
    spreadout_ref,
    up_ref,
    one_ref,
    mask_ref,
    out_ref,
    wide,
):
    step = pl.program_id(0)
    chans = field_ref.shape[2]
    probes, fine, rows, cols = out_ref.shape
    field = jnp.concatenate([field_ref[0, 0], field_ref[0, 1]], axis=1).astype(F32)
    at = pl.ds(step, 1)
    tangent = normed_step(
        spread_ref[0, 0:chans], base_ref[0].astype(F32), sigma_ref[at, :], gain_ref[...]
    )
    slope = slope_ref[0].astype(F32)
    hidden = mm(expand_ref[...], tangent)
    gated = (hidden * jnp.concatenate([slope, slope], axis=1)).astype(BF16)
    two = (field + mm(shrink_ref[...], gated)).astype(BF16)
    raised = mm(up_ref[...], mm(two, spreadout_ref[...]).astype(BF16))
    for half in range(2):
        y = step * 2 + half
        mask = mask_ref[pl.ds(y, 1), :]
        for p in range(probes):
            for t in range(cols // 128):
                lanes = slice(p * cols + t * 128, p * cols + (t + 1) * 128)
                wide[p, t, pl.ds(y, fine, stride=rows), :] = (
                    one_ref[half, :, lanes].astype(F32) + raised[:, lanes]
                ) * mask[:, t * 128 : (t + 1) * 128]

    @pl.when(step == rows // 2 - 1)
    def _():
        for p in range(probes):
            for t in range(cols // 128):
                out_ref[p, :, :, t * 128 : (t + 1) * 128] = (
                    wide[p, t].reshape(fine, rows, 128).astype(BF16)
                )


def coarse_level(spread, field, sigma, base, slope, gain, expand, shrink, spreadout, up, one, mask):
    lines, probes, chans, half = field.shape
    rows, fine, wide = one.shape
    cols = wide // 2
    row = lambda i: (i, 0, 0)
    return pl.pallas_call(
        coarse_kernel,
        grid=(lines,),
        in_specs=[
            pl.BlockSpec((1,) + spread.shape[1:], row),
            pl.BlockSpec((1, probes, chans, half), lambda i: (i, 0, 0, 0)),
            whole(sigma.shape),
            pl.BlockSpec((1, chans, half), row),
            pl.BlockSpec((1, slope.shape[1], half), row),
            whole(gain.shape),
            whole(expand.shape),
            whole(shrink.shape),
            whole(spreadout.shape),
            whole(up.shape),
            pl.BlockSpec((2, fine, wide), row),
            whole(mask.shape),
        ],
        out_specs=whole((probes, fine, rows, cols)),
        out_shape=jax.ShapeDtypeStruct((probes, fine, rows, cols), BF16),
        scratch_shapes=[pltpu.VMEM((probes, cols // 128, fine * rows, 128), F32)],
        compiler_params=params(),
        name="coarse_level",
    )(spread, field, sigma, base, slope, gain, expand, shrink, spreadout, up, one, mask)


def shifted(block, axis):
    count = lax.axis_size(axis)
    forward = [(i, i + 1) for i in range(count - 1)]
    backward = [(i + 1, i) for i in range(count - 1)]
    return (
        lambda low: lax.ppermute(low, axis, forward),
        lambda high: lax.ppermute(high, axis, backward),
    )


def with_halo(block, sides, width):
    for axis, dim in sides:
        up, down = shifted(block, axis)
        low = up(lax.slice_in_dim(block, block.shape[dim] - width, None, axis=dim))
        high = down(lax.slice_in_dim(block, 0, width, axis=dim))
        block = jnp.concatenate([low, block, high], axis=dim)
    return block


def local(
    probe_field,
    gate_slope,
    spectral_filter,
    weight_in,
    weight_out,
    weight_flux,
    send_cells,
    recv_slots,
    recv_weights,
    ocean_probe,
    ocean_mask,
    coupling,
    base_fine,
    sigma_fine,
    slope_fine,
    gain_fine,
    kernel_fine,
    expand_fine,
    shrink_fine,
    down_proj,
    base_coarse,
    sigma_coarse,
    slope_coarse,
    gain_coarse,
    kernel_coarse,
    expand_coarse,
    shrink_coarse,
    up_proj,
):
    probes, rows, width, lons = probe_field.shape
    bands = lax.axis_size("lat")
    blocks = lax.axis_size("chan")
    part = width // bands
    pair = probes * rows
    lats = rows * bands
    chans = width * blocks
    fields = weight_flux.shape[1]

    flat_probe = probe_field.reshape(pair, width, lons)
    turned = turn_channels(flat_probe).reshape(bands, part, pair, lons)
    gathered = lax.all_to_all(turned, "lat", split_axis=0, concat_axis=0, tiled=True)

    flux_rows = lax.dynamic_slice_in_dim(
        weight_flux, lax.axis_index("chan") * width, width, 0
    ).T
    none = jnp.zeros_like(flux_rows)
    flux_pair = jnp.concatenate(
        [
            jnp.concatenate([flux_rows, none], axis=1),
            jnp.concatenate([none, flux_rows], axis=1),
        ],
        axis=0,
    )
    probe_terms = lax.all_to_all(
        probe_flux(probe_field, flux_pair), "chan", split_axis=0, concat_axis=0, tiled=True
    )

    fwd_lon, inv_lon = fourier_tables(lons)
    fwd_lat, inv_lat = cosine_tables(lats)
    diff = (mm(fwd_lon, inv_lon) - jnp.eye(lons, dtype=F32)).astype(BF16)
    filt = lax.dynamic_slice_in_dim(
        spectral_filter, lax.axis_index("lat") * part, part, 1
    ).T.reshape(part, lats, 1)
    mixed = lat_filter(gathered, fwd_lat.T, inv_lat.T, filt, diff)
    regrouped = lax.all_to_all(
        mixed.reshape(bands * blocks, part, pair, 128),
        ("lat", "chan"),
        split_axis=0,
        concat_axis=0,
        tiled=True,
    ).reshape(chans, pair, 128)

    win = (
        weight_in.reshape(blocks, bands, part, -1).transpose(1, 0, 2, 3).reshape(chans, -1).T
    )
    folded = mm(weight_out, weight_flux).astype(BF16)
    wout = jnp.concatenate([weight_out, folded, folded], axis=1).T
    update, picked = pointwise(
        regrouped, gate_slope, win, wout, probe_terms, send_cells[0]
    )
    update_back = lax.all_to_all(update, "chan", split_axis=0, concat_axis=0, tiled=True)
    atmos_out = add_update(flat_probe, update_back.reshape(blocks, pair, width, 128)).reshape(
        probe_field.shape
    )

    tile_rows, tile_cols = ocean_mask.shape
    fine = ocean_probe.shape[1]
    mask = ocean_mask.astype(F32)
    masked = ocean_probe * ocean_mask.astype(BF16)
    padded = with_halo(masked, (("lat", 2), ("chan", 3)), 3).transpose(2, 0, 1, 3)
    spread = depthwise(padded, kernel_fine)
    start = masked.transpose(2, 1, 0, 3).reshape(tile_rows, fine, probes * tile_cols)
    base_rows = base_fine.transpose(1, 0, 2)
    slope_rows = slope_fine.transpose(1, 0, 2)
    base_lines = base_coarse.transpose(1, 0, 2)
    slope_lines = slope_coarse.transpose(1, 0, 2)
    couple_t = coupling.T
    no_couple = jnp.zeros_like(couple_t)
    couple = jnp.stack(
        [
            jnp.concatenate([couple_t, no_couple], axis=1),
            jnp.concatenate([no_couple, couple_t], axis=1),
        ]
    )
    mix = (kernel_fine[None, :, :, None] * couple.astype(F32)[:, :, None, :]).astype(BF16)
    mix = mix.reshape(probes, fine, 49 * probes * fields)
    lane = jnp.arange(probes * tile_cols, dtype=jnp.int32)
    meets = lane[:, None] // 2 == jnp.arange(probes * tile_cols // 2, dtype=jnp.int32)[None, :]
    pool = jnp.where(meets, 0.25, 0.0).astype(BF16)
    spreadout = jnp.where(meets.T, 1.0, 0.0).astype(BF16)

    arrived = lax.all_to_all(picked, "lat", split_axis=0, concat_axis=0, tiled=True)
    flux = combine(arrived, recv_slots[0], recv_weights[0], mask)
    up, down = shifted(flux, "lat")
    tall = jnp.concatenate([up(flux[tile_rows - 3 :]), flux, down(flux[:3])], axis=0)
    up, down = shifted(flux, "chan")
    left = up(tall[:, :, tile_cols - 128 :])
    right = down(tall[:, :, :128])
    one, coarse = fine_level(
        spread,
        start,
        tall,
        left,
        right,
        mask,
        sigma_fine,
        base_rows,
        slope_rows,
        gain_fine[:, None],
        mix,
        couple,
        expand_fine.T,
        shrink_fine.T,
        pool,
        down_proj.T,
    )
    coarse_padded = with_halo(coarse, (("lat", 0), ("chan", 3)), 3)
    coarse_spread = depthwise(coarse_padded, kernel_coarse)
    ocean_out = coarse_level(
        coarse_spread,
        coarse,
        sigma_coarse,
        base_lines,
        slope_lines,
        gain_coarse[:, None],
        expand_coarse.T,
        shrink_coarse.T,
        spreadout,
        up_proj.T,
        one,
        mask,
    )
    return (atmos_out, ocean_out)


def solution(mesh):
    tile = P(("lat", "chan"), None, None)
    rows_cols = P(None, "lat", "chan")
    return jax.shard_map(
        local,
        mesh=mesh,
        in_specs=(
            P(None, "lat", "chan", None),
            P("lat", None, "chan"),
            P(None, "chan"),
            P(),
            P(),
            P(),
            tile,
            tile,
            tile,
            P(None, None, "lat", "chan"),
            P("lat", "chan"),
            P(),
            rows_cols,
            P("lat", "chan"),
            rows_cols,
            P(),
            P(),
            P(),
            P(),
            P(),
            rows_cols,
            P("lat", "chan"),
            rows_cols,
            P(),
            P(),
            P(),
            P(),
            P(),
        ),
        out_specs=(P(None, "lat", "chan", None), P(None, None, "lat", "chan")),
        check_vma=False,
    )
```

```python
import functools
import math

import jax
import jax.numpy as jnp
import ml_dtypes
import numpy as np
from jax import lax
from jax.experimental import pallas as pl
from jax.experimental.pallas import tpu as pltpu
from jax.sharding import PartitionSpec as P

F32 = jnp.float32
BF16 = jnp.bfloat16
MESH = pl.DeviceIdType.MESH
VMEM_LIMIT = 56 * 1024 * 1024


def params(**more):
    return pltpu.CompilerParams(vmem_limit_bytes=VMEM_LIMIT, **more)


def cost(flops, nbytes):
    return pl.CostEstimate(flops=int(flops), bytes_accessed=int(nbytes), transcendentals=0)


def mm(a, b):
    return jnp.dot(a, b, preferred_element_type=F32)


def whole(shape):
    zeros = (0,) * len(shape)
    return pl.BlockSpec(shape, lambda *_: zeros)


def fourier_product(count):
    column = np.arange(count)
    half = count // 2
    wave = np.where(column <= half, column, column - half)
    angles = (column[:, None] * wave[None, :] % count) * (2.0 * math.pi / count)
    basis = np.where((column <= half)[None, :], np.cos(angles), np.sin(angles))
    forward = (basis / count).astype(ml_dtypes.bfloat16)
    factor = np.where((column == 0) | (column == half), 1.0, 2.0)
    inverse = (basis.T * factor[:, None]).astype(ml_dtypes.bfloat16)
    product = forward.astype(np.float64) @ inverse.astype(np.float64)
    return (product - np.eye(count)).astype(ml_dtypes.bfloat16)


def cosine_tables(count):
    degree = np.arange(count)
    phase = degree[None, :] * (2 * degree[:, None] + 1) % (4 * count)
    basis = np.cos(phase * (math.pi / (2 * count)))
    forward = (basis / count).astype(ml_dtypes.bfloat16)
    factor = np.where(degree == 0, 1.0, 2.0)
    inverse = (basis.T * factor[:, None]).astype(ml_dtypes.bfloat16)
    return (forward, inverse)


def turn_kernel(in_ref, out_ref, wide):
    rows, chans, lanes = in_ref.shape
    wide[...] = in_ref[...].astype(F32).reshape(rows * chans, lanes)
    for c in range(chans):
        out_ref[c] = wide[pl.ds(c, rows, stride=chans), :].astype(BF16)


def turn_channels(field):
    rows, chans, lons = field.shape
    return pl.pallas_call(
        turn_kernel,
        grid=(lons // 128,),
        in_specs=[pl.BlockSpec((rows, chans, 128), lambda i: (0, 0, i))],
        out_specs=pl.BlockSpec((chans, rows, 128), lambda i: (0, 0, i)),
        out_shape=jax.ShapeDtypeStruct((chans, rows, lons), BF16),
        scratch_shapes=[pltpu.VMEM((rows * chans, 128), F32)],
        compiler_params=params(),
        cost_estimate=cost(0, 4 * field.size),
        name="turn_channels",
    )(field)


def probe_flux_kernel(probe_ref, weight_ref, out_ref):
    weight = weight_ref[...]
    rows = probe_ref.shape[1]
    for n in range(0, rows, 2):
        pair = [
            mm(weight, jnp.concatenate([probe_ref[0, m], probe_ref[1, m]], axis=0))
            for m in (n, n + 1)
        ]
        both = jnp.concatenate(pair, axis=0).astype(BF16)
        for j in range(out_ref.shape[0]):
            out_ref[j, n * 8 : n * 8 + 16, :] = both[:, j * 128 : (j + 1) * 128]


def probe_flux(probe, weight):
    probes, rows, chans, lons = probe.shape
    blocks = lons // 128
    step = 4
    return pl.pallas_call(
        probe_flux_kernel,
        grid=(rows // step,),
        in_specs=[
            pl.BlockSpec((probes, step, chans, lons), lambda i: (0, i, 0, 0)),
            whole(weight.shape),
        ],
        out_specs=pl.BlockSpec((blocks, step * 8, 128), lambda i: (0, i, 0)),
        out_shape=jax.ShapeDtypeStruct((blocks, rows * 8, 128), BF16),
        compiler_params=params(),
        cost_estimate=cost(2 * 8 * probe.size, 2 * probe.size),
        name="probe_flux",
    )(probe, weight)


def filter_kernel(in_ref, fwd_ref, inv_ref, filt_ref, diff_ref, out_ref, wide, back):
    bands, _, pair, lons = in_ref.shape
    rows = pair // 2
    blocks = out_ref.shape[1]

    def load(b, carry):
        piece = in_ref[b, 0].astype(F32)
        at = pl.ds(pl.multiple_of(b * rows, 8), rows)
        wide[at, 0:lons] = piece[0:rows]
        wide[at, lons : 2 * lons] = piece[rows:pair]
        return carry

    lax.fori_loop(0, bands, load, 0)
    fwd = fwd_ref[...]
    inv = inv_ref[...]
    filt = filt_ref[0]
    chunk = 512

    def lat_filter(t, carry):
        at = pl.ds(pl.multiple_of(t * chunk, chunk), chunk)
        value = wide[:, at]
        filtered = (mm(fwd, value.astype(BF16)) * filt).astype(BF16)
        returned = mm(inv, filtered)
        back[:, at] = returned.astype(BF16)
        wide[:, at] = value + returned
        return carry

    lax.fori_loop(0, 2 * lons // chunk, lat_filter, 0)
    for p in range(2):
        for t in range(lons // 256):
            at = slice(p * lons + t * 256, p * lons + (t + 1) * 256)
            wide[:, at] = wide[:, at] + mm(
                back[:, p * lons : (p + 1) * lons], diff_ref[:, t * 256 : (t + 1) * 256]
            )

    def store(b, carry):
        at = pl.ds(pl.multiple_of(b * rows, 8), rows)
        for j in range(blocks):
            cols = slice(j * 128, (j + 1) * 128)
            more = slice(lons + j * 128, lons + (j + 1) * 128)
            out_ref[b, j, 0] = jnp.concatenate([wide[at, cols], wide[at, more]], axis=0).astype(
                BF16
            )
        return carry

    lax.fori_loop(0, bands, store, 0)


def lat_filter(received, fwd, inv, filt, diff):
    bands, chans, pair, lons = received.shape
    lats = fwd.shape[0]
    blocks = lons // 128
    return pl.pallas_call(
        filter_kernel,
        grid=(chans,),
        in_specs=[
            pl.BlockSpec((bands, 1, pair, lons), lambda i: (0, i, 0, 0)),
            whole(fwd.shape),
            whole(inv.shape),
            pl.BlockSpec((1, lats, 1), lambda i: (i, 0, 0)),
            whole(diff.shape),
        ],
        out_specs=pl.BlockSpec((bands, blocks, 1, pair, 128), lambda i: (0, 0, i, 0, 0)),
        out_shape=jax.ShapeDtypeStruct((bands, blocks, chans, pair, 128), BF16),
        scratch_shapes=[pltpu.VMEM((lats, 2 * lons), F32), pltpu.VMEM((lats, 2 * lons), BF16)],
        compiler_params=params(),
        cost_estimate=cost(8.4e9, 4 * received.size),
        name="lat_filter",
    )(received, fwd, inv, filt, diff)


def point_kernel(
    mixed_ref,
    slope_ref,
    win_ref,
    wout_ref,
    pflux_ref,
    cells_ref,
    first_ref,
    second_ref,
    picked_ref,
    wide,
    flux,
):
    chans, pair, lanes = mixed_ref.shape
    rows = pair // 2
    step = pl.program_id(0)

    @pl.when(step == 0)
    def _():
        def load(i, carry):
            at = pl.ds(pl.multiple_of(i * 8, 8), 8)
            wide[pl.ds(pl.multiple_of(i * 8 * pair, 8), 8 * pair), :] = (
                mixed_ref[at].astype(F32).reshape(8 * pair, lanes)
            )
            return carry

        lax.fori_loop(0, chans // 8, load, 0)

    value = jnp.concatenate(
        [wide[pl.ds(step + p * rows, chans, stride=pair), :] for p in range(2)], axis=1
    ).astype(BF16)
    slope = slope_ref[0].astype(F32)
    hidden = mm(win_ref[...], value)
    gated = (jnp.concatenate([slope, slope], axis=1) * hidden).astype(BF16)
    update = mm(wout_ref[...], gated)
    width = first_ref.shape[2]
    for j in range(first_ref.shape[0]):
        piece = update[j * width : (j + 1) * width].astype(BF16)
        first_ref[j, 0] = piece[:, 0:lanes]
        second_ref[j, 0] = piece[:, lanes : 2 * lanes]
    terms = update[chans : chans + 8]
    which = lax.broadcasted_iota(jnp.int32, (8, lanes), 0)
    flux[pl.ds(pl.multiple_of(step * 8, 8), 8), :] = jnp.where(
        which < 4, terms[:, 0:lanes], terms[:, lanes : 2 * lanes]
    )

    @pl.when(step == rows - 1)
    def _():
        total = flux[...]
        for j in range(pflux_ref.shape[0]):
            total = total + pflux_ref[j].astype(F32)
        total = total.astype(BF16)
        place = lax.broadcasted_iota(jnp.int32, (lanes, lanes), 0)
        for r in range(cells_ref.shape[0]):
            cells = cells_ref[r : r + 1, :]
            row = cells // lanes
            hot = jnp.where(place == cells - row * lanes, 1.0, 0.0).astype(BF16)
            found = mm(total, hot)
            picked = jnp.zeros((8, lanes), F32)
            for n in range(rows):
                picked = picked + jnp.where(row == n, found[n * 8 : (n + 1) * 8], 0.0)
            picked_ref[r] = picked


def pointwise(mixed, slope, win, wout, pflux, cells, blocks):
    chans, pair, lanes = mixed.shape
    rows, hid, _ = slope.shape
    width = chans // blocks
    return pl.pallas_call(
        point_kernel,
        grid=(rows,),
        in_specs=[
            whole(mixed.shape),
            pl.BlockSpec((1, hid, lanes), lambda i: (i, 0, 0)),
            whole(win.shape),
            whole(wout.shape),
            whole(pflux.shape),
            whole(cells.shape),
        ],
        out_specs=[
            pl.BlockSpec((blocks, 1, width, lanes), lambda i: (0, i, 0, 0)),
            pl.BlockSpec((blocks, 1, width, lanes), lambda i: (0, i, 0, 0)),
            whole((cells.shape[0], 8, lanes)),
        ],
        out_shape=[
            jax.ShapeDtypeStruct((blocks, rows, width, lanes), BF16),
            jax.ShapeDtypeStruct((blocks, rows, width, lanes), BF16),
            jax.ShapeDtypeStruct((cells.shape[0], 8, lanes), F32),
        ],
        scratch_shapes=[
            pltpu.VMEM((chans * pair, lanes), F32),
            pltpu.VMEM((rows * 8, lanes), F32),
        ],
        compiler_params=params(),
        cost_estimate=cost(7.3e9, 4 * mixed.size + 2 * slope.size),
        name="pointwise",
    )(mixed, slope, win, wout, pflux, cells)


def add_kernel(probe_ref, update_ref, *rest):
    out_ref = rest[-1]
    for j in range(update_ref.shape[0]):
        cols = slice(j * 128, (j + 1) * 128)
        out_ref[:, :, cols] = (
            probe_ref[:, :, cols].astype(F32) + update_ref[j].astype(F32)
        ).astype(BF16)


def add_update(probe, update, p, partial=None):
    rows, chans, lons = probe.shape
    blocks, count = update.shape[0], update.shape[1]
    step = 6
    base = p * (count // step)
    rest = () if partial is None else (partial,)
    return pl.pallas_call(
        add_kernel,
        grid=(count // step,),
        in_specs=[
            pl.BlockSpec((step, chans, lons), lambda i: (base + i, 0, 0)),
            pl.BlockSpec((blocks, step, chans, 128), lambda i: (0, i, 0, 0)),
        ]
        + [pl.BlockSpec(memory_space=pl.ANY) for _ in rest],
        out_specs=pl.BlockSpec((step, chans, lons), lambda i: (base + i, 0, 0)),
        out_shape=jax.ShapeDtypeStruct(probe.shape, BF16),
        input_output_aliases={2: 0} if rest else {},
        compiler_params=params(),
        cost_estimate=cost(update.size, 6 * update.size),
        name="add_update",
    )(probe, update, *rest)


def depth_sum(in_ref, p, first, taps_ref, wide, done):
    high, _, broad, chans = in_ref.shape
    rows, cols = done.shape[0], done.shape[1]
    halves = wide.shape[0]
    for y in range(high):
        for h in range(halves):
            lanes = min(128, chans - h * 128)
            wide[h, y, 0:broad, 0:lanes] = in_ref[y, p, :, h * 128 : h * 128 + lanes].astype(F32)

    def tile(i, carry):
        at = pl.multiple_of(i * 8, 8)
        for h in range(halves):
            lanes = slice(h * 128, (h + 1) * 128)
            total = [jnp.zeros((8, 128), F32) for _ in range(rows)]
            for b in range(7):
                taps = [taps_ref[(7 * a + b) * 8 : (7 * a + b + 1) * 8, lanes] for a in range(7)]
                for y in range(high):
                    moved = wide[h, y, pl.ds(at + (first + b), 8), :]
                    for a in range(7):
                        if 0 <= y - a < rows:
                            total[y - a] = total[y - a] + moved * taps[a]
            for y in range(rows):
                done[y, pl.ds(at, 8), lanes] = total[y]
        return carry

    lax.fori_loop(0, cols // 8, tile, 0)


def depth_kernel(in_ref, taps_ref, out_ref, wide, done):
    depth_sum(in_ref, 0, 0, taps_ref, wide, done)
    for y in range(done.shape[0]):
        out_ref[y] = done[y].T[0 : in_ref.shape[3]]


def tap_rows(kernel):
    chans = kernel.shape[0]
    full = -(-chans // 128) * 128
    return jnp.repeat(jnp.pad(kernel.T, ((0, 0), (0, full - chans))), 8, axis=0)


def depthwise(padded, kernel):
    high, probes, broad, chans = padded.shape
    rows, cols = high - 6, broad - 6
    halves = -(-chans // 128)
    taps = tap_rows(kernel)
    return pl.pallas_call(
        depth_kernel,
        grid=(probes,),
        in_specs=[
            pl.BlockSpec((high, 1, broad, chans), lambda p: (0, p, 0, 0)),
            whole(taps.shape),
        ],
        out_specs=pl.BlockSpec((rows, chans, cols), lambda p: (0, 0, p)),
        out_shape=jax.ShapeDtypeStruct((rows, chans, probes * cols), F32),
        scratch_shapes=[
            pltpu.VMEM((halves, high, -(-broad // 8) * 8, 128), F32),
            pltpu.VMEM((rows, cols, halves * 128), F32),
        ],
        compiler_params=params(),
        cost_estimate=cost(200 * rows * cols * chans * probes, 4 * padded.size),
        name="depthwise",
    )(padded, taps)


def greet(partners, more=()):
    barrier = pltpu.get_barrier_semaphore()
    for where in more:
        pl.semaphore_signal(barrier, inc=1, device_id=where, device_id_type=MESH)
    count = jnp.int32(len(more))
    for there, where in partners:

        @pl.when(there)
        def _(where=where):
            pl.semaphore_signal(barrier, inc=1, device_id=where, device_id_type=MESH)

        count = count + there.astype(jnp.int32)
    pl.semaphore_wait(barrier, count)


def swap_edges(low, high, sems, before, after, low_to, high_to):
    is_before, device_before = before
    is_after, device_after = after

    def to_before():
        return pltpu.make_async_remote_copy(
            low, low_to, sems.at[0], sems.at[1], device_id=device_before, device_id_type=MESH
        )

    def to_after():
        return pltpu.make_async_remote_copy(
            high, high_to, sems.at[2], sems.at[3], device_id=device_after, device_id_type=MESH
        )

    @pl.when(is_before)
    def _():
        to_before().start()

    @pl.when(is_after)
    def _():
        to_after().start()

    @pl.when(is_before)
    def _():
        to_before().wait_send()
        to_after().wait_recv()

    @pl.when(is_after)
    def _():
        to_after().wait_send()
        to_before().wait_recv()


def neighbours(bands, blocks):
    band, block = lax.axis_index("lat"), lax.axis_index("chan")
    return (
        (band > 0, (jnp.maximum(band - 1, 0), block)),
        (band < bands - 1, (jnp.minimum(band + 1, bands - 1), block)),
        (block > 0, (band, jnp.maximum(block - 1, 0))),
        (block < blocks - 1, (band, jnp.minimum(block + 1, blocks - 1))),
    )


def flux_kernel(
    blocks, picked_ref, slots_ref, weights_ref, mask_ref, out_ref, pool_ref, tall, send, recv, edge
):
    bands, fields, cap = picked_ref.shape
    rows, cols = mask_ref.shape
    band, block = lax.axis_index("lat"), lax.axis_index("chan")
    lat_before, lat_after, chan_before, chan_after = neighbours(bands, blocks)
    tall[...] = jnp.zeros_like(tall)
    pool_ref[pl.ds(band, 1)] = picked_ref[pl.ds(band, 1)]
    others = [(lax.rem(band + k, bands), block) for k in range(1, bands)]
    greet((chan_before, chan_after), others)

    copies = []
    for k, where in enumerate(others):
        copy = pltpu.make_async_remote_copy(
            picked_ref.at[where[0]],
            pool_ref.at[band],
            send.at[k],
            recv.at[k],
            device_id=where,
            device_id_type=MESH,
        )
        copy.start()
        copies.append(copy)
    for copy in copies:
        copy.wait()

    pool = pool_ref[...].reshape(bands * fields, cap).astype(BF16)
    place = lax.broadcasted_iota(jnp.int32, (cap, cols), 0)
    for y in range(rows):
        at = slice(y * cols, (y + 1) * cols)
        total = jnp.zeros((fields, cols), F32)
        for k in range(slots_ref.shape[0]):
            slots = slots_ref[k : k + 1, at]
            weights = weights_ref[k : k + 1, at]
            source = slots // cap
            hot = jnp.where(place == slots - source * cap, 1.0, 0.0).astype(BF16)
            found = mm(pool, hot)
            for b in range(bands):
                total = total + found[b * fields : (b + 1) * fields] * jnp.where(
                    source == b, weights, 0.0
                )
        tall[3 + y, :, 128 : 128 + cols] = total * mask_ref[y : y + 1, :]

    inner = pl.ds(128, cols)
    swap_edges(
        tall.at[pl.ds(3, 3), :, inner],
        tall.at[pl.ds(rows, 3), :, inner],
        edge.at[0],
        lat_before,
        lat_after,
        tall.at[pl.ds(rows + 3, 3), :, inner],
        tall.at[pl.ds(0, 3), :, inner],
    )
    swap_edges(
        tall.at[:, :, pl.ds(128, 128)],
        tall.at[:, :, pl.ds(cols, 128)],
        edge.at[1],
        chan_before,
        chan_after,
        tall.at[:, :, pl.ds(128 + cols, 128)],
        tall.at[:, :, pl.ds(0, 128)],
    )
    out_ref[...] = tall[...]


def flux_tile(picked, slots, weights, mask, blocks):
    bands, fields, _ = picked.shape
    rows, cols = mask.shape
    shape = (rows + 6, fields, cols + 256)
    return pl.pallas_call(
        functools.partial(flux_kernel, blocks),
        in_specs=[whole(a.shape) for a in (picked, slots, weights, mask)],
        out_specs=whole(shape),
        out_shape=jax.ShapeDtypeStruct(shape, F32),
        scratch_shapes=[
            pltpu.VMEM(picked.shape, F32),
            pltpu.VMEM(shape, F32),
            pltpu.SemaphoreType.DMA((bands - 1,)),
            pltpu.SemaphoreType.DMA((bands - 1,)),
            pltpu.SemaphoreType.DMA((2, 4)),
        ],
        compiler_params=params(collective_id=1, has_side_effects=True),
        name="flux_tile",
    )(picked, slots, weights, mask)


def edge_kernel(bands, blocks, field_ref, out_ref, tall, edge, own):
    lines, _, cols, _ = field_ref.shape
    lat_before, lat_after, chan_before, chan_after = neighbours(bands, blocks)
    tall[...] = jnp.zeros_like(tall)
    greet((lat_before, lat_after, chan_before, chan_after))
    inner = pl.ds(16, cols)
    copy = pltpu.make_async_copy(field_ref, tall.at[pl.ds(3, lines), :, inner, :], own)
    copy.start()
    swap_edges(
        field_ref.at[pl.ds(0, 3)],
        field_ref.at[pl.ds(lines - 3, 3)],
        edge.at[0],
        lat_before,
        lat_after,
        tall.at[pl.ds(lines + 3, 3), :, inner, :],
        tall.at[pl.ds(0, 3), :, inner, :],
    )
    copy.wait()
    swap_edges(
        tall.at[:, :, pl.ds(16, 16), :],
        tall.at[:, :, pl.ds(cols, 16), :],
        edge.at[1],
        chan_before,
        chan_after,
        tall.at[:, :, pl.ds(16 + cols, 16), :],
        tall.at[:, :, pl.ds(0, 16), :],
    )
    out_ref[...] = tall[...]


def coarse_edges(field, bands, blocks):
    lines, probes, cols, chans = field.shape
    shape = (lines + 6, probes, cols + 32, chans)
    return pl.pallas_call(
        functools.partial(edge_kernel, bands, blocks),
        in_specs=[whole(field.shape)],
        out_specs=whole(shape),
        out_shape=jax.ShapeDtypeStruct(shape, BF16),
        scratch_shapes=[
            pltpu.VMEM(shape, BF16),
            pltpu.SemaphoreType.DMA((2, 4)),
            pltpu.SemaphoreType.DMA,
        ],
        compiler_params=params(collective_id=2, has_side_effects=True),
        name="coarse_edges",
    )(field)


def normed_step(spread, base, sigma, gain):
    chans = spread.shape[0]
    wide_base = jnp.concatenate([base, base], axis=1)
    center = jnp.sum(spread, axis=0, keepdims=True) * (1.0 / chans)
    along = jnp.sum(wide_base * spread, axis=0, keepdims=True) * (1.0 / chans)
    scale = jnp.concatenate([sigma, sigma], axis=1)
    return (gain * scale * (spread - center - wide_base * along)).astype(BF16)


def fine_kernel(
    spread_ref,
    probe_ref,
    flux_ref,
    mask_ref,
    sigma_ref,
    base_ref,
    slope_ref,
    gain_ref,
    mix_ref,
    couple_ref,
    expand_ref,
    shrink_ref,
    pool_ref,
    down_ref,
    turn_ref,
    one_ref,
    coarse_ref,
    turned_ref,
    columns,
    held,
):
    step = pl.program_id(0)
    high = flux_ref.shape[0]
    cols = flux_ref.shape[2] - 256

    @pl.when(step == 0)
    def _():
        for y in range(high):
            row = flux_ref[y]
            for b in range(7):
                columns[(y * 7 + b) * 8 : (y * 7 + b + 1) * 8, :] = row[:, 125 + b : 125 + b + cols]

    near = columns[pl.ds(pl.multiple_of(step * 56, 8), 392), :].astype(BF16)
    center = columns[pl.ds(pl.multiple_of((step + 3) * 56 + 24, 8), 8), :].astype(BF16)
    spread = spread_ref[0] + jnp.concatenate([mm(mix_ref[p], near) for p in range(2)], axis=1)
    forcing = jnp.concatenate([mm(couple_ref[p], center) for p in range(2)], axis=1)
    start = (probe_ref[0].astype(F32) + forcing).astype(BF16).astype(F32)
    at = pl.ds(step, 1)
    tangent = normed_step(spread, base_ref[0].astype(F32), sigma_ref[at, :], gain_ref[...])
    slope = slope_ref[0].astype(F32)
    hidden = mm(expand_ref[...], tangent)
    gated = (hidden * jnp.concatenate([slope, slope], axis=1)).astype(BF16)
    mask = mask_ref[at, :]
    one = ((start + mm(shrink_ref[...], gated)) * jnp.concatenate([mask, mask], axis=1)).astype(BF16)
    one_ref[0] = one
    pooled = mm(one, pool_ref[...])

    @pl.when(step % 2 == 0)
    def _():
        held[...] = pooled

    @pl.when(step % 2 == 1)
    def _():
        both = (held[...] + pooled).astype(BF16)
        coarse_ref[0] = mm(down_ref[...], both).astype(BF16)
        turned = mm(both.T, turn_ref[...]).astype(BF16)
        half = turned.shape[0] // 2
        turned_ref[0, 0] = turned[0:half]
        turned_ref[0, 1] = turned[half : 2 * half]


def fine_level(spread, probe, flux, mask, sigma, base, slope, gain, mix, couple, expand, shrink, pool, down, turn):
    rows, chans, wide = spread.shape
    cols = wide // 2
    coarse = down.shape[0]
    row = lambda i: (i, 0, 0)
    return pl.pallas_call(
        fine_kernel,
        grid=(rows,),
        in_specs=[
            pl.BlockSpec((1, chans, wide), row),
            pl.BlockSpec((1, chans, wide), row),
            whole(flux.shape),
            whole(mask.shape),
            whole(sigma.shape),
            pl.BlockSpec((1, chans, cols), row),
            pl.BlockSpec((1, slope.shape[1], cols), row),
            whole(gain.shape),
            whole(mix.shape),
            whole(couple.shape),
            whole(expand.shape),
            whole(shrink.shape),
            whole(pool.shape),
            whole(down.shape),
            whole(turn.shape),
        ],
        out_specs=[
            pl.BlockSpec((1, chans, wide), row),
            pl.BlockSpec((1, coarse, cols), lambda i: (i // 2, 0, 0)),
            pl.BlockSpec((1, 2, cols // 2, turn.shape[1]), lambda i: (i // 2, 0, 0, 0)),
        ],
        out_shape=[
            jax.ShapeDtypeStruct((rows, chans, wide), BF16),
            jax.ShapeDtypeStruct((rows // 2, coarse, cols), BF16),
            jax.ShapeDtypeStruct((rows // 2, 2, cols // 2, turn.shape[1]), BF16),
        ],
        scratch_shapes=[
            pltpu.VMEM((flux.shape[0] * 56, cols), F32),
            pltpu.VMEM((chans, cols), F32),
        ],
        compiler_params=params(),
        name="fine_level",
    )(spread, probe, flux, mask, sigma, base, slope, gain, mix, couple, expand, shrink, pool, down, turn)


def coarse_kernel(
    around_ref,
    taps_ref,
    field_ref,
    sigma_ref,
    base_ref,
    slope_ref,
    gain_ref,
    expand_ref,
    shrink_ref,
    spreadout_ref,
    up_ref,
    one_ref,
    mask_ref,
    out_ref,
    wide,
    tall,
    done,
    spread,
):
    step = pl.program_id(0)
    chans = field_ref.shape[1]
    probes, fine, rows, cols = out_ref.shape

    @pl.when(step == 0)
    def _():
        half = done.shape[1]
        for p in range(probes):
            depth_sum(around_ref, p, 13, taps_ref, tall, done)
            for y in range(done.shape[0]):
                spread[y, :, p * half : (p + 1) * half] = done[y].T[0:chans]

    at = pl.ds(step, 1)
    tangent = normed_step(
        spread[step], base_ref[0].astype(F32), sigma_ref[at, :], gain_ref[...]
    )
    slope = slope_ref[0].astype(F32)
    hidden = mm(expand_ref[...], tangent)
    gated = (hidden * jnp.concatenate([slope, slope], axis=1)).astype(BF16)
    two = (field_ref[0].astype(F32) + mm(shrink_ref[...], gated)).astype(BF16)
    raised = mm(up_ref[...], mm(two, spreadout_ref[...]).astype(BF16))
    for half in range(2):
        y = step * 2 + half
        mask = mask_ref[pl.ds(y, 1), :]
        for p in range(probes):
            for t in range(cols // 128):
                lanes = slice(p * cols + t * 128, p * cols + (t + 1) * 128)
                wide[p, t, pl.ds(y, fine, stride=rows), :] = (
                    one_ref[half, :, lanes].astype(F32) + raised[:, lanes]
                ) * mask[:, t * 128 : (t + 1) * 128]

    @pl.when(step == rows // 2 - 1)
    def _():
        for p in range(probes):
            for t in range(cols // 128):
                out_ref[p, :, :, t * 128 : (t + 1) * 128] = (
                    wide[p, t].reshape(fine, rows, 128).astype(BF16)
                )


def coarse_level(
    around, kernel, field, sigma, base, slope, gain, expand, shrink, spreadout, up, one, mask
):
    lines, chans, double = field.shape
    half = double // 2
    rows, fine, wide = one.shape
    cols = wide // 2
    taps = tap_rows(kernel)
    row = lambda i: (i, 0, 0)
    return pl.pallas_call(
        coarse_kernel,
        grid=(lines,),
        in_specs=[
            whole(around.shape),
            whole(taps.shape),
            pl.BlockSpec((1, chans, double), row),
            whole(sigma.shape),
            pl.BlockSpec((1, chans, half), row),
            pl.BlockSpec((1, slope.shape[1], half), row),
            whole(gain.shape),
            whole(expand.shape),
            whole(shrink.shape),
            whole(spreadout.shape),
            whole(up.shape),
            pl.BlockSpec((2, fine, wide), row),
            whole(mask.shape),
        ],
        out_specs=whole((2, fine, rows, cols)),
        out_shape=jax.ShapeDtypeStruct((2, fine, rows, cols), BF16),
        scratch_shapes=[
            pltpu.VMEM((2, cols // 128, fine * rows, 128), F32),
            pltpu.VMEM((taps.shape[1] // 128, around.shape[0], around.shape[2], 128), F32),
            pltpu.VMEM((lines, half, taps.shape[1]), F32),
            pltpu.VMEM((lines, chans, double), F32),
        ],
        compiler_params=params(),
        cost_estimate=cost(1e9, 4e6),
        name="coarse_level",
    )(around, taps, field, sigma, base, slope, gain, expand, shrink, spreadout, up, one, mask)


def shifted(block, axis):
    count = lax.axis_size(axis)
    forward = [(i, i + 1) for i in range(count - 1)]
    backward = [(i + 1, i) for i in range(count - 1)]
    return (
        lambda low: lax.ppermute(low, axis, forward),
        lambda high: lax.ppermute(high, axis, backward),
    )


def with_halo(block, sides, width):
    for axis, dim in sides:
        up, down = shifted(block, axis)
        low = up(lax.slice_in_dim(block, block.shape[dim] - width, None, axis=dim))
        high = down(lax.slice_in_dim(block, 0, width, axis=dim))
        block = jnp.concatenate([low, block, high], axis=dim)
    return block


def local(
    probe_field,
    gate_slope,
    spectral_filter,
    weight_in,
    weight_out,
    weight_flux,
    send_cells,
    recv_slots,
    recv_weights,
    ocean_probe,
    ocean_mask,
    coupling,
    base_fine,
    sigma_fine,
    slope_fine,
    gain_fine,
    kernel_fine,
    expand_fine,
    shrink_fine,
    down_proj,
    base_coarse,
    sigma_coarse,
    slope_coarse,
    gain_coarse,
    kernel_coarse,
    expand_coarse,
    shrink_coarse,
    up_proj,
):
    probes, rows, width, lons = probe_field.shape
    bands = lax.axis_size("lat")
    blocks = lax.axis_size("chan")
    part = width // bands
    pair = probes * rows
    lats = rows * bands
    chans = width * blocks
    fields = weight_flux.shape[1]

    flat_probe = probe_field.reshape(pair, width, lons)
    turned = turn_channels(flat_probe).reshape(bands, part, pair, lons)
    gathered = lax.all_to_all(turned, "lat", split_axis=0, concat_axis=0, tiled=True)

    flux_rows = lax.dynamic_slice_in_dim(
        weight_flux, lax.axis_index("chan") * width, width, 0
    ).T
    none = jnp.zeros_like(flux_rows)
    flux_pair = jnp.concatenate(
        [
            jnp.concatenate([flux_rows, none], axis=1),
            jnp.concatenate([none, flux_rows], axis=1),
        ],
        axis=0,
    )
    probe_terms = lax.psum_scatter(
        probe_flux(probe_field, flux_pair), "chan", scatter_dimension=0, tiled=True
    )

    tile_rows, tile_cols = ocean_mask.shape
    fine = ocean_probe.shape[1]
    mask = ocean_mask.astype(F32)
    masked = ocean_probe * ocean_mask.astype(BF16)
    padded = with_halo(masked, (("lat", 2), ("chan", 3)), 3).transpose(2, 0, 3, 1)
    start = masked.transpose(2, 1, 0, 3).reshape(tile_rows, fine, probes * tile_cols)
    base_rows = base_fine.transpose(1, 0, 2)
    slope_rows = slope_fine.transpose(1, 0, 2)
    base_lines = base_coarse.transpose(1, 0, 2)
    slope_lines = slope_coarse.transpose(1, 0, 2)
    couple_t = coupling.T
    no_couple = jnp.zeros_like(couple_t)
    couple = jnp.stack(
        [
            jnp.concatenate([couple_t, no_couple], axis=1),
            jnp.concatenate([no_couple, couple_t], axis=1),
        ]
    )
    mix = (kernel_fine[None, :, :, None] * couple.astype(F32)[:, :, None, :]).astype(BF16)
    mix = mix.reshape(probes, fine, 49 * probes * fields)
    lane = jnp.arange(probes * tile_cols, dtype=jnp.int32)
    meets = lane[:, None] // 2 == jnp.arange(probes * tile_cols // 2, dtype=jnp.int32)[None, :]
    pool = jnp.where(meets, 0.25, 0.0).astype(BF16)
    spreadout = jnp.where(meets.T, 1.0, 0.0).astype(BF16)

    fwd_lat, inv_lat = cosine_tables(lats)
    diff = jnp.asarray(fourier_product(lons))
    filt = lax.dynamic_slice_in_dim(
        spectral_filter, lax.axis_index("lat") * part, part, 1
    ).T.reshape(part, lats, 1)
    gathered, padded, start, filt, probe_terms = lax.optimization_barrier(
        (gathered, padded, start, filt, probe_terms)
    )
    mixed = lat_filter(gathered, jnp.asarray(fwd_lat.T), jnp.asarray(inv_lat.T), filt, diff)
    regrouped = lax.all_to_all(
        mixed.reshape(bands * blocks, part, pair, 128),
        ("lat", "chan"),
        split_axis=0,
        concat_axis=0,
        tiled=True,
    ).reshape(chans, pair, 128)

    win = (
        weight_in.reshape(blocks, bands, part, -1).transpose(1, 0, 2, 3).reshape(chans, -1).T
    )
    folded = mm(weight_out, weight_flux).astype(BF16)
    wout = jnp.concatenate([weight_out, folded, folded], axis=1).T
    spread = depthwise(padded, kernel_fine)
    (
        regrouped,
        spread,
        win,
        wout,
        probe_terms,
        base_rows,
        slope_rows,
        base_lines,
        slope_lines,
        mix,
        couple,
        pool,
        spreadout,
        mask,
    ) = lax.optimization_barrier(
        (
            regrouped,
            spread,
            win,
            wout,
            probe_terms,
            base_rows,
            slope_rows,
            base_lines,
            slope_lines,
            mix,
            couple,
            pool,
            spreadout,
            mask,
        )
    )
    first, second, picked = pointwise(
        regrouped, gate_slope, win, wout, probe_terms, send_cells[0], blocks
    )

    tall = flux_tile(picked, recv_slots[0], recv_weights[0], mask, blocks)
    first, tall = lax.optimization_barrier((first, tall))
    first = lax.all_to_all(first, "chan", split_axis=0, concat_axis=0, tiled=True)
    one, coarse, turned = fine_level(
        spread,
        start,
        tall,
        mask,
        sigma_fine,
        base_rows,
        slope_rows,
        gain_fine[:, None],
        mix,
        couple,
        expand_fine.T,
        shrink_fine.T,
        pool,
        down_proj.T,
        jnp.pad(down_proj, ((0, 0), (0, 256 - down_proj.shape[1]))),
    )
    around = coarse_edges(turned, bands, blocks)
    second, around = lax.optimization_barrier((second, around))
    second = lax.all_to_all(second, "chan", split_axis=0, concat_axis=0, tiled=True)
    ocean_out = coarse_level(
        around,
        kernel_coarse,
        coarse,
        sigma_coarse,
        base_lines,
        slope_lines,
        gain_coarse[:, None],
        expand_coarse.T,
        shrink_coarse.T,
        spreadout,
        up_proj.T,
        one,
        mask,
    )
    partial = add_update(flat_probe, first, 0)
    atmos_out = add_update(flat_probe, second, 1, partial).reshape(probe_field.shape)
    return (atmos_out, ocean_out)


def solution(mesh):
    tile = P(("lat", "chan"), None, None)
    rows_cols = P(None, "lat", "chan")
    return jax.shard_map(
        local,
        mesh=mesh,
        in_specs=(
            P(None, "lat", "chan", None),
            P("lat", None, "chan"),
            P(None, "chan"),
            P(),
            P(),
            P(),
            tile,
            tile,
            tile,
            P(None, None, "lat", "chan"),
            P("lat", "chan"),
            P(),
            rows_cols,
            P("lat", "chan"),
            rows_cols,
            P(),
            P(),
            P(),
            P(),
            P(),
            rows_cols,
            P("lat", "chan"),
            rows_cols,
            P(),
            P(),
            P(),
            P(),
            P(),
        ),
        out_specs=(P(None, "lat", "chan", None), P(None, None, "lat", "chan")),
        check_vma=False,
    )
```

```python
import functools
import math

import jax
import jax.numpy as jnp
import ml_dtypes
import numpy as np
from jax import lax
from jax.experimental import pallas as pl
from jax.experimental.pallas import tpu as pltpu
from jax.sharding import PartitionSpec as P

F32 = jnp.float32
BF16 = jnp.bfloat16
MESH = pl.DeviceIdType.MESH
VMEM_LIMIT = 56 * 1024 * 1024


def params(**more):
    return pltpu.CompilerParams(vmem_limit_bytes=VMEM_LIMIT, **more)


def cost(flops, nbytes):
    return pl.CostEstimate(flops=int(flops), bytes_accessed=int(nbytes), transcendentals=0)


def mm(a, b):
    return jnp.dot(a, b, preferred_element_type=F32)


def whole(shape):
    zeros = (0,) * len(shape)
    return pl.BlockSpec(shape, lambda *_: zeros)


def fourier_product(count):
    column = np.arange(count)
    half = count // 2
    wave = np.where(column <= half, column, column - half)
    angles = (column[:, None] * wave[None, :] % count) * (2.0 * math.pi / count)
    basis = np.where((column <= half)[None, :], np.cos(angles), np.sin(angles))
    forward = (basis / count).astype(ml_dtypes.bfloat16)
    factor = np.where((column == 0) | (column == half), 1.0, 2.0)
    inverse = (basis.T * factor[:, None]).astype(ml_dtypes.bfloat16)
    product = forward.astype(np.float64) @ inverse.astype(np.float64)
    return (product - np.eye(count)).astype(ml_dtypes.bfloat16)


def cosine_tables(count):
    degree = np.arange(count)
    phase = degree[None, :] * (2 * degree[:, None] + 1) % (4 * count)
    basis = np.cos(phase * (math.pi / (2 * count)))
    forward = (basis / count).astype(ml_dtypes.bfloat16)
    factor = np.where(degree == 0, 1.0, 2.0)
    inverse = (basis.T * factor[:, None]).astype(ml_dtypes.bfloat16)
    return (forward, inverse)


def greet(partners, more=()):
    barrier = pltpu.get_barrier_semaphore()
    for where in more:
        pl.semaphore_signal(barrier, inc=1, device_id=where, device_id_type=MESH)
    count = jnp.int32(len(more))
    for there, where in partners:

        @pl.when(there)
        def _(where=where):
            pl.semaphore_signal(barrier, inc=1, device_id=where, device_id_type=MESH)

        count = count + there.astype(jnp.int32)
    pl.semaphore_wait(barrier, count)


def start_edges(low, high, sems, before, after, low_to, high_to):
    is_before, device_before = before
    is_after, device_after = after

    def to_before():
        return pltpu.make_async_remote_copy(
            low, low_to, sems.at[0], sems.at[1], device_id=device_before, device_id_type=MESH
        )

    def to_after():
        return pltpu.make_async_remote_copy(
            high, high_to, sems.at[2], sems.at[3], device_id=device_after, device_id_type=MESH
        )

    @pl.when(is_before)
    def _():
        to_before().start()

    @pl.when(is_after)
    def _():
        to_after().start()

    def finish():
        @pl.when(is_before)
        def _():
            to_before().wait_send()
            to_after().wait_recv()

        @pl.when(is_after)
        def _():
            to_after().wait_send()
            to_before().wait_recv()

    return finish


def swap_edges(*args):
    start_edges(*args)()


def neighbours(bands, blocks):
    band, block = lax.axis_index("lat"), lax.axis_index("chan")
    return (
        (band > 0, (jnp.maximum(band - 1, 0), block)),
        (band < bands - 1, (jnp.minimum(band + 1, bands - 1), block)),
        (block > 0, (band, jnp.maximum(block - 1, 0))),
        (block < blocks - 1, (band, jnp.minimum(block + 1, blocks - 1))),
    )


def ocean_rows_kernel(in_ref, mask_ref, out_ref, wide):
    _, chans, rows, cols = in_ref.shape
    value = in_ref[0].astype(F32) * mask_ref[...][None]
    for t in range(cols // 128):
        wide[t] = value[:, :, t * 128 : (t + 1) * 128].reshape(chans * rows, 128)
    for y in range(rows):
        for t in range(cols // 128):
            out_ref[y, 0, :, t * 128 : (t + 1) * 128] = wide[
                t, pl.ds(y, chans, stride=rows), :
            ].astype(BF16)


def ocean_rows(field, mask):
    probes, chans, rows, cols = field.shape
    return pl.pallas_call(
        ocean_rows_kernel,
        grid=(probes,),
        in_specs=[
            pl.BlockSpec((1, chans, rows, cols), lambda p: (p, 0, 0, 0)),
            whole(mask.shape),
        ],
        out_specs=pl.BlockSpec((rows, 1, chans, cols), lambda p: (0, p, 0, 0)),
        out_shape=jax.ShapeDtypeStruct((rows, probes, chans, cols), BF16),
        scratch_shapes=[pltpu.VMEM((cols // 128, chans * rows, 128), F32)],
        compiler_params=params(),
        cost_estimate=cost(field.size, 4 * field.size),
        name="ocean_rows",
    )(field, mask)


STEPS = (
    ((0, 1), (1, 0), (0, 3), (3, 0), (1, 1), (3, 3), (1, 3), (3, 1))
    + ((0, 2), (2, 0), (2, 2), (1, 2), (2, 1), (3, 2), (2, 3))
)


def lat_partner(band, step, side):
    dz, dx = step
    return lax.rem(band // side + dz, side) * side + lax.rem(lax.rem(band, side) + dx, side)


def open_kernel(
    blocks, probe_ref, ocean_ref, out_ref, around_ref, taken, wide, turned, tall, sems, own, edge
):
    send, recv, load = sems
    rows, chans, lons = probe_ref.shape
    bands, part = out_ref.shape[0], out_ref.shape[1]
    side = math.isqrt(bands)
    lines, _, _, cols = ocean_ref.shape
    pieces, lanes = taken.shape[0], taken.shape[3]
    band, block = lax.axis_index("lat"), lax.axis_index("chan")
    lat_before, lat_after, chan_before, chan_after = neighbours(bands, blocks)

    def take(i):
        return pltpu.make_async_copy(
            probe_ref.at[:, :, pl.ds(i * lanes, lanes)], taken.at[i], load.at[i]
        )

    for i in range(pieces):
        take(i).start()
    tall[...] = jnp.zeros_like(tall)
    others = [(lat_partner(band, step, side), block) for step in STEPS]
    greet((chan_before, chan_after), others)
    inner = pl.ds(128, cols)
    center = pltpu.make_async_copy(ocean_ref, tall.at[pl.ds(3, lines), :, :, inner], own.at[0])
    center.start()
    finish_rows = start_edges(
        ocean_ref.at[pl.ds(0, 3)],
        ocean_ref.at[pl.ds(lines - 3, 3)],
        edge.at[0],
        lat_before,
        lat_after,
        tall.at[pl.ds(lines + 3, 3), :, :, inner],
        tall.at[pl.ds(0, 3), :, :, inner],
    )
    copies = []
    for i in range(pieces):
        take(i).wait()
        for t in range(lanes // 128):
            at = slice(t * 128, (t + 1) * 128)
            wide[t] = taken[i, :, :, at].astype(F32).reshape(rows * chans, 128)
            for c in range(chans):
                turned[i, c, :, at] = wide[t, pl.ds(c, rows, stride=chans), :].astype(BF16)
        columns = pl.ds(i * lanes, lanes)
        for k, where in enumerate(others):
            copy = pltpu.make_async_remote_copy(
                turned.at[i, pl.ds(where[0] * part, part)],
                out_ref.at[band, :, :, columns],
                send.at[i, k],
                recv.at[i, k],
                device_id=where,
                device_id_type=MESH,
            )
            copy.start()
            copies.append(copy)
        copy = pltpu.make_async_copy(
            turned.at[i, pl.ds(band * part, part)],
            out_ref.at[band, :, :, columns],
            own.at[i + 1],
        )
        copy.start()
        copies.append(copy)
    center.wait()
    finish_rows()
    finish_columns = start_edges(
        tall.at[:, :, :, pl.ds(128, 128)],
        tall.at[:, :, :, pl.ds(cols, 128)],
        edge.at[1],
        chan_before,
        chan_after,
        tall.at[:, :, :, pl.ds(128 + cols, 128)],
        tall.at[:, :, :, pl.ds(0, 128)],
    )
    finish_columns()
    store = pltpu.make_async_copy(tall, around_ref, own.at[0])
    store.start()
    for copy in copies:
        copy.wait()
    store.wait()


def open_exchange(probe, ocean, bands, blocks):
    rows, chans, lons = probe.shape
    lines, probes, fine, cols = ocean.shape
    pieces, lanes = 4, lons // 4
    any_spec = pl.BlockSpec(memory_space=pl.ANY)
    tall = (lines + 6, probes, fine, cols + 256)
    return pl.pallas_call(
        functools.partial(open_kernel, blocks),
        in_specs=[any_spec, any_spec],
        out_specs=[any_spec, any_spec],
        out_shape=[
            jax.ShapeDtypeStruct((bands, chans // bands, rows, lons), BF16),
            jax.ShapeDtypeStruct(tall, BF16),
        ],
        scratch_shapes=[
            pltpu.VMEM((pieces, rows, chans, lanes), BF16),
            pltpu.VMEM((lanes // 128, rows * chans, 128), F32),
            pltpu.VMEM((pieces, chans, rows, lanes), BF16),
            pltpu.VMEM(tall, BF16),
            [
                pltpu.SemaphoreType.DMA((pieces, bands - 1)),
                pltpu.SemaphoreType.DMA((pieces, bands - 1)),
                pltpu.SemaphoreType.DMA((pieces,)),
            ],
            pltpu.SemaphoreType.DMA((pieces + 1,)),
            pltpu.SemaphoreType.DMA((2, 4)),
        ],
        compiler_params=params(collective_id=3, has_side_effects=True),
        cost_estimate=cost(0, 4 * probe.size),
        name="open_exchange",
    )(probe, ocean)


def probe_flux_kernel(probe_ref, weight_ref, out_ref):
    weight = weight_ref[...]
    rows = probe_ref.shape[1]
    for n in range(0, rows, 2):
        pair = [
            mm(weight, jnp.concatenate([probe_ref[0, m], probe_ref[1, m]], axis=0))
            for m in (n, n + 1)
        ]
        both = jnp.concatenate(pair, axis=0).astype(BF16)
        for j in range(out_ref.shape[0]):
            out_ref[j, n * 8 : n * 8 + 16, :] = both[:, j * 128 : (j + 1) * 128]


def probe_flux(probe, weight):
    probes, rows, chans, lons = probe.shape
    blocks = lons // 128
    step = 4
    return pl.pallas_call(
        probe_flux_kernel,
        grid=(rows // step,),
        in_specs=[
            pl.BlockSpec((probes, step, chans, lons), lambda i: (0, i, 0, 0)),
            whole(weight.shape),
        ],
        out_specs=pl.BlockSpec((blocks, step * 8, 128), lambda i: (0, i, 0)),
        out_shape=jax.ShapeDtypeStruct((blocks, rows * 8, 128), BF16),
        compiler_params=params(),
        cost_estimate=cost(2 * 8 * probe.size, 2 * probe.size),
        name="probe_flux",
    )(probe, weight)


def filter_kernel(in_ref, fwd_ref, inv_ref, filt_ref, diff_ref, out_ref, wide, back):
    bands, _, pair, lons = in_ref.shape
    rows = pair // 2
    blocks = out_ref.shape[1]

    def load(b, carry):
        piece = in_ref[b, 0].astype(F32)
        at = pl.ds(pl.multiple_of(b * rows, 8), rows)
        wide[at, 0:lons] = piece[0:rows]
        wide[at, lons : 2 * lons] = piece[rows:pair]
        return carry

    lax.fori_loop(0, bands, load, 0)
    fwd = fwd_ref[...]
    inv = inv_ref[...]
    filt = filt_ref[0]
    chunk = 512

    def lat_filter(t, carry):
        at = pl.ds(pl.multiple_of(t * chunk, chunk), chunk)
        value = wide[:, at]
        filtered = (mm(fwd, value.astype(BF16)) * filt).astype(BF16)
        returned = mm(inv, filtered)
        back[:, at] = returned.astype(BF16)
        wide[:, at] = value + returned
        return carry

    lax.fori_loop(0, 2 * lons // chunk, lat_filter, 0)
    for p in range(2):
        for t in range(lons // 256):
            at = slice(p * lons + t * 256, p * lons + (t + 1) * 256)
            wide[:, at] = wide[:, at] + mm(
                back[:, p * lons : (p + 1) * lons], diff_ref[:, t * 256 : (t + 1) * 256]
            )

    def store(b, carry):
        at = pl.ds(pl.multiple_of(b * rows, 8), rows)
        for j in range(blocks):
            cols = slice(j * 128, (j + 1) * 128)
            more = slice(lons + j * 128, lons + (j + 1) * 128)
            out_ref[b, j, 0] = jnp.concatenate([wide[at, cols], wide[at, more]], axis=0).astype(
                BF16
            )
        return carry

    lax.fori_loop(0, bands, store, 0)


def lat_filter(received, fwd, inv, filt, diff):
    bands, chans, pair, lons = received.shape
    lats = fwd.shape[0]
    blocks = lons // 128
    return pl.pallas_call(
        filter_kernel,
        grid=(chans,),
        in_specs=[
            pl.BlockSpec((bands, 1, pair, lons), lambda i: (0, i, 0, 0)),
            whole(fwd.shape),
            whole(inv.shape),
            pl.BlockSpec((1, lats, 1), lambda i: (i, 0, 0)),
            whole(diff.shape),
        ],
        out_specs=pl.BlockSpec((bands, blocks, 1, pair, 128), lambda i: (0, 0, i, 0, 0)),
        out_shape=jax.ShapeDtypeStruct((bands, blocks, chans, pair, 128), BF16),
        scratch_shapes=[pltpu.VMEM((lats, 2 * lons), F32), pltpu.VMEM((lats, 2 * lons), BF16)],
        compiler_params=params(),
        cost_estimate=cost(8.4e9, 4 * received.size),
        name="lat_filter",
    )(received, fwd, inv, filt, diff)


def point_kernel(
    mixed_ref,
    slope_ref,
    win_ref,
    wout_ref,
    pflux_ref,
    cells_ref,
    first_ref,
    second_ref,
    picked_ref,
    wide,
    flux,
):
    chans, pair, lanes = mixed_ref.shape
    rows = pair // 2
    step = pl.program_id(0)

    @pl.when(step == 0)
    def _():
        def load(i, carry):
            at = pl.ds(pl.multiple_of(i * 8, 8), 8)
            wide[pl.ds(pl.multiple_of(i * 8 * pair, 8), 8 * pair), :] = (
                mixed_ref[at].astype(F32).reshape(8 * pair, lanes)
            )
            return carry

        lax.fori_loop(0, chans // 8, load, 0)

    value = jnp.concatenate(
        [wide[pl.ds(step + p * rows, chans, stride=pair), :] for p in range(2)], axis=1
    ).astype(BF16)
    slope = slope_ref[0].astype(F32)
    hidden = mm(win_ref[...], value)
    gated = (jnp.concatenate([slope, slope], axis=1) * hidden).astype(BF16)
    update = mm(wout_ref[...], gated)
    width = first_ref.shape[2]
    for j in range(first_ref.shape[0]):
        piece = update[j * width : (j + 1) * width].astype(BF16)
        first_ref[j, 0] = piece[:, 0:lanes]
        second_ref[j, 0] = piece[:, lanes : 2 * lanes]
    terms = update[chans : chans + 8]
    which = lax.broadcasted_iota(jnp.int32, (8, lanes), 0)
    flux[pl.ds(pl.multiple_of(step * 8, 8), 8), :] = jnp.where(
        which < 4, terms[:, 0:lanes], terms[:, lanes : 2 * lanes]
    )

    @pl.when(step == rows - 1)
    def _():
        total = flux[...]
        for j in range(pflux_ref.shape[0]):
            total = total + pflux_ref[j].astype(F32)
        total = total.astype(BF16)
        place = lax.broadcasted_iota(jnp.int32, (lanes, lanes), 0)
        for r in range(cells_ref.shape[0]):
            cells = cells_ref[r : r + 1, :]
            row = cells // lanes
            hot = jnp.where(place == cells - row * lanes, 1.0, 0.0).astype(BF16)
            found = mm(total, hot)
            picked = jnp.zeros((8, lanes), F32)
            for n in range(rows):
                picked = picked + jnp.where(row == n, found[n * 8 : (n + 1) * 8], 0.0)
            picked_ref[r] = picked


def pointwise(mixed, slope, win, wout, pflux, cells, blocks):
    chans, pair, lanes = mixed.shape
    rows, hid, _ = slope.shape
    width = chans // blocks
    return pl.pallas_call(
        point_kernel,
        grid=(rows,),
        in_specs=[
            whole(mixed.shape),
            pl.BlockSpec((1, hid, lanes), lambda i: (i, 0, 0)),
            whole(win.shape),
            whole(wout.shape),
            whole(pflux.shape),
            whole(cells.shape),
        ],
        out_specs=[
            pl.BlockSpec((blocks, 1, width, lanes), lambda i: (0, i, 0, 0)),
            pl.BlockSpec((blocks, 1, width, lanes), lambda i: (0, i, 0, 0)),
            whole((cells.shape[0], 8, lanes)),
        ],
        out_shape=[
            jax.ShapeDtypeStruct((blocks, rows, width, lanes), BF16),
            jax.ShapeDtypeStruct((blocks, rows, width, lanes), BF16),
            jax.ShapeDtypeStruct((cells.shape[0], 8, lanes), F32),
        ],
        scratch_shapes=[
            pltpu.VMEM((chans * pair, lanes), F32),
            pltpu.VMEM((rows * 8, lanes), F32),
        ],
        compiler_params=params(),
        cost_estimate=cost(7.3e9, 4 * mixed.size + 2 * slope.size),
        name="pointwise",
    )(mixed, slope, win, wout, pflux, cells)


def add_kernel(probe_ref, update_ref, *rest):
    out_ref = rest[-1]
    for j in range(update_ref.shape[0]):
        cols = slice(j * 128, (j + 1) * 128)
        out_ref[:, :, cols] = (
            probe_ref[:, :, cols].astype(F32) + update_ref[j].astype(F32)
        ).astype(BF16)


def add_update(probe, update, p, partial=None):
    rows, chans, lons = probe.shape
    blocks, count = update.shape[0], update.shape[1]
    step = 6
    base = p * (count // step)
    rest = () if partial is None else (partial,)
    return pl.pallas_call(
        add_kernel,
        grid=(count // step,),
        in_specs=[
            pl.BlockSpec((step, chans, lons), lambda i: (base + i, 0, 0)),
            pl.BlockSpec((blocks, step, chans, 128), lambda i: (0, i, 0, 0)),
        ]
        + [pl.BlockSpec(memory_space=pl.ANY) for _ in rest],
        out_specs=pl.BlockSpec((step, chans, lons), lambda i: (base + i, 0, 0)),
        out_shape=jax.ShapeDtypeStruct(probe.shape, BF16),
        input_output_aliases={2: 0} if rest else {},
        compiler_params=params(),
        cost_estimate=cost(update.size, 6 * update.size),
        name="add_update",
    )(probe, update, *rest)


def depth_sum(first, taps_ref, wide, done):
    halves, high = wide.shape[0], wide.shape[1]
    rows, cols = done.shape[0], done.shape[1]

    def tile(i, carry):
        at = pl.multiple_of(i * 8, 8)
        for h in range(halves):
            lanes = slice(h * 128, (h + 1) * 128)
            total = [jnp.zeros((8, 128), F32) for _ in range(rows)]
            for b in range(7):
                taps = [taps_ref[(7 * a + b) * 8 : (7 * a + b + 1) * 8, lanes] for a in range(7)]
                for y in range(high):
                    moved = wide[h, y, pl.ds(at + (first + b), 8), :]
                    for a in range(7):
                        if 0 <= y - a < rows:
                            total[y - a] = total[y - a] + moved * taps[a]
            for y in range(rows):
                done[y, pl.ds(at, 8), lanes] = total[y]
        return carry

    lax.fori_loop(0, cols // 8, tile, 0)


def depth_kernel(in_ref, taps_ref, out_ref, wide, done):
    high, _, chans, broad = in_ref.shape
    for y in range(high):
        value = in_ref[y, 0].astype(F32)
        for h in range(wide.shape[0]):
            top = min(128, chans - h * 128)
            part = value[h * 128 : h * 128 + top]
            wide[h, y, :, 0:top] = part.T
    depth_sum(125, taps_ref, wide, done)
    for y in range(done.shape[0]):
        out_ref[y] = done[y].T[0:chans]


def tap_rows(kernel):
    chans = kernel.shape[0]
    full = -(-chans // 128) * 128
    return jnp.repeat(jnp.pad(kernel.T, ((0, 0), (0, full - chans))), 8, axis=0)


def depthwise(around, kernel):
    high, probes, chans, broad = around.shape
    rows, cols = high - 6, broad - 256
    halves = -(-chans // 128)
    taps = tap_rows(kernel)
    return pl.pallas_call(
        depth_kernel,
        grid=(probes,),
        in_specs=[
            pl.BlockSpec((high, 1, chans, broad), lambda p: (0, p, 0, 0)),
            whole(taps.shape),
        ],
        out_specs=pl.BlockSpec((rows, chans, cols), lambda p: (0, 0, p)),
        out_shape=jax.ShapeDtypeStruct((rows, chans, probes * cols), F32),
        scratch_shapes=[
            pltpu.VMEM((halves, high, broad, 128), F32),
            pltpu.VMEM((rows, cols, halves * 128), F32),
        ],
        compiler_params=params(),
        cost_estimate=cost(200 * rows * cols * chans * probes, 4 * around.size),
        name="depthwise",
    )(around, taps)


def flux_kernel(
    blocks, picked_ref, slots_ref, weights_ref, mask_ref, out_ref, pool_ref, tall, send, recv, edge
):
    bands, fields, cap = picked_ref.shape
    rows, cols = mask_ref.shape
    band, block = lax.axis_index("lat"), lax.axis_index("chan")
    lat_before, lat_after, chan_before, chan_after = neighbours(bands, blocks)
    tall[...] = jnp.zeros_like(tall)
    pool_ref[pl.ds(band, 1)] = picked_ref[pl.ds(band, 1)]
    others = [(lax.rem(band + k, bands), block) for k in range(1, bands)]
    greet((chan_before, chan_after), others)

    copies = []
    for k, where in enumerate(others):
        copy = pltpu.make_async_remote_copy(
            picked_ref.at[where[0]],
            pool_ref.at[band],
            send.at[k],
            recv.at[k],
            device_id=where,
            device_id_type=MESH,
        )
        copy.start()
        copies.append(copy)
    for copy in copies:
        copy.wait()

    pool = pool_ref[...].reshape(bands * fields, cap).astype(BF16)
    place = lax.broadcasted_iota(jnp.int32, (cap, cols), 0)
    for y in range(rows):
        at = slice(y * cols, (y + 1) * cols)
        total = jnp.zeros((fields, cols), F32)
        for k in range(slots_ref.shape[0]):
            slots = slots_ref[k : k + 1, at]
            weights = weights_ref[k : k + 1, at]
            source = slots // cap
            hot = jnp.where(place == slots - source * cap, 1.0, 0.0).astype(BF16)
            found = mm(pool, hot)
            for b in range(bands):
                total = total + found[b * fields : (b + 1) * fields] * jnp.where(
                    source == b, weights, 0.0
                )
        tall[3 + y, :, 128 : 128 + cols] = total * mask_ref[y : y + 1, :]

    inner = pl.ds(128, cols)
    swap_edges(
        tall.at[pl.ds(3, 3), :, inner],
        tall.at[pl.ds(rows, 3), :, inner],
        edge.at[0],
        lat_before,
        lat_after,
        tall.at[pl.ds(rows + 3, 3), :, inner],
        tall.at[pl.ds(0, 3), :, inner],
    )
    swap_edges(
        tall.at[:, :, pl.ds(128, 128)],
        tall.at[:, :, pl.ds(cols, 128)],
        edge.at[1],
        chan_before,
        chan_after,
        tall.at[:, :, pl.ds(128 + cols, 128)],
        tall.at[:, :, pl.ds(0, 128)],
    )
    out_ref[...] = tall[...]


def flux_tile(picked, slots, weights, mask, blocks):
    bands, fields, _ = picked.shape
    rows, cols = mask.shape
    shape = (rows + 6, fields, cols + 256)
    return pl.pallas_call(
        functools.partial(flux_kernel, blocks),
        in_specs=[whole(a.shape) for a in (picked, slots, weights, mask)],
        out_specs=whole(shape),
        out_shape=jax.ShapeDtypeStruct(shape, F32),
        scratch_shapes=[
            pltpu.VMEM(picked.shape, F32),
            pltpu.VMEM(shape, F32),
            pltpu.SemaphoreType.DMA((bands - 1,)),
            pltpu.SemaphoreType.DMA((bands - 1,)),
            pltpu.SemaphoreType.DMA((2, 4)),
        ],
        compiler_params=params(collective_id=1, has_side_effects=True),
        name="flux_tile",
    )(picked, slots, weights, mask)


def edge_kernel(bands, blocks, field_ref, out_ref, tall, edge, own):
    lines, _, cols, _ = field_ref.shape
    lat_before, lat_after, chan_before, chan_after = neighbours(bands, blocks)
    tall[...] = jnp.zeros_like(tall)
    greet((lat_before, lat_after, chan_before, chan_after))
    inner = pl.ds(16, cols)
    copy = pltpu.make_async_copy(field_ref, tall.at[pl.ds(3, lines), :, inner, :], own)
    copy.start()
    swap_edges(
        field_ref.at[pl.ds(0, 3)],
        field_ref.at[pl.ds(lines - 3, 3)],
        edge.at[0],
        lat_before,
        lat_after,
        tall.at[pl.ds(lines + 3, 3), :, inner, :],
        tall.at[pl.ds(0, 3), :, inner, :],
    )
    copy.wait()
    swap_edges(
        tall.at[:, :, pl.ds(16, 16), :],
        tall.at[:, :, pl.ds(cols, 16), :],
        edge.at[1],
        chan_before,
        chan_after,
        tall.at[:, :, pl.ds(16 + cols, 16), :],
        tall.at[:, :, pl.ds(0, 16), :],
    )
    out_ref[...] = tall[...]


def coarse_edges(field, bands, blocks):
    lines, probes, cols, chans = field.shape
    shape = (lines + 6, probes, cols + 32, chans)
    return pl.pallas_call(
        functools.partial(edge_kernel, bands, blocks),
        in_specs=[whole(field.shape)],
        out_specs=whole(shape),
        out_shape=jax.ShapeDtypeStruct(shape, BF16),
        scratch_shapes=[
            pltpu.VMEM(shape, BF16),
            pltpu.SemaphoreType.DMA((2, 4)),
            pltpu.SemaphoreType.DMA,
        ],
        compiler_params=params(collective_id=2, has_side_effects=True),
        name="coarse_edges",
    )(field)


def normed_step(spread, base, sigma, gain):
    chans = spread.shape[0]
    wide_base = jnp.concatenate([base, base], axis=1)
    center = jnp.sum(spread, axis=0, keepdims=True) * (1.0 / chans)
    along = jnp.sum(wide_base * spread, axis=0, keepdims=True) * (1.0 / chans)
    scale = jnp.concatenate([sigma, sigma], axis=1)
    return (gain * scale * (spread - center - wide_base * along)).astype(BF16)


def fine_kernel(
    spread_ref,
    probe_ref,
    flux_ref,
    mask_ref,
    sigma_ref,
    base_ref,
    slope_ref,
    gain_ref,
    mix_ref,
    couple_ref,
    expand_ref,
    shrink_ref,
    pool_ref,
    down_ref,
    turn_ref,
    one_ref,
    coarse_ref,
    turned_ref,
    columns,
    held,
):
    step = pl.program_id(0)
    high = flux_ref.shape[0]
    cols = flux_ref.shape[2] - 256

    @pl.when(step == 0)
    def _():
        for y in range(high):
            row = flux_ref[y]
            for b in range(7):
                columns[(y * 7 + b) * 8 : (y * 7 + b + 1) * 8, :] = row[:, 125 + b : 125 + b + cols]

    near = columns[pl.ds(pl.multiple_of(step * 56, 8), 392), :].astype(BF16)
    center = columns[pl.ds(pl.multiple_of((step + 3) * 56 + 24, 8), 8), :].astype(BF16)
    spread = spread_ref[0] + jnp.concatenate([mm(mix_ref[p], near) for p in range(2)], axis=1)
    forcing = jnp.concatenate([mm(couple_ref[p], center) for p in range(2)], axis=1)
    probe = jnp.concatenate([probe_ref[0, 0], probe_ref[0, 1]], axis=1).astype(F32)
    start = (probe + forcing).astype(BF16).astype(F32)
    at = pl.ds(step, 1)
    tangent = normed_step(spread, base_ref[0].astype(F32), sigma_ref[at, :], gain_ref[...])
    slope = slope_ref[0].astype(F32)
    hidden = mm(expand_ref[...], tangent)
    gated = (hidden * jnp.concatenate([slope, slope], axis=1)).astype(BF16)
    mask = mask_ref[at, :]
    one = ((start + mm(shrink_ref[...], gated)) * jnp.concatenate([mask, mask], axis=1)).astype(BF16)
    one_ref[0] = one
    pooled = mm(one, pool_ref[...])

    @pl.when(step % 2 == 0)
    def _():
        held[...] = pooled

    @pl.when(step % 2 == 1)
    def _():
        both = (held[...] + pooled).astype(BF16)
        coarse_ref[0] = mm(down_ref[...], both).astype(BF16)
        turned = mm(both.T, turn_ref[...]).astype(BF16)
        half = turned.shape[0] // 2
        turned_ref[0, 0] = turned[0:half]
        turned_ref[0, 1] = turned[half : 2 * half]


def fine_level(spread, probe, flux, mask, sigma, base, slope, gain, mix, couple, expand, shrink, pool, down, turn):
    rows, chans, wide = spread.shape
    cols = wide // 2
    coarse = down.shape[0]
    row = lambda i: (i, 0, 0)
    return pl.pallas_call(
        fine_kernel,
        grid=(rows,),
        in_specs=[
            pl.BlockSpec((1, chans, wide), row),
            pl.BlockSpec((1,) + probe.shape[1:], lambda i: (i, 0, 0, 0)),
            whole(flux.shape),
            whole(mask.shape),
            whole(sigma.shape),
            pl.BlockSpec((1, chans, cols), row),
            pl.BlockSpec((1, slope.shape[1], cols), row),
            whole(gain.shape),
            whole(mix.shape),
            whole(couple.shape),
            whole(expand.shape),
            whole(shrink.shape),
            whole(pool.shape),
            whole(down.shape),
            whole(turn.shape),
        ],
        out_specs=[
            pl.BlockSpec((1, chans, wide), row),
            pl.BlockSpec((1, coarse, cols), lambda i: (i // 2, 0, 0)),
            pl.BlockSpec((1, 2, cols // 2, turn.shape[1]), lambda i: (i // 2, 0, 0, 0)),
        ],
        out_shape=[
            jax.ShapeDtypeStruct((rows, chans, wide), BF16),
            jax.ShapeDtypeStruct((rows // 2, coarse, cols), BF16),
            jax.ShapeDtypeStruct((rows // 2, 2, cols // 2, turn.shape[1]), BF16),
        ],
        scratch_shapes=[
            pltpu.VMEM((flux.shape[0] * 56, cols), F32),
            pltpu.VMEM((chans, cols), F32),
        ],
        compiler_params=params(),
        name="fine_level",
    )(spread, probe, flux, mask, sigma, base, slope, gain, mix, couple, expand, shrink, pool, down, turn)


def coarse_kernel(
    around_ref,
    taps_ref,
    field_ref,
    sigma_ref,
    base_ref,
    slope_ref,
    gain_ref,
    expand_ref,
    shrink_ref,
    spreadout_ref,
    up_ref,
    one_ref,
    mask_ref,
    out_ref,
    wide,
    tall,
    done,
    spread,
):
    step = pl.program_id(0)
    chans = field_ref.shape[1]
    probes, fine, rows, cols = out_ref.shape

    @pl.when(step == 0)
    def _():
        half = done.shape[1]
        for p in range(probes):
            for y in range(tall.shape[1]):
                for h in range(tall.shape[0]):
                    top = min(128, chans - h * 128)
                    tall[h, y, :, 0:top] = around_ref[y, p, :, h * 128 : h * 128 + top].astype(F32)
            depth_sum(13, taps_ref, tall, done)
            for y in range(done.shape[0]):
                spread[y, :, p * half : (p + 1) * half] = done[y].T[0:chans]

    at = pl.ds(step, 1)
    tangent = normed_step(
        spread[step], base_ref[0].astype(F32), sigma_ref[at, :], gain_ref[...]
    )
    slope = slope_ref[0].astype(F32)
    hidden = mm(expand_ref[...], tangent)
    gated = (hidden * jnp.concatenate([slope, slope], axis=1)).astype(BF16)
    two = (field_ref[0].astype(F32) + mm(shrink_ref[...], gated)).astype(BF16)
    raised = mm(up_ref[...], mm(two, spreadout_ref[...]).astype(BF16))
    for half in range(2):
        y = step * 2 + half
        mask = mask_ref[pl.ds(y, 1), :]
        for p in range(probes):
            for t in range(cols // 128):
                lanes = slice(p * cols + t * 128, p * cols + (t + 1) * 128)
                wide[p, t, pl.ds(y, fine, stride=rows), :] = (
                    one_ref[half, :, lanes].astype(F32) + raised[:, lanes]
                ) * mask[:, t * 128 : (t + 1) * 128]

    @pl.when(step == rows // 2 - 1)
    def _():
        for p in range(probes):
            for t in range(cols // 128):
                out_ref[p, :, :, t * 128 : (t + 1) * 128] = (
                    wide[p, t].reshape(fine, rows, 128).astype(BF16)
                )


def coarse_level(
    around, kernel, field, sigma, base, slope, gain, expand, shrink, spreadout, up, one, mask
):
    lines, chans, double = field.shape
    half = double // 2
    rows, fine, wide = one.shape
    cols = wide // 2
    taps = tap_rows(kernel)
    row = lambda i: (i, 0, 0)
    return pl.pallas_call(
        coarse_kernel,
        grid=(lines,),
        in_specs=[
            whole(around.shape),
            whole(taps.shape),
            pl.BlockSpec((1, chans, double), row),
            whole(sigma.shape),
            pl.BlockSpec((1, chans, half), row),
            pl.BlockSpec((1, slope.shape[1], half), row),
            whole(gain.shape),
            whole(expand.shape),
            whole(shrink.shape),
            whole(spreadout.shape),
            whole(up.shape),
            pl.BlockSpec((2, fine, wide), row),
            whole(mask.shape),
        ],
        out_specs=whole((2, fine, rows, cols)),
        out_shape=jax.ShapeDtypeStruct((2, fine, rows, cols), BF16),
        scratch_shapes=[
            pltpu.VMEM((2, cols // 128, fine * rows, 128), F32),
            pltpu.VMEM((taps.shape[1] // 128, around.shape[0], around.shape[2], 128), F32),
            pltpu.VMEM((lines, half, taps.shape[1]), F32),
            pltpu.VMEM((lines, chans, double), F32),
        ],
        compiler_params=params(),
        cost_estimate=cost(1e9, 4e6),
        name="coarse_level",
    )(around, taps, field, sigma, base, slope, gain, expand, shrink, spreadout, up, one, mask)


def local(
    probe_field,
    gate_slope,
    spectral_filter,
    weight_in,
    weight_out,
    weight_flux,
    send_cells,
    recv_slots,
    recv_weights,
    ocean_probe,
    ocean_mask,
    coupling,
    base_fine,
    sigma_fine,
    slope_fine,
    gain_fine,
    kernel_fine,
    expand_fine,
    shrink_fine,
    down_proj,
    base_coarse,
    sigma_coarse,
    slope_coarse,
    gain_coarse,
    kernel_coarse,
    expand_coarse,
    shrink_coarse,
    up_proj,
):
    probes, rows, width, lons = probe_field.shape
    bands = lax.axis_size("lat")
    blocks = lax.axis_size("chan")
    part = width // bands
    pair = probes * rows
    lats = rows * bands
    chans = width * blocks
    fields = weight_flux.shape[1]

    flat_probe = probe_field.reshape(pair, width, lons)

    flux_rows = lax.dynamic_slice_in_dim(
        weight_flux, lax.axis_index("chan") * width, width, 0
    ).T
    none = jnp.zeros_like(flux_rows)
    flux_pair = jnp.concatenate(
        [
            jnp.concatenate([flux_rows, none], axis=1),
            jnp.concatenate([none, flux_rows], axis=1),
        ],
        axis=0,
    )
    terms = probe_flux(probe_field, flux_pair)

    tile_rows, tile_cols = ocean_mask.shape
    fine = ocean_probe.shape[1]
    mask = ocean_mask.astype(F32)
    start = ocean_rows(ocean_probe, mask)
    base_rows = base_fine.transpose(1, 0, 2)
    slope_rows = slope_fine.transpose(1, 0, 2)
    base_lines = base_coarse.transpose(1, 0, 2)
    slope_lines = slope_coarse.transpose(1, 0, 2)
    couple_t = coupling.T
    no_couple = jnp.zeros_like(couple_t)
    couple = jnp.stack(
        [
            jnp.concatenate([couple_t, no_couple], axis=1),
            jnp.concatenate([no_couple, couple_t], axis=1),
        ]
    )
    mix = (kernel_fine[None, :, :, None] * couple.astype(F32)[:, :, None, :]).astype(BF16)
    mix = mix.reshape(probes, fine, 49 * probes * fields)
    lane = jnp.arange(probes * tile_cols, dtype=jnp.int32)
    meets = lane[:, None] // 2 == jnp.arange(probes * tile_cols // 2, dtype=jnp.int32)[None, :]
    pool = jnp.where(meets, 0.25, 0.0).astype(BF16)
    spreadout = jnp.where(meets.T, 1.0, 0.0).astype(BF16)

    gathered, around = open_exchange(flat_probe, start, bands, blocks)

    fwd_lat, inv_lat = cosine_tables(lats)
    diff = jnp.asarray(fourier_product(lons))
    filt = lax.dynamic_slice_in_dim(
        spectral_filter, lax.axis_index("lat") * part, part, 1
    ).T.reshape(part, lats, 1)
    gathered, filt = lax.optimization_barrier((gathered, filt))
    mixed = lat_filter(gathered, jnp.asarray(fwd_lat.T), jnp.asarray(inv_lat.T), filt, diff)
    regrouped = lax.all_to_all(
        mixed.reshape(bands * blocks, part, pair, 128),
        ("lat", "chan"),
        split_axis=0,
        concat_axis=0,
        tiled=True,
    ).reshape(chans, pair, 128)

    win = (
        weight_in.reshape(blocks, bands, part, -1).transpose(1, 0, 2, 3).reshape(chans, -1).T
    )
    folded = mm(weight_out, weight_flux).astype(BF16)
    wout = jnp.concatenate([weight_out, folded, folded], axis=1).T
    probe_terms = lax.psum_scatter(terms, "chan", scatter_dimension=0, tiled=True)
    spread = depthwise(around, kernel_fine)
    (
        regrouped,
        spread,
        win,
        wout,
        probe_terms,
        base_rows,
        slope_rows,
        base_lines,
        slope_lines,
        mix,
        couple,
        pool,
        spreadout,
        mask,
    ) = lax.optimization_barrier(
        (
            regrouped,
            spread,
            win,
            wout,
            probe_terms,
            base_rows,
            slope_rows,
            base_lines,
            slope_lines,
            mix,
            couple,
            pool,
            spreadout,
            mask,
        )
    )
    first, second, picked = pointwise(
        regrouped, gate_slope, win, wout, probe_terms, send_cells[0], blocks
    )

    tall = flux_tile(picked, recv_slots[0], recv_weights[0], mask, blocks)
    first, tall = lax.optimization_barrier((first, tall))
    first = lax.all_to_all(first, "chan", split_axis=0, concat_axis=0, tiled=True)
    one, coarse, turned = fine_level(
        spread,
        start,
        tall,
        mask,
        sigma_fine,
        base_rows,
        slope_rows,
        gain_fine[:, None],
        mix,
        couple,
        expand_fine.T,
        shrink_fine.T,
        pool,
        down_proj.T,
        jnp.pad(down_proj, ((0, 0), (0, 256 - down_proj.shape[1]))),
    )
    around = coarse_edges(turned, bands, blocks)
    second, around = lax.optimization_barrier((second, around))
    second = lax.all_to_all(second, "chan", split_axis=0, concat_axis=0, tiled=True)
    ocean_out = coarse_level(
        around,
        kernel_coarse,
        coarse,
        sigma_coarse,
        base_lines,
        slope_lines,
        gain_coarse[:, None],
        expand_coarse.T,
        shrink_coarse.T,
        spreadout,
        up_proj.T,
        one,
        mask,
    )
    partial = add_update(flat_probe, first, 0)
    atmos_out = add_update(flat_probe, second, 1, partial).reshape(probe_field.shape)
    return (atmos_out, ocean_out)


def solution(mesh):
    tile = P(("lat", "chan"), None, None)
    rows_cols = P(None, "lat", "chan")
    return jax.shard_map(
        local,
        mesh=mesh,
        in_specs=(
            P(None, "lat", "chan", None),
            P("lat", None, "chan"),
            P(None, "chan"),
            P(),
            P(),
            P(),
            tile,
            tile,
            tile,
            P(None, None, "lat", "chan"),
            P("lat", "chan"),
            P(),
            rows_cols,
            P("lat", "chan"),
            rows_cols,
            P(),
            P(),
            P(),
            P(),
            P(),
            rows_cols,
            P("lat", "chan"),
            rows_cols,
            P(),
            P(),
            P(),
            P(),
            P(),
        ),
        out_specs=(P(None, "lat", "chan", None), P(None, None, "lat", "chan")),
        check_vma=False,
    )
```

```python
import functools
import math

import jax
import jax.numpy as jnp
import ml_dtypes
import numpy as np
from jax import lax
from jax.experimental import pallas as pl
from jax.experimental.pallas import tpu as pltpu
from jax.sharding import PartitionSpec as P

F32 = jnp.float32
BF16 = jnp.bfloat16
MESH = pl.DeviceIdType.MESH
VMEM_LIMIT = 56 * 1024 * 1024


def params(**more):
    return pltpu.CompilerParams(vmem_limit_bytes=VMEM_LIMIT, **more)


def cost(flops, nbytes):
    return pl.CostEstimate(flops=int(flops), bytes_accessed=int(nbytes), transcendentals=0)


def mm(a, b):
    return jnp.dot(a, b, preferred_element_type=F32)


def whole(shape):
    zeros = (0,) * len(shape)
    return pl.BlockSpec(shape, lambda *_: zeros)


def fourier_product(count):
    column = np.arange(count)
    half = count // 2
    wave = np.where(column <= half, column, column - half)
    angles = (column[:, None] * wave[None, :] % count) * (2.0 * math.pi / count)
    basis = np.where((column <= half)[None, :], np.cos(angles), np.sin(angles))
    forward = (basis / count).astype(ml_dtypes.bfloat16)
    factor = np.where((column == 0) | (column == half), 1.0, 2.0)
    inverse = (basis.T * factor[:, None]).astype(ml_dtypes.bfloat16)
    product = forward.astype(np.float64) @ inverse.astype(np.float64)
    return (product - np.eye(count)).astype(ml_dtypes.bfloat16)


def cosine_tables(count):
    degree = np.arange(count)
    phase = degree[None, :] * (2 * degree[:, None] + 1) % (4 * count)
    basis = np.cos(phase * (math.pi / (2 * count)))
    forward = (basis / count).astype(ml_dtypes.bfloat16)
    factor = np.where(degree == 0, 1.0, 2.0)
    inverse = (basis.T * factor[:, None]).astype(ml_dtypes.bfloat16)
    return (forward, inverse)


def greet(partners, more=()):
    barrier = pltpu.get_barrier_semaphore()
    for where in more:
        pl.semaphore_signal(barrier, inc=1, device_id=where, device_id_type=MESH)
    count = jnp.int32(len(more))
    for there, where in partners:

        @pl.when(there)
        def _(where=where):
            pl.semaphore_signal(barrier, inc=1, device_id=where, device_id_type=MESH)

        count = count + there.astype(jnp.int32)
    pl.semaphore_wait(barrier, count)


def start_edges(low, high, sems, before, after, low_to, high_to):
    is_before, device_before = before
    is_after, device_after = after

    def to_before():
        return pltpu.make_async_remote_copy(
            low, low_to, sems.at[0], sems.at[1], device_id=device_before, device_id_type=MESH
        )

    def to_after():
        return pltpu.make_async_remote_copy(
            high, high_to, sems.at[2], sems.at[3], device_id=device_after, device_id_type=MESH
        )

    @pl.when(is_before)
    def _():
        to_before().start()

    @pl.when(is_after)
    def _():
        to_after().start()

    def finish():
        @pl.when(is_before)
        def _():
            to_before().wait_send()
            to_after().wait_recv()

        @pl.when(is_after)
        def _():
            to_after().wait_send()
            to_before().wait_recv()

    return finish


def swap_edges(*args):
    start_edges(*args)()


def neighbours(bands, blocks):
    band, block = lax.axis_index("lat"), lax.axis_index("chan")
    return (
        (band > 0, (jnp.maximum(band - 1, 0), block)),
        (band < bands - 1, (jnp.minimum(band + 1, bands - 1), block)),
        (block > 0, (band, jnp.maximum(block - 1, 0))),
        (block < blocks - 1, (band, jnp.minimum(block + 1, blocks - 1))),
    )


def chan_peers(blocks):
    band, block = lax.axis_index("lat"), lax.axis_index("chan")
    return [(band, lax.rem(block + k, blocks)) for k in range(1, blocks)]


def homeward(update_ref, back_ref, first, sems):
    send, recv, own = sems
    blocks, _, count = back_ref.shape[:3]
    block = lax.axis_index("chan")
    some = pl.ds(first, count)
    copies = [
        pltpu.make_async_remote_copy(
            update_ref.at[where[1], :, some],
            back_ref.at[block],
            send.at[k],
            recv.at[k],
            device_id=where,
            device_id_type=MESH,
        )
        for k, where in enumerate(chan_peers(blocks))
    ]
    return copies + [
        pltpu.make_async_copy(update_ref.at[block, :, some], back_ref.at[block], own.at[0])
    ]


def homeward_sems(blocks):
    return [
        pltpu.SemaphoreType.DMA((blocks - 1,)),
        pltpu.SemaphoreType.DMA((blocks - 1,)),
        pltpu.SemaphoreType.DMA((1,)),
    ]


def homeward_shape(update, count):
    blocks, probes, _, width, lanes = update.shape
    return jax.ShapeDtypeStruct((blocks, probes, count, width, lanes), BF16)


SENT_GROUPS = 2
SENT = ((8, 4), (12, 4), (16, 8))
ANYWHERE = pl.BlockSpec(memory_space=pl.ANY)


def ocean_rows_kernel(in_ref, mask_ref, out_ref, wide):
    _, chans, rows, cols = in_ref.shape
    value = in_ref[0].astype(F32) * mask_ref[...][None]
    for t in range(cols // 128):
        wide[t] = value[:, :, t * 128 : (t + 1) * 128].reshape(chans * rows, 128)
    for y in range(rows):
        for t in range(cols // 128):
            out_ref[y, 0, :, t * 128 : (t + 1) * 128] = wide[
                t, pl.ds(y, chans, stride=rows), :
            ].astype(BF16)


def ocean_rows(field, mask):
    probes, chans, rows, cols = field.shape
    return pl.pallas_call(
        ocean_rows_kernel,
        grid=(probes,),
        in_specs=[
            pl.BlockSpec((1, chans, rows, cols), lambda p: (p, 0, 0, 0)),
            whole(mask.shape),
        ],
        out_specs=pl.BlockSpec((rows, 1, chans, cols), lambda p: (0, p, 0, 0)),
        out_shape=jax.ShapeDtypeStruct((rows, probes, chans, cols), BF16),
        scratch_shapes=[pltpu.VMEM((cols // 128, chans * rows, 128), F32)],
        compiler_params=params(),
        cost_estimate=cost(field.size, 4 * field.size),
        name="ocean_rows",
    )(field, mask)


STEPS = (
    ((0, 1), (1, 0), (0, 3), (3, 0), (1, 1), (3, 3), (1, 3), (3, 1))
    + ((0, 2), (2, 0), (2, 2), (1, 2), (2, 1), (3, 2), (2, 3))
)


def lat_partner(band, step, side):
    dz, dx = step
    return lax.rem(band // side + dz, side) * side + lax.rem(lax.rem(band, side) + dx, side)


def open_kernel(
    blocks, probe_ref, ocean_ref, out_ref, around_ref, taken, wide, turned, tall, sems, own, edge
):
    send, recv, load = sems
    rows, chans, lons = probe_ref.shape
    bands, part = out_ref.shape[0], out_ref.shape[1]
    side = math.isqrt(bands)
    lines, _, _, cols = ocean_ref.shape
    pieces, lanes = taken.shape[0], taken.shape[3]
    band, block = lax.axis_index("lat"), lax.axis_index("chan")
    lat_before, lat_after, chan_before, chan_after = neighbours(bands, blocks)

    def take(i):
        return pltpu.make_async_copy(
            probe_ref.at[:, :, pl.ds(i * lanes, lanes)], taken.at[i], load.at[i]
        )

    for i in range(pieces):
        take(i).start()
    tall[...] = jnp.zeros_like(tall)
    others = [(lat_partner(band, step, side), block) for step in STEPS]
    greet((chan_before, chan_after), others)
    inner = pl.ds(128, cols)
    center = pltpu.make_async_copy(ocean_ref, tall.at[pl.ds(3, lines), :, :, inner], own.at[0])
    center.start()
    finish_rows = start_edges(
        ocean_ref.at[pl.ds(0, 3)],
        ocean_ref.at[pl.ds(lines - 3, 3)],
        edge.at[0],
        lat_before,
        lat_after,
        tall.at[pl.ds(lines + 3, 3), :, :, inner],
        tall.at[pl.ds(0, 3), :, :, inner],
    )
    copies = []
    for i in range(pieces):
        take(i).wait()
        for t in range(lanes // 128):
            at = slice(t * 128, (t + 1) * 128)
            wide[t] = taken[i, :, :, at].astype(F32).reshape(rows * chans, 128)
            for c in range(chans):
                turned[i, c, :, at] = wide[t, pl.ds(c, rows, stride=chans), :].astype(BF16)
        columns = pl.ds(i * lanes, lanes)
        for k, where in enumerate(others):
            copy = pltpu.make_async_remote_copy(
                turned.at[i, pl.ds(where[0] * part, part)],
                out_ref.at[band, :, :, columns],
                send.at[i, k],
                recv.at[i, k],
                device_id=where,
                device_id_type=MESH,
            )
            copy.start()
            copies.append(copy)
        copy = pltpu.make_async_copy(
            turned.at[i, pl.ds(band * part, part)],
            out_ref.at[band, :, :, columns],
            own.at[i + 1],
        )
        copy.start()
        copies.append(copy)
    center.wait()
    finish_rows()
    finish_columns = start_edges(
        tall.at[:, :, :, pl.ds(128, 128)],
        tall.at[:, :, :, pl.ds(cols, 128)],
        edge.at[1],
        chan_before,
        chan_after,
        tall.at[:, :, :, pl.ds(128 + cols, 128)],
        tall.at[:, :, :, pl.ds(0, 128)],
    )
    finish_columns()
    store = pltpu.make_async_copy(tall, around_ref, own.at[0])
    store.start()
    for copy in copies:
        copy.wait()
    store.wait()


def open_exchange(probe, ocean, bands, blocks):
    rows, chans, lons = probe.shape
    lines, probes, fine, cols = ocean.shape
    pieces, lanes = 4, lons // 4
    any_spec = pl.BlockSpec(memory_space=pl.ANY)
    tall = (lines + 6, probes, fine, cols + 256)
    return pl.pallas_call(
        functools.partial(open_kernel, blocks),
        in_specs=[any_spec, any_spec],
        out_specs=[any_spec, any_spec],
        out_shape=[
            jax.ShapeDtypeStruct((bands, chans // bands, rows, lons), BF16),
            jax.ShapeDtypeStruct(tall, BF16),
        ],
        scratch_shapes=[
            pltpu.VMEM((pieces, rows, chans, lanes), BF16),
            pltpu.VMEM((lanes // 128, rows * chans, 128), F32),
            pltpu.VMEM((pieces, chans, rows, lanes), BF16),
            pltpu.VMEM(tall, BF16),
            [
                pltpu.SemaphoreType.DMA((pieces, bands - 1)),
                pltpu.SemaphoreType.DMA((pieces, bands - 1)),
                pltpu.SemaphoreType.DMA((pieces,)),
            ],
            pltpu.SemaphoreType.DMA((pieces + 1,)),
            pltpu.SemaphoreType.DMA((2, 4)),
        ],
        compiler_params=params(collective_id=3, has_side_effects=True),
        cost_estimate=cost(0, 4 * probe.size),
        name="open_exchange",
    )(probe, ocean)


def probe_flux_kernel(probe_ref, weight_ref, out_ref):
    weight = weight_ref[...]
    rows = probe_ref.shape[1]
    for n in range(0, rows, 2):
        pair = [
            mm(weight, jnp.concatenate([probe_ref[0, m], probe_ref[1, m]], axis=0))
            for m in (n, n + 1)
        ]
        both = jnp.concatenate(pair, axis=0).astype(BF16)
        for j in range(out_ref.shape[0]):
            out_ref[j, n * 8 : n * 8 + 16, :] = both[:, j * 128 : (j + 1) * 128]


def probe_flux(probe, weight):
    probes, rows, chans, lons = probe.shape
    blocks = lons // 128
    step = 4
    return pl.pallas_call(
        probe_flux_kernel,
        grid=(rows // step,),
        in_specs=[
            pl.BlockSpec((probes, step, chans, lons), lambda i: (0, i, 0, 0)),
            whole(weight.shape),
        ],
        out_specs=pl.BlockSpec((blocks, step * 8, 128), lambda i: (0, i, 0)),
        out_shape=jax.ShapeDtypeStruct((blocks, rows * 8, 128), BF16),
        compiler_params=params(),
        cost_estimate=cost(2 * 8 * probe.size, 2 * probe.size),
        name="probe_flux",
    )(probe, weight)


def filter_kernel(in_ref, fwd_ref, inv_ref, filt_ref, diff_ref, out_ref, wide, back):
    bands, _, pair, lons = in_ref.shape
    rows = pair // 2
    blocks = out_ref.shape[1]

    def load(b, carry):
        piece = in_ref[b, 0].astype(F32)
        at = pl.ds(pl.multiple_of(b * rows, 8), rows)
        wide[at, 0:lons] = piece[0:rows]
        wide[at, lons : 2 * lons] = piece[rows:pair]
        return carry

    lax.fori_loop(0, bands, load, 0)
    filt = filt_ref[0]
    for t in range(2):
        at = slice(t * lons, (t + 1) * lons)
        value = wide[:, at]
        filtered = (mm(fwd_ref[...], value.astype(BF16)) * filt).astype(BF16)
        returned = mm(inv_ref[...], filtered)
        back[:, at] = returned.astype(BF16)
        wide[:, at] = value + returned
    for p in range(2):
        for t in range(lons // 256):
            at = slice(p * lons + t * 256, p * lons + (t + 1) * 256)
            wide[:, at] = wide[:, at] + mm(
                back[:, p * lons : (p + 1) * lons], diff_ref[:, t * 256 : (t + 1) * 256]
            )

    def store(b, carry):
        at = pl.ds(pl.multiple_of(b * rows, 8), rows)
        for j in range(blocks):
            cols = slice(j * 128, (j + 1) * 128)
            more = slice(lons + j * 128, lons + (j + 1) * 128)
            out_ref[b, j, 0] = jnp.concatenate([wide[at, cols], wide[at, more]], axis=0).astype(
                BF16
            )
        return carry

    lax.fori_loop(0, bands, store, 0)


def lat_filter(received, fwd, inv, filt, diff):
    bands, chans, pair, lons = received.shape
    lats = fwd.shape[0]
    blocks = lons // 128
    return pl.pallas_call(
        filter_kernel,
        grid=(chans,),
        in_specs=[
            pl.BlockSpec((bands, 1, pair, lons), lambda i: (0, i, 0, 0)),
            whole(fwd.shape),
            whole(inv.shape),
            pl.BlockSpec((1, lats, 1), lambda i: (i, 0, 0)),
            whole(diff.shape),
        ],
        out_specs=pl.BlockSpec((bands, blocks, 1, pair, 128), lambda i: (0, 0, i, 0, 0)),
        out_shape=jax.ShapeDtypeStruct((bands, blocks, chans, pair, 128), BF16),
        scratch_shapes=[pltpu.VMEM((lats, 2 * lons), F32), pltpu.VMEM((lats, 2 * lons), BF16)],
        compiler_params=params(),
        cost_estimate=cost(8.4e9, 4 * received.size),
        name="lat_filter",
    )(received, fwd, inv, filt, diff)


GROUP = 4


def point_kernel(
    sent,
    mixed_ref,
    slope_ref,
    win_ref,
    wout_ref,
    pflux_ref,
    cells_ref,
    out_ref,
    picked_ref,
    *rest,
):
    back_refs = rest[:sent]
    wide, flux, ship, home_sems = rest[sent:]
    chans, pair, lanes = mixed_ref.shape
    rows = pair // 2
    step = pl.program_id(0)
    send, recv, own = home_sems
    blocks = out_ref.shape[0]
    block = lax.axis_index("chan")
    peers = chan_peers(blocks)

    def homeward_group(i):
        copies = [
            pltpu.make_async_remote_copy(
                ship.at[i, where[1]],
                back_refs[i].at[block],
                send.at[i, k],
                recv.at[i, k],
                device_id=where,
                device_id_type=MESH,
            )
            for k, where in enumerate(peers)
        ]
        return copies + [
            pltpu.make_async_copy(ship.at[i, block], back_refs[i].at[block], own.at[i])
        ]

    @pl.when(step == 0)
    def _():
        greet((), peers)

        def load(i, carry):
            at = pl.ds(pl.multiple_of(i * 8, 8), 8)
            wide[pl.ds(pl.multiple_of(i * 8 * pair, 8), 8 * pair), :] = (
                mixed_ref[at].astype(F32).reshape(8 * pair, lanes)
            )
            return carry

        lax.fori_loop(0, chans // 8, load, 0)

    which = lax.broadcasted_iota(jnp.int32, (8, lanes), 0)
    width = out_ref.shape[3]
    gated = []
    for g in range(GROUP):
        value = jnp.concatenate(
            [
                wide[pl.ds(step * GROUP + g + p * rows, chans, stride=pair), :]
                for p in range(2)
            ],
            axis=1,
        ).astype(BF16)
        slope = slope_ref[g].astype(F32)
        hidden = mm(win_ref[...], value)
        gated.append((jnp.concatenate([slope, slope], axis=1) * hidden).astype(BF16))
    for g in range(GROUP):
        update = mm(wout_ref[...], gated[g])
        for j in range(blocks):
            piece = update[j * width : (j + 1) * width].astype(BF16)
            out_ref[j, 0, g] = piece[:, 0:lanes]
            out_ref[j, 1, g] = piece[:, lanes : 2 * lanes]
        terms = update[chans : chans + 8]
        flux[pl.ds(pl.multiple_of((step * GROUP + g) * 8, 8), 8), :] = jnp.where(
            which < 4, terms[:, 0:lanes], terms[:, lanes : 2 * lanes]
        )

    for i in range(sent):

        @pl.when(step == i)
        def _(i=i):
            ship[i] = out_ref[...]
            for copy in homeward_group(i):
                copy.start()

    @pl.when(step == rows // GROUP - 1)
    def _():
        total = flux[...]
        for j in range(pflux_ref.shape[0]):
            total = total + pflux_ref[j].astype(F32)
        total = total.astype(BF16)
        place = lax.broadcasted_iota(jnp.int32, (lanes, lanes), 0)
        for r in range(cells_ref.shape[0]):
            cells = cells_ref[r : r + 1, :]
            row = cells // lanes
            hot = jnp.where(place == cells - row * lanes, 1.0, 0.0).astype(BF16)
            found = mm(total, hot)
            picked = jnp.zeros((8, lanes), F32)
            for n in range(rows):
                picked = picked + jnp.where(row == n, found[n * 8 : (n + 1) * 8], 0.0)
            picked_ref[r] = picked
        for i in range(sent):
            for copy in homeward_group(i):
                copy.wait()


def pointwise(mixed, slope, win, wout, pflux, cells, blocks, sent):
    chans, pair, lanes = mixed.shape
    rows, hid, _ = slope.shape
    width = chans // blocks
    shipped = (sent, blocks, 2, GROUP, width, lanes)
    return pl.pallas_call(
        functools.partial(point_kernel, sent),
        grid=(rows // GROUP,),
        in_specs=[
            whole(mixed.shape),
            pl.BlockSpec((GROUP, hid, lanes), lambda i: (i, 0, 0)),
            whole(win.shape),
            whole(wout.shape),
            whole(pflux.shape),
            whole(cells.shape),
        ],
        out_specs=[
            pl.BlockSpec((blocks, 2, GROUP, width, lanes), lambda i: (0, 0, i, 0, 0)),
            whole((cells.shape[0], 8, lanes)),
        ]
        + [ANYWHERE] * sent,
        out_shape=[
            jax.ShapeDtypeStruct((blocks, 2, rows, width, lanes), BF16),
            jax.ShapeDtypeStruct((cells.shape[0], 8, lanes), F32),
        ]
        + [jax.ShapeDtypeStruct(shipped[1:], BF16)] * sent,
        scratch_shapes=[
            pltpu.VMEM((chans * pair, lanes), F32),
            pltpu.VMEM((rows * 8, lanes), F32),
            pltpu.VMEM(shipped, BF16),
            [
                pltpu.SemaphoreType.DMA((sent, blocks - 1)),
                pltpu.SemaphoreType.DMA((sent, blocks - 1)),
                pltpu.SemaphoreType.DMA((sent,)),
            ],
        ],
        compiler_params=params(collective_id=6, has_side_effects=True),
        cost_estimate=cost(7.3e9, 4 * mixed.size + 2 * slope.size),
        name="pointwise",
    )(mixed, slope, win, wout, pflux, cells)


def add_kernel(starts, probe_ref, *refs):
    out_ref = refs[-1]
    step = pl.program_id(1)
    for k, update_ref in enumerate(refs[:-1]):

        @pl.when((step >= starts[k]) & (step < starts[k + 1]))
        def _(update_ref=update_ref):
            for j in range(update_ref.shape[0]):
                cols = slice(j * 128, (j + 1) * 128)
                out_ref[:, :, cols] = probe_ref[:, :, cols] + update_ref[j, 0]


def add_update(probe, parts):
    lines, chans, lons = probe.shape
    blocks = parts[0].shape[0]
    rows = lines // 2
    step = 4
    counts = [a.shape[2] // step for a in parts]
    starts = [sum(counts[:k]) for k in range(len(counts) + 1)]

    def spec(k):
        return pl.BlockSpec(
            (blocks, 1, step, chans, 128),
            lambda p, i: (0, p, jnp.clip(i - starts[k], 0, counts[k] - 1), 0, 0),
        )

    field = pl.BlockSpec((step, chans, lons), lambda p, i: (p * (rows // step) + i, 0, 0))
    return pl.pallas_call(
        functools.partial(add_kernel, starts),
        grid=(2, rows // step),
        in_specs=[field] + [spec(k) for k in range(len(parts))],
        out_specs=field,
        out_shape=jax.ShapeDtypeStruct(probe.shape, BF16),
        compiler_params=params(),
        cost_estimate=cost(probe.size, 6 * probe.size),
        name="add_update",
    )(probe, *parts)


def depth_sum(first, taps_ref, wide, done):
    halves, high = wide.shape[0], wide.shape[1]
    rows, cols = done.shape[0], done.shape[1]

    def tile(i, carry):
        at = pl.multiple_of(i * 8, 8)
        for h in range(halves):
            lanes = slice(h * 128, (h + 1) * 128)
            total = [jnp.zeros((8, 128), F32) for _ in range(rows)]
            for b in range(7):
                taps = [taps_ref[(7 * a + b) * 8 : (7 * a + b + 1) * 8, lanes] for a in range(7)]
                for y in range(high):
                    moved = wide[h, y, pl.ds(at + (first + b), 8), :]
                    for a in range(7):
                        if 0 <= y - a < rows:
                            total[y - a] = total[y - a] + moved * taps[a]
            for y in range(rows):
                done[y, pl.ds(at, 8), lanes] = total[y]
        return carry

    lax.fori_loop(0, cols // 8, tile, 0)


def depth_kernel(in_ref, taps_ref, out_ref, wide, done):
    high, _, chans, broad = in_ref.shape
    for y in range(high):
        value = in_ref[y, 0].astype(F32)
        for h in range(wide.shape[0]):
            top = min(128, chans - h * 128)
            part = value[h * 128 : h * 128 + top]
            wide[h, y, :, 0:top] = part.T
    depth_sum(125, taps_ref, wide, done)
    for y in range(done.shape[0]):
        out_ref[y] = done[y].T[0:chans]


def tap_rows(kernel):
    chans = kernel.shape[0]
    full = -(-chans // 128) * 128
    return jnp.repeat(jnp.pad(kernel.T, ((0, 0), (0, full - chans))), 8, axis=0)


def depthwise(around, kernel):
    high, probes, chans, broad = around.shape
    rows, cols = high - 6, broad - 256
    halves = -(-chans // 128)
    taps = tap_rows(kernel)
    return pl.pallas_call(
        depth_kernel,
        grid=(probes,),
        in_specs=[
            pl.BlockSpec((high, 1, chans, broad), lambda p: (0, p, 0, 0)),
            whole(taps.shape),
        ],
        out_specs=pl.BlockSpec((rows, chans, cols), lambda p: (0, 0, p)),
        out_shape=jax.ShapeDtypeStruct((rows, chans, probes * cols), F32),
        scratch_shapes=[
            pltpu.VMEM((halves, high, broad, 128), F32),
            pltpu.VMEM((rows, cols, halves * 128), F32),
        ],
        compiler_params=params(),
        cost_estimate=cost(200 * rows * cols * chans * probes, 4 * around.size),
        name="depthwise",
    )(around, taps)


def flux_kernel(
    rows_sent,
    blocks,
    picked_ref,
    slots_ref,
    weights_ref,
    mask_ref,
    update_ref,
    out_ref,
    back_ref,
    pool_ref,
    tall,
    send,
    recv,
    edge,
    home_sems,
):
    bands, fields, cap = picked_ref.shape
    rows, cols = mask_ref.shape
    band, block = lax.axis_index("lat"), lax.axis_index("chan")
    lat_before, lat_after, chan_before, chan_after = neighbours(bands, blocks)
    tall[...] = jnp.zeros_like(tall)
    pool_ref[pl.ds(band, 1)] = picked_ref[pl.ds(band, 1)]
    others = [(lax.rem(band + k, bands), block) for k in range(1, bands)]
    greet((), others + chan_peers(blocks))

    copies = []
    for k, where in enumerate(others):
        copy = pltpu.make_async_remote_copy(
            picked_ref.at[where[0]],
            pool_ref.at[band],
            send.at[k],
            recv.at[k],
            device_id=where,
            device_id_type=MESH,
        )
        copy.start()
        copies.append(copy)
    home = homeward(update_ref, back_ref, rows_sent[0], home_sems)
    for copy in home:
        copy.start()
    for copy in copies:
        copy.wait()

    pool = pool_ref[...].reshape(bands * fields, cap).astype(BF16)
    place = lax.broadcasted_iota(jnp.int32, (cap, cols), 0)
    for y in range(rows):
        at = slice(y * cols, (y + 1) * cols)
        total = jnp.zeros((fields, cols), F32)
        for k in range(slots_ref.shape[0]):
            slots = slots_ref[k : k + 1, at]
            weights = weights_ref[k : k + 1, at]
            source = slots // cap
            hot = jnp.where(place == slots - source * cap, 1.0, 0.0).astype(BF16)
            found = mm(pool, hot)
            for b in range(bands):
                total = total + found[b * fields : (b + 1) * fields] * jnp.where(
                    source == b, weights, 0.0
                )
        tall[3 + y, :, 128 : 128 + cols] = total * mask_ref[y : y + 1, :]

    inner = pl.ds(128, cols)
    swap_edges(
        tall.at[pl.ds(3, 3), :, inner],
        tall.at[pl.ds(rows, 3), :, inner],
        edge.at[0],
        lat_before,
        lat_after,
        tall.at[pl.ds(rows + 3, 3), :, inner],
        tall.at[pl.ds(0, 3), :, inner],
    )
    swap_edges(
        tall.at[:, :, pl.ds(128, 128)],
        tall.at[:, :, pl.ds(cols, 128)],
        edge.at[1],
        chan_before,
        chan_after,
        tall.at[:, :, pl.ds(128 + cols, 128)],
        tall.at[:, :, pl.ds(0, 128)],
    )
    out_ref[...] = tall[...]
    for copy in home:
        copy.wait()


def flux_tile(picked, slots, weights, mask, update, rows_sent):
    bands, fields, _ = picked.shape
    blocks = update.shape[0]
    rows, cols = mask.shape
    shape = (rows + 6, fields, cols + 256)
    return pl.pallas_call(
        functools.partial(flux_kernel, rows_sent, blocks),
        in_specs=[whole(a.shape) for a in (picked, slots, weights, mask)] + [ANYWHERE],
        out_specs=[whole(shape), ANYWHERE],
        out_shape=[
            jax.ShapeDtypeStruct(shape, F32),
            homeward_shape(update, rows_sent[1]),
        ],
        scratch_shapes=[
            pltpu.VMEM(picked.shape, F32),
            pltpu.VMEM(shape, F32),
            pltpu.SemaphoreType.DMA((bands - 1,)),
            pltpu.SemaphoreType.DMA((bands - 1,)),
            pltpu.SemaphoreType.DMA((2, 4)),
            homeward_sems(blocks),
        ],
        compiler_params=params(collective_id=1, has_side_effects=True),
        name="flux_tile",
    )(picked, slots, weights, mask, update)


def normed_step(spread, base, sigma, gain):
    chans = spread.shape[0]
    wide_base = jnp.concatenate([base, base], axis=1)
    center = jnp.sum(spread, axis=0, keepdims=True) * (1.0 / chans)
    along = jnp.sum(wide_base * spread, axis=0, keepdims=True) * (1.0 / chans)
    scale = jnp.concatenate([sigma, sigma], axis=1)
    return (gain * scale * (spread - center - wide_base * along)).astype(BF16)


def row_edges(bands, blocks, line, lines, rows_ref, edges_ref, sems):
    before, after, _, _ = neighbours(bands, blocks)
    pairs = []
    if line < 3:
        pairs.append((before, 3 + line, after))
    if line >= lines - 3:
        pairs.append((after, line - (lines - 3), before))
    return [
        (
            there,
            comes[0],
            pltpu.make_async_remote_copy(
                rows_ref.at[line],
                edges_ref.at[slot],
                sems.at[0, slot],
                sems.at[1, slot],
                device_id=where,
                device_id_type=MESH,
            ),
        )
        for (there, where), slot, comes in pairs
    ]


def fine_kernel(
    bands,
    rows_sent,
    spread_ref,
    probe_ref,
    flux_ref,
    mask_ref,
    sigma_ref,
    base_ref,
    slope_ref,
    gain_ref,
    mix_ref,
    couple_ref,
    expand_ref,
    shrink_ref,
    pool_ref,
    down_ref,
    turn_ref,
    update_ref,
    one_ref,
    coarse_ref,
    turned_ref,
    edges_ref,
    back_ref,
    columns,
    held,
    edge_sems,
    home_sems,
):
    step = pl.program_id(0)
    blocks = back_ref.shape[0]
    lines = held.shape[0]
    home = homeward(update_ref, back_ref, rows_sent[0], home_sems)
    high = flux_ref.shape[0]
    cols = flux_ref.shape[2] - 256

    @pl.when(step == 0)
    def _():
        before, after, _, _ = neighbours(bands, blocks)
        greet((before, after), chan_peers(blocks))
        for copy in home:
            copy.start()
        for y in range(high):
            row = flux_ref[y]
            for b in range(7):
                columns[(y * 7 + b) * 8 : (y * 7 + b + 1) * 8, :] = row[:, 125 + b : 125 + b + cols]

    pooled = []
    for h in range(2):
        y = step * 2 + h
        near = columns[pl.ds(pl.multiple_of(y * 56, 8), 392), :].astype(BF16)
        center = columns[pl.ds(pl.multiple_of((y + 3) * 56 + 24, 8), 8), :].astype(BF16)
        spread = spread_ref[h] + jnp.concatenate(
            [mm(mix_ref[p], near) for p in range(2)], axis=1
        )
        forcing = jnp.concatenate([mm(couple_ref[p], center) for p in range(2)], axis=1)
        probe = jnp.concatenate([probe_ref[h, 0], probe_ref[h, 1]], axis=1).astype(F32)
        start = (probe + forcing).astype(BF16).astype(F32)
        at = pl.ds(y, 1)
        tangent = normed_step(spread, base_ref[h].astype(F32), sigma_ref[at, :], gain_ref[...])
        slope = slope_ref[h].astype(F32)
        hidden = mm(expand_ref[...], tangent)
        gated = (hidden * jnp.concatenate([slope, slope], axis=1)).astype(BF16)
        mask = mask_ref[at, :]
        one = (
            (start + mm(shrink_ref[...], gated)) * jnp.concatenate([mask, mask], axis=1)
        ).astype(BF16)
        one_ref[h] = one
        pooled.append(mm(one, pool_ref[...]))

    both = (pooled[0] + pooled[1]).astype(BF16)
    coarse_ref[0] = mm(down_ref[...], both).astype(BF16)
    turned = mm(both.T, turn_ref[...]).astype(BF16)
    half = turned.shape[0] // 2
    turned_ref[0, 0] = turned[0:half]
    turned_ref[0, 1] = turned[half : 2 * half]
    for line in range(lines):

        @pl.when(step == line)
        def _(line=line):
            held[line] = turned_ref[0]
            for there, _, copy in row_edges(
                bands, blocks, line, lines, held, edges_ref, edge_sems
            ):

                @pl.when(there)
                def _(copy=copy):
                    copy.start()

    @pl.when(step == lines - 1)
    def _():
        for line in range(lines):
            for there, comes, copy in row_edges(
                bands, blocks, line, lines, held, edges_ref, edge_sems
            ):

                @pl.when(there)
                def _(copy=copy):
                    copy.wait_send()

                @pl.when(comes)
                def _(copy=copy):
                    copy.wait_recv()

        for copy in home:
            copy.wait()


def fine_level(
    spread,
    probe,
    flux,
    mask,
    sigma,
    base,
    slope,
    gain,
    mix,
    couple,
    expand,
    shrink,
    pool,
    down,
    turn,
    update,
    bands,
    rows_sent,
):
    rows, chans, wide = spread.shape
    cols = wide // 2
    coarse = down.shape[0]
    lines = rows // 2
    turned = (2, cols // 2, turn.shape[1])
    row = lambda i: (i, 0, 0)
    return pl.pallas_call(
        functools.partial(fine_kernel, bands, rows_sent),
        grid=(lines,),
        in_specs=[
            pl.BlockSpec((2, chans, wide), row),
            pl.BlockSpec((2,) + probe.shape[1:], lambda i: (i, 0, 0, 0)),
            whole(flux.shape),
            whole(mask.shape),
            whole(sigma.shape),
            pl.BlockSpec((2, chans, cols), row),
            pl.BlockSpec((2, slope.shape[1], cols), row),
            whole(gain.shape),
            whole(mix.shape),
            whole(couple.shape),
            whole(expand.shape),
            whole(shrink.shape),
            whole(pool.shape),
            whole(down.shape),
            whole(turn.shape),
            ANYWHERE,
        ],
        out_specs=[
            pl.BlockSpec((2, chans, wide), row),
            pl.BlockSpec((1, coarse, cols), row),
            pl.BlockSpec((1,) + turned, lambda i: (i, 0, 0, 0)),
            ANYWHERE,
            ANYWHERE,
        ],
        out_shape=[
            jax.ShapeDtypeStruct((rows, chans, wide), BF16),
            jax.ShapeDtypeStruct((lines, coarse, cols), BF16),
            jax.ShapeDtypeStruct((lines,) + turned, BF16),
            jax.ShapeDtypeStruct((6,) + turned, BF16),
            homeward_shape(update, rows_sent[1]),
        ],
        scratch_shapes=[
            pltpu.VMEM((flux.shape[0] * 56, cols), F32),
            pltpu.VMEM((lines,) + turned, BF16),
            pltpu.SemaphoreType.DMA((2, 6)),
            homeward_sems(update.shape[0]),
        ],
        compiler_params=params(collective_id=4, has_side_effects=True),
        name="fine_level",
    )(
        spread,
        probe,
        flux,
        mask,
        sigma,
        base,
        slope,
        gain,
        mix,
        couple,
        expand,
        shrink,
        pool,
        down,
        turn,
        update,
    )


def coarse_kernel(
    bands,
    rows_sent,
    turned_ref,
    edges_ref,
    taps_ref,
    field_ref,
    sigma_ref,
    base_ref,
    slope_ref,
    gain_ref,
    expand_ref,
    shrink_ref,
    spreadout_ref,
    up_ref,
    one_ref,
    mask_ref,
    update_ref,
    out_ref,
    back_ref,
    around,
    wide,
    tall,
    done,
    spread,
    edge,
    home_sems,
):
    blocks = back_ref.shape[0]
    home = homeward(update_ref, back_ref, rows_sent[0], home_sems)
    lines, chans, _ = field_ref.shape
    probes, fine, rows, cols = out_ref.shape
    half = cols // 2
    before, after, chan_before, chan_after = neighbours(bands, blocks)
    inner = slice(16, 16 + half)
    around[...] = jnp.zeros_like(around)
    around[3 : 3 + lines, :, inner, :] = turned_ref[...]

    @pl.when(before[0])
    def _():
        around[0:3, :, inner, :] = edges_ref[0:3]

    @pl.when(after[0])
    def _():
        around[3 + lines : 6 + lines, :, inner, :] = edges_ref[3:6]

    greet((), chan_peers(blocks))
    finish = start_edges(
        around.at[:, :, pl.ds(16, 16), :],
        around.at[:, :, pl.ds(half, 16), :],
        edge,
        chan_before,
        chan_after,
        around.at[:, :, pl.ds(16 + half, 16), :],
        around.at[:, :, pl.ds(0, 16), :],
    )
    for copy in home:
        copy.start()
    finish()
    for p in range(probes):
        for y in range(tall.shape[1]):
            for h in range(tall.shape[0]):
                lanes = slice(h * 128, (h + 1) * 128)
                tall[h, y] = around[y, p, :, lanes].astype(F32)
        depth_sum(13, taps_ref, tall, done)
        for y in range(lines):
            spread[y, :, p * half : (p + 1) * half] = done[y].T[0:chans]

    gated = []
    for y in range(lines):
        tangent = normed_step(
            spread[y], base_ref[y].astype(F32), sigma_ref[y : y + 1, :], gain_ref[...]
        )
        slope = slope_ref[y].astype(F32)
        hidden = mm(expand_ref[...], tangent)
        gated.append((hidden * jnp.concatenate([slope, slope], axis=1)).astype(BF16))
    for y in range(lines):
        two = (field_ref[y].astype(F32) + mm(shrink_ref[...], gated[y])).astype(BF16)
        raised = mm(up_ref[...], mm(two, spreadout_ref[...]).astype(BF16))
        for h in range(2):
            line = y * 2 + h
            mask = mask_ref[line : line + 1, :]
            for p in range(probes):
                for t in range(cols // 128):
                    lanes = slice(p * cols + t * 128, p * cols + (t + 1) * 128)
                    wide[p, t, pl.ds(line, fine, stride=rows), :] = (
                        one_ref[line, :, lanes].astype(F32) + raised[:, lanes]
                    ) * mask[:, t * 128 : (t + 1) * 128]
    for p in range(probes):
        for t in range(cols // 128):
            out_ref[p, :, :, t * 128 : (t + 1) * 128] = (
                wide[p, t].reshape(fine, rows, 128).astype(BF16)
            )
    for copy in home:
        copy.wait()


def coarse_level(
    turned,
    edges,
    taps,
    field,
    sigma,
    base,
    slope,
    gain,
    expand,
    shrink,
    spreadout,
    up,
    one,
    mask,
    update,
    bands,
    rows_sent,
):
    lines, chans, double = field.shape
    half = double // 2
    rows, fine, _ = one.shape
    cols = double
    high = lines + 6
    operands = (
        (turned, edges, taps, field, sigma, base, slope, gain)
        + (expand, shrink, spreadout, up, one, mask)
    )
    return pl.pallas_call(
        functools.partial(coarse_kernel, bands, rows_sent),
        in_specs=[whole(a.shape) for a in operands] + [ANYWHERE],
        out_specs=[whole((2, fine, rows, cols)), ANYWHERE],
        out_shape=[
            jax.ShapeDtypeStruct((2, fine, rows, cols), BF16),
            homeward_shape(update, rows_sent[1]),
        ],
        scratch_shapes=[
            pltpu.VMEM((high, 2, half + 32, taps.shape[1]), BF16),
            pltpu.VMEM((2, cols // 128, fine * rows, 128), F32),
            pltpu.VMEM((taps.shape[1] // 128, high, half + 32, 128), F32),
            pltpu.VMEM((lines, half, taps.shape[1]), F32),
            pltpu.VMEM((lines, chans, double), F32),
            pltpu.SemaphoreType.DMA((4,)),
            homeward_sems(update.shape[0]),
        ],
        compiler_params=params(collective_id=5, has_side_effects=True),
        cost_estimate=cost(1e9, 4e6),
        name="coarse_level",
    )(*operands, update)


def local(
    probe_field,
    gate_slope,
    spectral_filter,
    weight_in,
    weight_out,
    weight_flux,
    send_cells,
    recv_slots,
    recv_weights,
    ocean_probe,
    ocean_mask,
    coupling,
    base_fine,
    sigma_fine,
    slope_fine,
    gain_fine,
    kernel_fine,
    expand_fine,
    shrink_fine,
    down_proj,
    base_coarse,
    sigma_coarse,
    slope_coarse,
    gain_coarse,
    kernel_coarse,
    expand_coarse,
    shrink_coarse,
    up_proj,
):
    probes, rows, width, lons = probe_field.shape
    bands = lax.axis_size("lat")
    blocks = lax.axis_size("chan")
    part = width // bands
    pair = probes * rows
    lats = rows * bands
    chans = width * blocks
    fields = weight_flux.shape[1]

    flat_probe = probe_field.reshape(pair, width, lons)

    flux_rows = lax.dynamic_slice_in_dim(
        weight_flux, lax.axis_index("chan") * width, width, 0
    ).T
    none = jnp.zeros_like(flux_rows)
    flux_pair = jnp.concatenate(
        [
            jnp.concatenate([flux_rows, none], axis=1),
            jnp.concatenate([none, flux_rows], axis=1),
        ],
        axis=0,
    )
    terms = probe_flux(probe_field, flux_pair)

    tile_rows, tile_cols = ocean_mask.shape
    fine = ocean_probe.shape[1]
    mask = ocean_mask.astype(F32)
    start = ocean_rows(ocean_probe, mask)
    base_rows = base_fine.transpose(1, 0, 2)
    slope_rows = slope_fine.transpose(1, 0, 2)
    base_lines = base_coarse.transpose(1, 0, 2)
    slope_lines = slope_coarse.transpose(1, 0, 2)
    couple_t = coupling.T
    no_couple = jnp.zeros_like(couple_t)
    couple = jnp.stack(
        [
            jnp.concatenate([couple_t, no_couple], axis=1),
            jnp.concatenate([no_couple, couple_t], axis=1),
        ]
    )
    mix = (kernel_fine[None, :, :, None] * couple.astype(F32)[:, :, None, :]).astype(BF16)
    mix = mix.reshape(probes, fine, 49 * probes * fields)
    lane = jnp.arange(probes * tile_cols, dtype=jnp.int32)
    meets = lane[:, None] // 2 == jnp.arange(probes * tile_cols // 2, dtype=jnp.int32)[None, :]
    pool = jnp.where(meets, 0.25, 0.0).astype(BF16)
    spreadout = jnp.where(meets.T, 1.0, 0.0).astype(BF16)

    gathered, around = open_exchange(flat_probe, start, bands, blocks)

    fwd_lat, inv_lat = cosine_tables(lats)
    diff = jnp.asarray(fourier_product(lons))
    filt = lax.dynamic_slice_in_dim(
        spectral_filter, lax.axis_index("lat") * part, part, 1
    ).T.reshape(part, lats, 1)
    gathered, filt = lax.optimization_barrier((gathered, filt))
    mixed = lat_filter(gathered, jnp.asarray(fwd_lat.T), jnp.asarray(inv_lat.T), filt, diff)
    regrouped = lax.all_to_all(
        mixed.reshape(bands * blocks, part, pair, 128),
        ("lat", "chan"),
        split_axis=0,
        concat_axis=0,
        tiled=True,
    ).reshape(chans, pair, 128)

    win = (
        weight_in.reshape(blocks, bands, part, -1).transpose(1, 0, 2, 3).reshape(chans, -1).T
    )
    folded = mm(weight_out, weight_flux).astype(BF16)
    wout = jnp.concatenate([weight_out, folded, folded], axis=1).T
    probe_terms = lax.psum_scatter(terms, "chan", scatter_dimension=0, tiled=True)
    spread = depthwise(around, kernel_fine)
    early = (
        spread,
        start,
        mask,
        win,
        wout,
        probe_terms,
        base_rows,
        slope_rows,
        base_lines,
        slope_lines,
        gain_fine[:, None],
        mix,
        couple,
        expand_fine.T,
        shrink_fine.T,
        pool,
        down_proj.T,
        jnp.pad(down_proj, ((0, 0), (0, 256 - down_proj.shape[1]))),
        tap_rows(kernel_coarse),
        gain_coarse[:, None],
        expand_coarse.T,
        shrink_coarse.T,
        spreadout,
        up_proj.T,
        send_cells[0],
        recv_slots[0],
        recv_weights[0],
    )
    regrouped, early = lax.optimization_barrier((regrouped, early))
    (
        spread,
        start,
        mask,
        win,
        wout,
        probe_terms,
        base_rows,
        slope_rows,
        base_lines,
        slope_lines,
        gain_one,
        mix,
        couple,
        expand_one,
        shrink_one,
        pool,
        down,
        turn,
        taps,
        gain_two,
        expand_two,
        shrink_two,
        spreadout,
        raise_two,
        cells,
        slots,
        weights,
    ) = early
    update, picked, *shipped = pointwise(
        regrouped, gate_slope, win, wout, probe_terms, cells, blocks, SENT_GROUPS
    )

    tall, back0 = flux_tile(picked, slots, weights, mask, update, SENT[0])
    one, coarse, turned, edges, back1 = fine_level(
        spread,
        start,
        tall,
        mask,
        sigma_fine,
        base_rows,
        slope_rows,
        gain_one,
        mix,
        couple,
        expand_one,
        shrink_one,
        pool,
        down,
        turn,
        update,
        bands,
        SENT[1],
    )
    ocean_out, back2 = coarse_level(
        turned,
        edges,
        taps,
        coarse,
        sigma_coarse,
        base_lines,
        slope_lines,
        gain_two,
        expand_two,
        shrink_two,
        spreadout,
        raise_two,
        one,
        mask,
        update,
        bands,
        SENT[2],
    )
    parts = (*shipped, back0, back1, back2)
    atmos_out = add_update(flat_probe, parts).reshape(probe_field.shape)
    return (atmos_out, ocean_out)


def solution(mesh):
    tile = P(("lat", "chan"), None, None)
    rows_cols = P(None, "lat", "chan")
    return jax.shard_map(
        local,
        mesh=mesh,
        in_specs=(
            P(None, "lat", "chan", None),
            P("lat", None, "chan"),
            P(None, "chan"),
            P(),
            P(),
            P(),
            tile,
            tile,
            tile,
            P(None, None, "lat", "chan"),
            P("lat", "chan"),
            P(),
            rows_cols,
            P("lat", "chan"),
            rows_cols,
            P(),
            P(),
            P(),
            P(),
            P(),
            rows_cols,
            P("lat", "chan"),
            rows_cols,
            P(),
            P(),
            P(),
            P(),
            P(),
        ),
        out_specs=(P(None, "lat", "chan", None), P(None, None, "lat", "chan")),
        check_vma=False,
    )
```

```python
import functools
import math

import jax
import jax.numpy as jnp
import ml_dtypes
import numpy as np
from jax import lax
from jax.experimental import pallas as pl
from jax.experimental.pallas import tpu as pltpu
from jax.sharding import PartitionSpec as P

F32 = jnp.float32
BF16 = jnp.bfloat16
MESH = pl.DeviceIdType.MESH
VMEM_LIMIT = 56 * 1024 * 1024


def params(**more):
    return pltpu.CompilerParams(vmem_limit_bytes=VMEM_LIMIT, **more)


def cost(flops, nbytes):
    return pl.CostEstimate(flops=int(flops), bytes_accessed=int(nbytes), transcendentals=0)


def mm(a, b):
    return jnp.dot(a, b, preferred_element_type=F32)


def whole(shape):
    zeros = (0,) * len(shape)
    return pl.BlockSpec(shape, lambda *_: zeros)


def fourier_product(count):
    column = np.arange(count)
    half = count // 2
    wave = np.where(column <= half, column, column - half)
    angles = (column[:, None] * wave[None, :] % count) * (2.0 * math.pi / count)
    basis = np.where((column <= half)[None, :], np.cos(angles), np.sin(angles))
    forward = (basis / count).astype(ml_dtypes.bfloat16)
    factor = np.where((column == 0) | (column == half), 1.0, 2.0)
    inverse = (basis.T * factor[:, None]).astype(ml_dtypes.bfloat16)
    product = forward.astype(np.float64) @ inverse.astype(np.float64)
    return (product - np.eye(count)).astype(ml_dtypes.bfloat16)


def cosine_tables(count):
    degree = np.arange(count)
    phase = degree[None, :] * (2 * degree[:, None] + 1) % (4 * count)
    basis = np.cos(phase * (math.pi / (2 * count)))
    forward = (basis / count).astype(ml_dtypes.bfloat16)
    factor = np.where(degree == 0, 1.0, 2.0)
    inverse = (basis.T * factor[:, None]).astype(ml_dtypes.bfloat16)
    return (forward, inverse)


def greet(partners, more=()):
    barrier = pltpu.get_barrier_semaphore()
    for where in more:
        pl.semaphore_signal(barrier, inc=1, device_id=where, device_id_type=MESH)
    count = jnp.int32(len(more))
    for there, where in partners:

        @pl.when(there)
        def _(where=where):
            pl.semaphore_signal(barrier, inc=1, device_id=where, device_id_type=MESH)

        count = count + there.astype(jnp.int32)
    pl.semaphore_wait(barrier, count)


def start_edges(low, high, sems, before, after, low_to, high_to):
    is_before, device_before = before
    is_after, device_after = after

    def to_before():
        return pltpu.make_async_remote_copy(
            low, low_to, sems.at[0], sems.at[1], device_id=device_before, device_id_type=MESH
        )

    def to_after():
        return pltpu.make_async_remote_copy(
            high, high_to, sems.at[2], sems.at[3], device_id=device_after, device_id_type=MESH
        )

    @pl.when(is_before)
    def _():
        to_before().start()

    @pl.when(is_after)
    def _():
        to_after().start()

    def finish():
        @pl.when(is_before)
        def _():
            to_before().wait_send()
            to_after().wait_recv()

        @pl.when(is_after)
        def _():
            to_after().wait_send()
            to_before().wait_recv()

    return finish


def swap_edges(*args):
    start_edges(*args)()


def neighbours(bands, blocks):
    band, block = lax.axis_index("lat"), lax.axis_index("chan")
    return (
        (band > 0, (jnp.maximum(band - 1, 0), block)),
        (band < bands - 1, (jnp.minimum(band + 1, bands - 1), block)),
        (block > 0, (band, jnp.maximum(block - 1, 0))),
        (block < blocks - 1, (band, jnp.minimum(block + 1, blocks - 1))),
    )


def chan_peers(blocks):
    band, block = lax.axis_index("lat"), lax.axis_index("chan")
    return [(band, lax.rem(block + k, blocks)) for k in range(1, blocks)]


def homeward(update_ref, back_ref, first, sems):
    send, recv, own = sems
    blocks, _, count = back_ref.shape[:3]
    block = lax.axis_index("chan")
    some = pl.ds(first, count)
    copies = [
        pltpu.make_async_remote_copy(
            update_ref.at[where[1], :, some],
            back_ref.at[block],
            send.at[k],
            recv.at[k],
            device_id=where,
            device_id_type=MESH,
        )
        for k, where in enumerate(chan_peers(blocks))
    ]
    return copies + [
        pltpu.make_async_copy(update_ref.at[block, :, some], back_ref.at[block], own.at[0])
    ]


def homeward_sems(blocks):
    return [
        pltpu.SemaphoreType.DMA((blocks - 1,)),
        pltpu.SemaphoreType.DMA((blocks - 1,)),
        pltpu.SemaphoreType.DMA((1,)),
    ]


def homeward_shape(update, count):
    blocks, probes, _, width, lanes = update.shape
    return jax.ShapeDtypeStruct((blocks, probes, count, width, lanes), BF16)


SENT_GROUPS = 1
SENT = ((4, 4), (8, 8), (16, 8))
ANYWHERE = pl.BlockSpec(memory_space=pl.ANY)


def ocean_rows_kernel(in_ref, mask_ref, out_ref, wide):
    _, chans, rows, cols = in_ref.shape
    value = in_ref[0].astype(F32) * mask_ref[...].astype(F32)[None]
    for t in range(cols // 128):
        wide[t] = value[:, :, t * 128 : (t + 1) * 128].reshape(chans * rows, 128)
    for y in range(rows):
        for t in range(cols // 128):
            out_ref[y, 0, :, t * 128 : (t + 1) * 128] = wide[
                t, pl.ds(y, chans, stride=rows), :
            ].astype(BF16)


def ocean_rows(field, mask):
    probes, chans, rows, cols = field.shape
    return pl.pallas_call(
        ocean_rows_kernel,
        grid=(probes,),
        in_specs=[
            pl.BlockSpec((1, chans, rows, cols), lambda p: (p, 0, 0, 0)),
            whole(mask.shape),
        ],
        out_specs=pl.BlockSpec((rows, 1, chans, cols), lambda p: (0, p, 0, 0)),
        out_shape=jax.ShapeDtypeStruct((rows, probes, chans, cols), BF16),
        scratch_shapes=[pltpu.VMEM((cols // 128, chans * rows, 128), F32)],
        compiler_params=params(),
        cost_estimate=cost(field.size, 4 * field.size),
        name="ocean_rows",
    )(field, mask)


STEPS = (
    ((0, 1), (1, 0), (0, 3), (3, 0), (1, 1), (3, 3), (1, 3), (3, 1))
    + ((0, 2), (2, 0), (2, 2), (1, 2), (2, 1), (3, 2), (2, 3))
)


def lat_partner(band, step, side):
    dz, dx = step
    return lax.rem(band // side + dz, side) * side + lax.rem(lax.rem(band, side) + dx, side)


def open_kernel(
    blocks, probe_ref, ocean_ref, out_ref, around_ref, taken, wide, turned, tall, sems, own, edge
):
    send, recv, load = sems
    rows, chans, lons = probe_ref.shape
    bands, part = out_ref.shape[0], out_ref.shape[1]
    side = math.isqrt(bands)
    lines, _, _, cols = ocean_ref.shape
    pieces, lanes = taken.shape[0], taken.shape[3]
    band, block = lax.axis_index("lat"), lax.axis_index("chan")
    lat_before, lat_after, chan_before, chan_after = neighbours(bands, blocks)

    def take(i):
        return pltpu.make_async_copy(
            probe_ref.at[:, :, pl.ds(i * lanes, lanes)], taken.at[i], load.at[i]
        )

    for i in range(pieces):
        take(i).start()
    tall[...] = jnp.zeros_like(tall)
    others = [(lat_partner(band, step, side), block) for step in STEPS]
    greet((chan_before, chan_after), others)
    inner = pl.ds(128, cols)
    center = pltpu.make_async_copy(ocean_ref, tall.at[pl.ds(3, lines), :, :, inner], own.at[0])
    center.start()
    finish_rows = start_edges(
        ocean_ref.at[pl.ds(0, 3)],
        ocean_ref.at[pl.ds(lines - 3, 3)],
        edge.at[0],
        lat_before,
        lat_after,
        tall.at[pl.ds(lines + 3, 3), :, :, inner],
        tall.at[pl.ds(0, 3), :, :, inner],
    )
    copies = []
    for i in range(pieces):
        take(i).wait()
        for t in range(lanes // 128):
            at = slice(t * 128, (t + 1) * 128)
            wide[t] = taken[i, :, :, at].astype(F32).reshape(rows * chans, 128)
            for c in range(chans):
                turned[i, c, :, at] = wide[t, pl.ds(c, rows, stride=chans), :].astype(BF16)
        columns = pl.ds(i * lanes, lanes)
        for k, where in enumerate(others):
            copy = pltpu.make_async_remote_copy(
                turned.at[i, pl.ds(where[0] * part, part)],
                out_ref.at[band, :, :, columns],
                send.at[i, k],
                recv.at[i, k],
                device_id=where,
                device_id_type=MESH,
            )
            copy.start()
            copies.append(copy)
        copy = pltpu.make_async_copy(
            turned.at[i, pl.ds(band * part, part)],
            out_ref.at[band, :, :, columns],
            own.at[i + 1],
        )
        copy.start()
        copies.append(copy)
    center.wait()
    finish_rows()
    finish_columns = start_edges(
        tall.at[:, :, :, pl.ds(128, 128)],
        tall.at[:, :, :, pl.ds(cols, 128)],
        edge.at[1],
        chan_before,
        chan_after,
        tall.at[:, :, :, pl.ds(128 + cols, 128)],
        tall.at[:, :, :, pl.ds(0, 128)],
    )
    finish_columns()
    store = pltpu.make_async_copy(tall, around_ref, own.at[0])
    store.start()
    for copy in copies:
        copy.wait()
    store.wait()


def open_exchange(probe, ocean, bands, blocks):
    rows, chans, lons = probe.shape
    lines, probes, fine, cols = ocean.shape
    pieces, lanes = 4, lons // 4
    any_spec = pl.BlockSpec(memory_space=pl.ANY)
    tall = (lines + 6, probes, fine, cols + 256)
    return pl.pallas_call(
        functools.partial(open_kernel, blocks),
        in_specs=[any_spec, any_spec],
        out_specs=[any_spec, any_spec],
        out_shape=[
            jax.ShapeDtypeStruct((bands, chans // bands, rows, lons), BF16),
            jax.ShapeDtypeStruct(tall, BF16),
        ],
        scratch_shapes=[
            pltpu.VMEM((pieces, rows, chans, lanes), BF16),
            pltpu.VMEM((lanes // 128, rows * chans, 128), F32),
            pltpu.VMEM((pieces, chans, rows, lanes), BF16),
            pltpu.VMEM(tall, BF16),
            [
                pltpu.SemaphoreType.DMA((pieces, bands - 1)),
                pltpu.SemaphoreType.DMA((pieces, bands - 1)),
                pltpu.SemaphoreType.DMA((pieces,)),
            ],
            pltpu.SemaphoreType.DMA((pieces + 1,)),
            pltpu.SemaphoreType.DMA((2, 4)),
        ],
        compiler_params=params(collective_id=3, has_side_effects=True),
        cost_estimate=cost(0, 4 * probe.size),
        name="open_exchange",
    )(probe, ocean)


def probe_flux_kernel(probe_ref, weight_ref, out_ref):
    weight = weight_ref[...]
    rows = probe_ref.shape[1]
    for n in range(0, rows, 2):
        pair = [
            mm(weight, jnp.concatenate([probe_ref[0, m], probe_ref[1, m]], axis=0))
            for m in (n, n + 1)
        ]
        both = jnp.concatenate(pair, axis=0).astype(BF16)
        for j in range(out_ref.shape[0]):
            out_ref[j, n * 8 : n * 8 + 16, :] = both[:, j * 128 : (j + 1) * 128]


def probe_flux(probe, weight):
    probes, rows, chans, lons = probe.shape
    blocks = lons // 128
    step = 4
    return pl.pallas_call(
        probe_flux_kernel,
        grid=(rows // step,),
        in_specs=[
            pl.BlockSpec((probes, step, chans, lons), lambda i: (0, i, 0, 0)),
            whole(weight.shape),
        ],
        out_specs=pl.BlockSpec((blocks, step * 8, 128), lambda i: (0, i, 0)),
        out_shape=jax.ShapeDtypeStruct((blocks, rows * 8, 128), BF16),
        compiler_params=params(),
        cost_estimate=cost(2 * 8 * probe.size, 2 * probe.size),
        name="probe_flux",
    )(probe, weight)


def filter_kernel(in_ref, fwd_ref, inv_ref, filt_ref, diff_ref, out_ref, wide, back):
    bands, _, pair, lons = in_ref.shape
    rows = pair // 2
    which = lax.broadcasted_iota(jnp.int32, filt_ref.shape, 1)
    filt = jnp.sum(
        jnp.where(which == pl.program_id(0), filt_ref[...], 0.0), axis=1, keepdims=True
    )
    for b in range(bands):
        piece = in_ref[b, 0].astype(F32)
        wide[b * rows : (b + 1) * rows, 0:lons] = piece[0:rows]
        wide[b * rows : (b + 1) * rows, lons : 2 * lons] = piece[rows:pair]
    for t in range(2):
        at = slice(t * lons, (t + 1) * lons)
        value = wide[:, at]
        filtered = (mm(fwd_ref[...], value.astype(BF16)) * filt).astype(BF16)
        returned = mm(inv_ref[...], filtered)
        back[:, at] = returned.astype(BF16)
        wide[:, at] = value + returned
    for t in range(lons // 256):
        cols = slice(t * 256, (t + 1) * 256)
        mixed = [
            wide[:, p * lons + t * 256 : p * lons + (t + 1) * 256]
            + mm(back[:, p * lons : (p + 1) * lons], diff_ref[:, cols])
            for p in range(2)
        ]
        for b in range(bands):
            at = slice(b * rows, (b + 1) * rows)
            both = jnp.concatenate([mixed[0][at], mixed[1][at]], axis=0).astype(BF16)
            for j in range(2):
                out_ref[b, 2 * t + j, 0] = both[:, j * 128 : (j + 1) * 128]


def lat_filter(received, fwd, inv, filt, diff):
    bands, chans, pair, lons = received.shape
    lats = fwd.shape[0]
    blocks = lons // 128
    return pl.pallas_call(
        filter_kernel,
        grid=(chans,),
        in_specs=[
            pl.BlockSpec((bands, 1, pair, lons), lambda i: (0, i, 0, 0)),
            whole(fwd.shape),
            whole(inv.shape),
            whole(filt.shape),
            whole(diff.shape),
        ],
        out_specs=pl.BlockSpec((bands, blocks, 1, pair, 128), lambda i: (0, 0, i, 0, 0)),
        out_shape=jax.ShapeDtypeStruct((bands, blocks, chans, pair, 128), BF16),
        scratch_shapes=[pltpu.VMEM((lats, 2 * lons), F32), pltpu.VMEM((lats, 2 * lons), BF16)],
        compiler_params=params(),
        cost_estimate=cost(8.4e9, 4 * received.size),
        name="lat_filter",
    )(received, fwd, inv, filt, diff)


GROUP = 4


def point_kernel(
    sent,
    mixed_ref,
    slope_ref,
    win_ref,
    wout_ref,
    pflux_ref,
    cells_ref,
    out_ref,
    picked_ref,
    *rest,
):
    back_refs = rest[:sent]
    wide, flux, ship, home_sems = rest[sent:]
    chans, pair, lanes = mixed_ref.shape
    rows = pair // 2
    step = pl.program_id(0)
    send, recv, own = home_sems
    blocks = out_ref.shape[0]
    block = lax.axis_index("chan")
    peers = chan_peers(blocks)

    def homeward_group(i):
        copies = [
            pltpu.make_async_remote_copy(
                ship.at[i, where[1]],
                back_refs[i].at[block],
                send.at[i, k],
                recv.at[i, k],
                device_id=where,
                device_id_type=MESH,
            )
            for k, where in enumerate(peers)
        ]
        return copies + [
            pltpu.make_async_copy(ship.at[i, block], back_refs[i].at[block], own.at[i])
        ]

    @pl.when(step == 0)
    def _():
        greet((), peers)

        def load(i, carry):
            at = pl.ds(pl.multiple_of(i * 8, 8), 8)
            wide[pl.ds(pl.multiple_of(i * 8 * pair, 8), 8 * pair), :] = (
                mixed_ref[at].astype(F32).reshape(8 * pair, lanes)
            )
            return carry

        lax.fori_loop(0, chans // 8, load, 0)

    which = lax.broadcasted_iota(jnp.int32, (8, lanes), 0)
    width = out_ref.shape[3]
    gated = []
    for g in range(GROUP):
        value = jnp.concatenate(
            [
                wide[pl.ds(step * GROUP + g + p * rows, chans, stride=pair), :]
                for p in range(2)
            ],
            axis=1,
        ).astype(BF16)
        slope = slope_ref[g].astype(F32)
        hidden = mm(win_ref[...], value)
        gated.append((jnp.concatenate([slope, slope], axis=1) * hidden).astype(BF16))
    for g in range(GROUP):
        update = mm(wout_ref[...], gated[g])
        for j in range(blocks):
            piece = update[j * width : (j + 1) * width].astype(BF16)
            out_ref[j, 0, g] = piece[:, 0:lanes]
            out_ref[j, 1, g] = piece[:, lanes : 2 * lanes]
        terms = update[chans : chans + 8]
        flux[pl.ds(pl.multiple_of((step * GROUP + g) * 8, 8), 8), :] = jnp.where(
            which < 4, terms[:, 0:lanes], terms[:, lanes : 2 * lanes]
        )

    for i in range(sent):

        @pl.when(step == i)
        def _(i=i):
            ship[i] = out_ref[...]
            for copy in homeward_group(i):
                copy.start()

    @pl.when(step == rows // GROUP - 1)
    def _():
        total = flux[...]
        for j in range(pflux_ref.shape[0]):
            total = total + pflux_ref[j].astype(F32)
        total = total.astype(BF16)
        place = lax.broadcasted_iota(jnp.int32, (lanes, lanes), 0)
        for r in range(cells_ref.shape[0]):
            cells = cells_ref[r : r + 1, :]
            row = cells // lanes
            hot = jnp.where(place == cells - row * lanes, 1.0, 0.0).astype(BF16)
            found = mm(total, hot)
            picked = jnp.zeros((8, lanes), F32)
            for n in range(rows):
                picked = picked + jnp.where(row == n, found[n * 8 : (n + 1) * 8], 0.0)
            picked_ref[r] = picked
        for i in range(sent):
            for copy in homeward_group(i):
                copy.wait()


def pointwise(mixed, slope, win, wout, pflux, cells, blocks, sent):
    chans, pair, lanes = mixed.shape
    rows, hid, _ = slope.shape
    width = chans // blocks
    shipped = (sent, blocks, 2, GROUP, width, lanes)
    return pl.pallas_call(
        functools.partial(point_kernel, sent),
        grid=(rows // GROUP,),
        in_specs=[
            whole(mixed.shape),
            pl.BlockSpec((GROUP, hid, lanes), lambda i: (i, 0, 0)),
            whole(win.shape),
            whole(wout.shape),
            whole(pflux.shape),
            whole(cells.shape),
        ],
        out_specs=[
            pl.BlockSpec((blocks, 2, GROUP, width, lanes), lambda i: (0, 0, i, 0, 0)),
            whole((cells.shape[0], 8, lanes)),
        ]
        + [ANYWHERE] * sent,
        out_shape=[
            jax.ShapeDtypeStruct((blocks, 2, rows, width, lanes), BF16),
            jax.ShapeDtypeStruct((cells.shape[0], 8, lanes), F32),
        ]
        + [jax.ShapeDtypeStruct(shipped[1:], BF16)] * sent,
        scratch_shapes=[
            pltpu.VMEM((chans * pair, lanes), F32),
            pltpu.VMEM((rows * 8, lanes), F32),
            pltpu.VMEM(shipped, BF16),
            [
                pltpu.SemaphoreType.DMA((sent, blocks - 1)),
                pltpu.SemaphoreType.DMA((sent, blocks - 1)),
                pltpu.SemaphoreType.DMA((sent,)),
            ],
        ],
        compiler_params=params(collective_id=6, has_side_effects=True),
        cost_estimate=cost(7.3e9, 4 * mixed.size + 2 * slope.size),
        name="pointwise",
    )(mixed, slope, win, wout, pflux, cells)


def add_kernel(starts, probe_ref, *refs):
    out_ref = refs[-1]
    step = pl.program_id(0)
    for k, update_ref in enumerate(refs[:-1]):

        @pl.when((step >= starts[k]) & (step < starts[k + 1]))
        def _(update_ref=update_ref):
            for j in range(update_ref.shape[0]):
                cols = slice(j * 128, (j + 1) * 128)
                out_ref[:, :, :, cols] = probe_ref[:, :, :, cols] + update_ref[j]


def add_update(probe, parts):
    probes, rows, chans, lons = probe.shape
    blocks = parts[0].shape[0]
    step = 4
    counts = [a.shape[2] // step for a in parts]
    starts = [sum(counts[:k]) for k in range(len(counts) + 1)]

    def spec(k):
        return pl.BlockSpec(
            (blocks, probes, step, chans, 128),
            lambda i: (0, 0, jnp.clip(i - starts[k], 0, counts[k] - 1), 0, 0),
        )

    field = pl.BlockSpec((probes, step, chans, lons), lambda i: (0, i, 0, 0))
    return pl.pallas_call(
        functools.partial(add_kernel, starts),
        grid=(rows // step,),
        in_specs=[field] + [spec(k) for k in range(len(parts))],
        out_specs=field,
        out_shape=jax.ShapeDtypeStruct(probe.shape, BF16),
        compiler_params=params(),
        cost_estimate=cost(probe.size, 6 * probe.size),
        name="add_update",
    )(probe, *parts)


def depth_sum(first, taps_ref, wide, done):
    halves, high = wide.shape[0], wide.shape[1]
    rows, cols = done.shape[0], done.shape[1]

    def tile(i, carry):
        at = pl.multiple_of(i * 8, 8)
        for h in range(halves):
            lanes = slice(h * 128, (h + 1) * 128)
            total = [jnp.zeros((8, 128), F32) for _ in range(rows)]
            for b in range(7):
                taps = [taps_ref[(7 * a + b) * 8 : (7 * a + b + 1) * 8, lanes] for a in range(7)]
                for y in range(high):
                    moved = wide[h, y, pl.ds(at + (first + b), 8), :]
                    for a in range(7):
                        if 0 <= y - a < rows:
                            total[y - a] = total[y - a] + moved * taps[a]
            for y in range(rows):
                done[y, pl.ds(at, 8), lanes] = total[y]
        return carry

    lax.fori_loop(0, cols // 8, tile, 0)


def depth_kernel(in_ref, taps_ref, out_ref, wide, done):
    high, _, chans, broad = in_ref.shape
    for y in range(high):
        value = in_ref[y, 0].astype(F32)
        for h in range(wide.shape[0]):
            top = min(128, chans - h * 128)
            part = value[h * 128 : h * 128 + top]
            wide[h, y, :, 0:top] = part.T
    depth_sum(125, taps_ref, wide, done)
    for y in range(done.shape[0]):
        out_ref[y] = done[y].T[0:chans]


def tap_rows(kernel):
    chans = kernel.shape[0]
    full = -(-chans // 128) * 128
    return jnp.repeat(jnp.pad(kernel.T, ((0, 0), (0, full - chans))), 8, axis=0)


def depthwise(around, kernel):
    high, probes, chans, broad = around.shape
    rows, cols = high - 6, broad - 256
    halves = -(-chans // 128)
    taps = tap_rows(kernel)
    return pl.pallas_call(
        depth_kernel,
        grid=(probes,),
        in_specs=[
            pl.BlockSpec((high, 1, chans, broad), lambda p: (0, p, 0, 0)),
            whole(taps.shape),
        ],
        out_specs=pl.BlockSpec((rows, chans, cols), lambda p: (0, 0, p)),
        out_shape=jax.ShapeDtypeStruct((rows, chans, probes * cols), F32),
        scratch_shapes=[
            pltpu.VMEM((halves, high, broad, 128), F32),
            pltpu.VMEM((rows, cols, halves * 128), F32),
        ],
        compiler_params=params(),
        cost_estimate=cost(200 * rows * cols * chans * probes, 4 * around.size),
        name="depthwise",
    )(around, taps)


def normed_step(spread, base, sigma, gain):
    chans = spread.shape[0]
    wide_base = jnp.concatenate([base, base], axis=1)
    center = jnp.sum(spread, axis=0, keepdims=True) * (1.0 / chans)
    along = jnp.sum(wide_base * spread, axis=0, keepdims=True) * (1.0 / chans)
    scale = jnp.concatenate([sigma, sigma], axis=1)
    return (gain * scale * (spread - center - wide_base * along)).astype(BF16)


def row_edges(bands, blocks, line, lines, around, inner, sems):
    before, after, _, _ = neighbours(bands, blocks)
    pairs = []
    if line < 3:
        pairs.append((before, lines + 3 + line, 3 + line, after))
    if line >= lines - 3:
        pairs.append((after, line - (lines - 3), line - (lines - 3), before))
    return [
        (
            there,
            comes[0],
            pltpu.make_async_remote_copy(
                around.at[3 + line, :, inner, :],
                around.at[to, :, inner, :],
                sems.at[0, slot],
                sems.at[1, slot],
                device_id=where,
                device_id_type=MESH,
            ),
        )
        for (there, where), to, slot, comes in pairs
    ]


def ocean_kernel(
    bands,
    rows_sent,
    picked_ref,
    slots_ref,
    weights_ref,
    mask_ref,
    spread_ref,
    probe_ref,
    sigma_ref,
    base_ref,
    slope_ref,
    gain_ref,
    mix_ref,
    couple_ref,
    expand_ref,
    shrink_ref,
    pool_ref,
    down_ref,
    turn_ref,
    taps_ref,
    sigma_two_ref,
    base_two_ref,
    slope_two_ref,
    gain_two_ref,
    expand_two_ref,
    shrink_two_ref,
    spreadout_ref,
    up_ref,
    update_ref,
    out_ref,
    *rest,
):
    stages = len(rows_sent)
    back_refs = rest[:stages]
    (pool, flux, columns, one, coarse, around, wide, tall, done, spread_two) = rest[
        stages : stages + 10
    ]
    send, recv, flux_sems, row_sems, column_sems = rest[stages + 10 : stages + 15]
    home_sems = rest[stages + 15]
    step = pl.program_id(0)
    blocks = update_ref.shape[0]
    probes, fine, rows, cols = out_ref.shape
    lines = rows // 2
    half = cols // 2
    fields = picked_ref.shape[1]
    cap = picked_ref.shape[2]
    band, block = lax.axis_index("lat"), lax.axis_index("chan")
    before, after, chan_before, chan_after = neighbours(bands, blocks)
    inner = pl.ds(16, half)
    homes = [
        homeward(update_ref, back_refs[k], rows_sent[k][0], home_sems[k]) for k in range(stages)
    ]

    def start_home(k):
        for copy in homes[k]:
            copy.start()

    @pl.when(step == 0)
    def _():
        flux[...] = jnp.zeros_like(flux)
        around[...] = jnp.zeros_like(around)
        pool[pl.ds(band, 1)] = picked_ref[pl.ds(band, 1)]
        others = [(lax.rem(band + k, bands), block) for k in range(1, bands)]
        greet((), others + chan_peers(blocks))
        copies = []
        for k, where in enumerate(others):
            copy = pltpu.make_async_remote_copy(
                picked_ref.at[where[0]],
                pool.at[band],
                send.at[k],
                recv.at[k],
                device_id=where,
                device_id_type=MESH,
            )
            copy.start()
            copies.append(copy)
        start_home(0)
        for copy in copies:
            copy.wait()

        values = pool[...].reshape(bands * fields, cap).astype(BF16)
        place = lax.broadcasted_iota(jnp.int32, (cap, cols), 0)
        for y in range(rows):
            at = slice(y * cols, (y + 1) * cols)
            total = jnp.zeros((fields, cols), F32)
            for k in range(slots_ref.shape[0]):
                slots = slots_ref[k : k + 1, at]
                weights = weights_ref[k : k + 1, at]
                source = slots // cap
                hot = jnp.where(place == slots - source * cap, 1.0, 0.0).astype(BF16)
                found = mm(values, hot)
                for b in range(bands):
                    total = total + found[b * fields : (b + 1) * fields] * jnp.where(
                        source == b, weights, 0.0
                    )
            flux[3 + y, :, 128 : 128 + cols] = total * mask_ref[y : y + 1, :]

        center = pl.ds(128, cols)
        swap_edges(
            flux.at[pl.ds(3, 3), :, center],
            flux.at[pl.ds(rows, 3), :, center],
            flux_sems.at[0],
            before,
            after,
            flux.at[pl.ds(rows + 3, 3), :, center],
            flux.at[pl.ds(0, 3), :, center],
        )
        swap_edges(
            flux.at[:, :, pl.ds(128, 128)],
            flux.at[:, :, pl.ds(cols, 128)],
            flux_sems.at[1],
            chan_before,
            chan_after,
            flux.at[:, :, pl.ds(128 + cols, 128)],
            flux.at[:, :, pl.ds(0, 128)],
        )
        start_home(1)
        for y in range(rows + 6):
            row = flux[y]
            for b in range(7):
                columns[(y * 7 + b) * 8 : (y * 7 + b + 1) * 8, :] = row[:, 125 + b : 125 + b + cols]

    pooled = []
    for h in range(2):
        y = step * 2 + h
        near = columns[pl.ds(pl.multiple_of(y * 56, 8), 392), :].astype(BF16)
        center = columns[pl.ds(pl.multiple_of((y + 3) * 56 + 24, 8), 8), :].astype(BF16)
        spread = spread_ref[h] + jnp.concatenate(
            [mm(mix_ref[p], near) for p in range(2)], axis=1
        )
        forcing = jnp.concatenate([mm(couple_ref[p], center) for p in range(2)], axis=1)
        probe = jnp.concatenate([probe_ref[h, 0], probe_ref[h, 1]], axis=1).astype(F32)
        start = (probe + forcing).astype(BF16).astype(F32)
        at = pl.ds(y, 1)
        tangent = normed_step(spread, base_ref[h].astype(F32), sigma_ref[at, :], gain_ref[...])
        slope = slope_ref[h].astype(F32)
        hidden = mm(expand_ref[...], tangent)
        gated = (hidden * jnp.concatenate([slope, slope], axis=1)).astype(BF16)
        mask = mask_ref[at, :]
        level = (
            (start + mm(shrink_ref[...], gated)) * jnp.concatenate([mask, mask], axis=1)
        ).astype(BF16)
        one[y] = level
        pooled.append(mm(level, pool_ref[...]))

    both = (pooled[0] + pooled[1]).astype(BF16)
    coarse[step] = mm(down_ref[...], both).astype(BF16)
    turned = mm(both.T, turn_ref[...]).astype(BF16)
    for line in range(lines):

        @pl.when(step == line)
        def _(line=line):
            around[3 + line, 0, 16 : 16 + half, :] = turned[0:half]
            around[3 + line, 1, 16 : 16 + half, :] = turned[half : 2 * half]
            for there, _, copy in row_edges(bands, blocks, line, lines, around, inner, row_sems):

                @pl.when(there)
                def _(copy=copy):
                    copy.start()

    @pl.when(step == lines - 1)
    def _():
        for line in range(lines):
            for there, comes, copy in row_edges(
                bands, blocks, line, lines, around, inner, row_sems
            ):

                @pl.when(there)
                def _(copy=copy):
                    copy.wait_send()

                @pl.when(comes)
                def _(copy=copy):
                    copy.wait_recv()

        finish = start_edges(
            around.at[:, :, pl.ds(16, 16), :],
            around.at[:, :, pl.ds(half, 16), :],
            column_sems,
            chan_before,
            chan_after,
            around.at[:, :, pl.ds(16 + half, 16), :],
            around.at[:, :, pl.ds(0, 16), :],
        )
        start_home(2)
        finish()
        chans = coarse.shape[1]
        for p in range(probes):
            for y in range(tall.shape[1]):
                for h in range(tall.shape[0]):
                    tall[h, y] = around[y, p, :, h * 128 : (h + 1) * 128].astype(F32)
            depth_sum(13, taps_ref, tall, done)
            for y in range(lines):
                spread_two[y, :, p * half : (p + 1) * half] = done[y].T[0:chans]

        acts = []
        for y in range(lines):
            tangent = normed_step(
                spread_two[y],
                base_two_ref[y].astype(F32),
                sigma_two_ref[y : y + 1, :],
                gain_two_ref[...],
            )
            slope = slope_two_ref[y].astype(F32)
            hidden = mm(expand_two_ref[...], tangent)
            acts.append((hidden * jnp.concatenate([slope, slope], axis=1)).astype(BF16))
        for y in range(lines):
            two = (coarse[y].astype(F32) + mm(shrink_two_ref[...], acts[y])).astype(BF16)
            raised = mm(up_ref[...], mm(two, spreadout_ref[...]).astype(BF16))
            for h in range(2):
                line = y * 2 + h
                mask = mask_ref[line : line + 1, :]
                for p in range(probes):
                    for t in range(cols // 128):
                        lanes = slice(p * cols + t * 128, p * cols + (t + 1) * 128)
                        wide[p, t, pl.ds(line, fine, stride=rows), :] = (
                            one[line, :, lanes].astype(F32) + raised[:, lanes]
                        ) * mask[:, t * 128 : (t + 1) * 128]
        for p in range(probes):
            for t in range(cols // 128):
                out_ref[p, :, :, t * 128 : (t + 1) * 128] = (
                    wide[p, t].reshape(fine, rows, 128).astype(BF16)
                )
        for home in homes:
            for copy in home:
                copy.wait()


def ocean_levels(routed, fine_args, coarse_args, update, bands, rows_sent):
    picked, slots, weights, mask = routed
    spread, probe, sigma, base, slope = fine_args[:5]
    taps = coarse_args[0]
    down = fine_args[11]
    rows, chans, double = spread.shape
    cols = double // 2
    lines, half = rows // 2, cols // 2
    high = lines + 6
    fields = picked.shape[1]
    blocks = update.shape[0]
    row = lambda i: (i, 0, 0)
    streamed = [
        pl.BlockSpec((2, chans, double), row),
        pl.BlockSpec((2,) + probe.shape[1:], lambda i: (i, 0, 0, 0)),
        whole(sigma.shape),
        pl.BlockSpec((2, chans, cols), row),
        pl.BlockSpec((2, slope.shape[1], cols), row),
    ]
    return pl.pallas_call(
        functools.partial(ocean_kernel, bands, rows_sent),
        grid=(lines,),
        in_specs=[whole(a.shape) for a in routed]
        + streamed
        + [whole(a.shape) for a in fine_args[5:] + coarse_args]
        + [ANYWHERE],
        out_specs=[whole((2, chans, rows, cols))] + [ANYWHERE] * len(rows_sent),
        out_shape=[jax.ShapeDtypeStruct((2, chans, rows, cols), BF16)]
        + [homeward_shape(update, count) for _, count in rows_sent],
        scratch_shapes=[
            pltpu.VMEM(picked.shape, F32),
            pltpu.VMEM((rows + 6, fields, cols + 256), F32),
            pltpu.VMEM(((rows + 6) * 56, cols), F32),
            pltpu.VMEM((rows, chans, double), BF16),
            pltpu.VMEM((lines, down.shape[0], cols), BF16),
            pltpu.VMEM((high, 2, half + 32, taps.shape[1]), BF16),
            pltpu.VMEM((2, cols // 128, chans * rows, 128), F32),
            pltpu.VMEM((taps.shape[1] // 128, high, half + 32, 128), F32),
            pltpu.VMEM((lines, half, taps.shape[1]), F32),
            pltpu.VMEM((lines, down.shape[0], cols), F32),
            pltpu.SemaphoreType.DMA((bands - 1,)),
            pltpu.SemaphoreType.DMA((bands - 1,)),
            pltpu.SemaphoreType.DMA((2, 4)),
            pltpu.SemaphoreType.DMA((2, 6)),
            pltpu.SemaphoreType.DMA((4,)),
            [homeward_sems(blocks) for _ in rows_sent],
        ],
        compiler_params=params(collective_id=1, has_side_effects=True),
        cost_estimate=cost(5e9, 2e7),
        name="ocean_levels",
    )(*routed, *fine_args, *coarse_args, update)


def local(
    probe_field,
    gate_slope,
    spectral_filter,
    weight_in,
    weight_out,
    weight_flux,
    send_cells,
    recv_slots,
    recv_weights,
    ocean_probe,
    ocean_mask,
    coupling,
    base_fine,
    sigma_fine,
    slope_fine,
    gain_fine,
    kernel_fine,
    expand_fine,
    shrink_fine,
    down_proj,
    base_coarse,
    sigma_coarse,
    slope_coarse,
    gain_coarse,
    kernel_coarse,
    expand_coarse,
    shrink_coarse,
    up_proj,
):
    probes, rows, width, lons = probe_field.shape
    bands = lax.axis_size("lat")
    blocks = lax.axis_size("chan")
    part = width // bands
    pair = probes * rows
    lats = rows * bands
    chans = width * blocks
    fields = weight_flux.shape[1]

    flat_probe = probe_field.reshape(pair, width, lons)

    flux_rows = lax.dynamic_slice_in_dim(
        weight_flux, lax.axis_index("chan") * width, width, 0
    ).T
    none = jnp.zeros_like(flux_rows)
    flux_pair = jnp.concatenate(
        [
            jnp.concatenate([flux_rows, none], axis=1),
            jnp.concatenate([none, flux_rows], axis=1),
        ],
        axis=0,
    )
    terms = probe_flux(probe_field, flux_pair)

    tile_rows, tile_cols = ocean_mask.shape
    fine = ocean_probe.shape[1]
    mask = ocean_mask.astype(F32)
    start = ocean_rows(ocean_probe, ocean_mask)
    base_rows = base_fine.transpose(1, 0, 2)
    slope_rows = slope_fine.transpose(1, 0, 2)
    base_lines = base_coarse.transpose(1, 0, 2)
    slope_lines = slope_coarse.transpose(1, 0, 2)
    couple_t = coupling.T
    no_couple = jnp.zeros_like(couple_t)
    couple = jnp.stack(
        [
            jnp.concatenate([couple_t, no_couple], axis=1),
            jnp.concatenate([no_couple, couple_t], axis=1),
        ]
    )
    mix = (kernel_fine[None, :, :, None] * couple.astype(F32)[:, :, None, :]).astype(BF16)
    mix = mix.reshape(probes, fine, 49 * probes * fields)
    lane = jnp.arange(probes * tile_cols, dtype=jnp.int32)
    meets = lane[:, None] // 2 == jnp.arange(probes * tile_cols // 2, dtype=jnp.int32)[None, :]
    pool = jnp.where(meets, 0.25, 0.0).astype(BF16)
    spreadout = jnp.where(meets.T, 1.0, 0.0).astype(BF16)

    gathered, around = open_exchange(flat_probe, start, bands, blocks)

    fwd_lat, inv_lat = cosine_tables(lats)
    diff = jnp.asarray(fourier_product(lons))
    filt = lax.dynamic_slice_in_dim(spectral_filter, lax.axis_index("lat") * part, part, 1)
    gathered, filt = lax.optimization_barrier((gathered, filt))
    mixed = lat_filter(gathered, jnp.asarray(fwd_lat.T), jnp.asarray(inv_lat.T), filt, diff)
    regrouped = lax.all_to_all(
        mixed.reshape(bands * blocks, part, pair, 128),
        ("lat", "chan"),
        split_axis=0,
        concat_axis=0,
        tiled=True,
    ).reshape(chans, pair, 128)

    win = (
        weight_in.reshape(blocks, bands, part, -1).transpose(1, 0, 2, 3).reshape(chans, -1).T
    )
    folded = mm(weight_out, weight_flux).astype(BF16)
    wout = jnp.concatenate([weight_out, folded, folded], axis=1).T
    probe_terms = lax.psum_scatter(terms, "chan", scatter_dimension=0, tiled=True)
    spread = depthwise(around, kernel_fine)
    early = (
        spread,
        start,
        mask,
        win,
        wout,
        probe_terms,
        base_rows,
        slope_rows,
        base_lines,
        slope_lines,
        gain_fine[:, None],
        mix,
        couple,
        expand_fine.T,
        shrink_fine.T,
        pool,
        down_proj.T,
        jnp.pad(down_proj, ((0, 0), (0, 256 - down_proj.shape[1]))),
        tap_rows(kernel_coarse),
        gain_coarse[:, None],
        expand_coarse.T,
        shrink_coarse.T,
        spreadout,
        up_proj.T,
        send_cells[0],
        recv_slots[0],
        recv_weights[0],
    )
    regrouped, early = lax.optimization_barrier((regrouped, early))
    (
        spread,
        start,
        mask,
        win,
        wout,
        probe_terms,
        base_rows,
        slope_rows,
        base_lines,
        slope_lines,
        gain_one,
        mix,
        couple,
        expand_one,
        shrink_one,
        pool,
        down,
        turn,
        taps,
        gain_two,
        expand_two,
        shrink_two,
        spreadout,
        raise_two,
        cells,
        slots,
        weights,
    ) = early
    update, picked, *shipped = pointwise(
        regrouped, gate_slope, win, wout, probe_terms, cells, blocks, SENT_GROUPS
    )

    ocean_out, *backs = ocean_levels(
        (picked, slots, weights, mask),
        (spread, start, sigma_fine, base_rows, slope_rows, gain_one, mix, couple)
        + (expand_one, shrink_one, pool, down, turn),
        (taps, sigma_coarse, base_lines, slope_lines, gain_two, expand_two, shrink_two)
        + (spreadout, raise_two),
        update,
        bands,
        SENT,
    )
    parts = (*shipped, *backs)
    atmos_out = add_update(probe_field, parts)
    return (atmos_out, ocean_out)


def solution(mesh):
    tile = P(("lat", "chan"), None, None)
    rows_cols = P(None, "lat", "chan")
    return jax.shard_map(
        local,
        mesh=mesh,
        in_specs=(
            P(None, "lat", "chan", None),
            P("lat", None, "chan"),
            P(None, "chan"),
            P(),
            P(),
            P(),
            tile,
            tile,
            tile,
            P(None, None, "lat", "chan"),
            P("lat", "chan"),
            P(),
            rows_cols,
            P("lat", "chan"),
            rows_cols,
            P(),
            P(),
            P(),
            P(),
            P(),
            rows_cols,
            P("lat", "chan"),
            rows_cols,
            P(),
            P(),
            P(),
            P(),
            P(),
        ),
        out_specs=(P(None, "lat", "chan", None), P(None, None, "lat", "chan")),
        check_vma=False,
    )
```

```python
import functools
import math

import jax
import jax.numpy as jnp
import ml_dtypes
import numpy as np
from jax import lax
from jax.experimental import pallas as pl
from jax.experimental.pallas import tpu as pltpu
from jax.sharding import PartitionSpec as P

F32 = jnp.float32
BF16 = jnp.bfloat16
MESH = pl.DeviceIdType.MESH
VMEM_LIMIT = 56 * 1024 * 1024


def params(**more):
    return pltpu.CompilerParams(vmem_limit_bytes=VMEM_LIMIT, **more)


def cost(flops, nbytes):
    return pl.CostEstimate(flops=int(flops), bytes_accessed=int(nbytes), transcendentals=0)


def mm(a, b):
    return jnp.dot(a, b, preferred_element_type=F32)


def whole(shape):
    zeros = (0,) * len(shape)
    return pl.BlockSpec(shape, lambda *_: zeros)


def fourier_product(count):
    column = np.arange(count)
    half = count // 2
    wave = np.where(column <= half, column, column - half)
    angles = (column[:, None] * wave[None, :] % count) * (2.0 * math.pi / count)
    basis = np.where((column <= half)[None, :], np.cos(angles), np.sin(angles))
    forward = (basis / count).astype(ml_dtypes.bfloat16)
    factor = np.where((column == 0) | (column == half), 1.0, 2.0)
    inverse = (basis.T * factor[:, None]).astype(ml_dtypes.bfloat16)
    product = forward.astype(np.float64) @ inverse.astype(np.float64)
    return (product - np.eye(count)).astype(ml_dtypes.bfloat16)


def cosine_tables(count):
    degree = np.arange(count)
    phase = degree[None, :] * (2 * degree[:, None] + 1) % (4 * count)
    basis = np.cos(phase * (math.pi / (2 * count)))
    forward = (basis / count).astype(ml_dtypes.bfloat16)
    factor = np.where(degree == 0, 1.0, 2.0)
    inverse = (basis.T * factor[:, None]).astype(ml_dtypes.bfloat16)
    return (forward, inverse)


def greet(partners, more=()):
    barrier = pltpu.get_barrier_semaphore()
    for where in more:
        pl.semaphore_signal(barrier, inc=1, device_id=where, device_id_type=MESH)
    count = jnp.int32(len(more))
    for there, where in partners:

        @pl.when(there)
        def _(where=where):
            pl.semaphore_signal(barrier, inc=1, device_id=where, device_id_type=MESH)

        count = count + there.astype(jnp.int32)
    pl.semaphore_wait(barrier, count)


def start_edges(low, high, sems, before, after, low_to, high_to):
    is_before, device_before = before
    is_after, device_after = after

    def to_before():
        return pltpu.make_async_remote_copy(
            low, low_to, sems.at[0], sems.at[1], device_id=device_before, device_id_type=MESH
        )

    def to_after():
        return pltpu.make_async_remote_copy(
            high, high_to, sems.at[2], sems.at[3], device_id=device_after, device_id_type=MESH
        )

    @pl.when(is_before)
    def _():
        to_before().start()

    @pl.when(is_after)
    def _():
        to_after().start()

    def finish():
        @pl.when(is_before)
        def _():
            to_before().wait_send()
            to_after().wait_recv()

        @pl.when(is_after)
        def _():
            to_after().wait_send()
            to_before().wait_recv()

    return finish


def swap_edges(*args):
    start_edges(*args)()


def neighbours(bands, blocks):
    band, block = lax.axis_index("lat"), lax.axis_index("chan")
    return (
        (band > 0, (jnp.maximum(band - 1, 0), block)),
        (band < bands - 1, (jnp.minimum(band + 1, bands - 1), block)),
        (block > 0, (band, jnp.maximum(block - 1, 0))),
        (block < blocks - 1, (band, jnp.minimum(block + 1, blocks - 1))),
    )


def chan_peers(blocks):
    band, block = lax.axis_index("lat"), lax.axis_index("chan")
    return [(band, lax.rem(block + k, blocks)) for k in range(1, blocks)]


def homeward(update_ref, back_ref, first, sems):
    send, recv, own = sems
    blocks, _, count = back_ref.shape[:3]
    block = lax.axis_index("chan")
    some = pl.ds(first, count)
    copies = [
        pltpu.make_async_remote_copy(
            update_ref.at[where[1], :, some],
            back_ref.at[block],
            send.at[k],
            recv.at[k],
            device_id=where,
            device_id_type=MESH,
        )
        for k, where in enumerate(chan_peers(blocks))
    ]
    return copies + [
        pltpu.make_async_copy(update_ref.at[block, :, some], back_ref.at[block], own.at[0])
    ]


def homeward_sems(blocks):
    return [
        pltpu.SemaphoreType.DMA((blocks - 1,)),
        pltpu.SemaphoreType.DMA((blocks - 1,)),
        pltpu.SemaphoreType.DMA((1,)),
    ]


def homeward_shape(update, count):
    blocks, probes, _, width, lanes = update.shape
    return jax.ShapeDtypeStruct((blocks, probes, count, width, lanes), BF16)


SENT_GROUPS = 1
SENT = ((4, 4), (8, 8), (16, 8))
ANYWHERE = pl.BlockSpec(memory_space=pl.ANY)


STEPS = (
    ((0, 1), (1, 0), (0, 3), (3, 0), (1, 1), (3, 3), (1, 3), (3, 1))
    + ((0, 2), (2, 0), (2, 2), (1, 2), (2, 1), (3, 2), (2, 3))
)


def lat_partner(band, step, side):
    dz, dx = step
    return lax.rem(band // side + dz, side) * side + lax.rem(lax.rem(band, side) + dx, side)


def open_kernel(
    blocks,
    probe_ref,
    ocean_ref,
    mask_ref,
    out_ref,
    around_ref,
    start_ref,
    taken,
    wide,
    turned,
    tall,
    sems,
    own,
    edge,
):
    send, recv, load = sems
    rows, chans, lons = probe_ref.shape
    bands, part = out_ref.shape[0], out_ref.shape[1]
    side = math.isqrt(bands)
    probes, fine, lines, cols = ocean_ref.shape
    pieces, lanes = taken.shape[0], taken.shape[3]
    band, block = lax.axis_index("lat"), lax.axis_index("chan")
    lat_before, lat_after, chan_before, chan_after = neighbours(bands, blocks)

    def take(i):
        return pltpu.make_async_copy(
            probe_ref.at[:, :, pl.ds(i * lanes, lanes)], taken.at[i], load.at[i]
        )

    for i in range(pieces):
        take(i).start()
    tall[...] = jnp.zeros_like(tall)
    mask = mask_ref[...].astype(F32)
    for p in range(probes):
        for t in range(cols // 128):
            at = slice(t * 128, (t + 1) * 128)
            value = ocean_ref[p, :, :, at].astype(F32) * mask[:, at][None]
            wide[t, 0 : fine * lines, :] = value.reshape(fine * lines, 128)
            for y in range(lines):
                tall[3 + y, p, :, 128 + t * 128 : 256 + t * 128] = wide[
                    t, pl.ds(y, fine, stride=lines), :
                ].astype(BF16)
    others = [(lat_partner(band, step, side), block) for step in STEPS]
    greet((chan_before, chan_after), others)
    inner = pl.ds(128, cols)
    finish_rows = start_edges(
        tall.at[pl.ds(3, 3), :, :, inner],
        tall.at[pl.ds(lines, 3), :, :, inner],
        edge.at[0],
        lat_before,
        lat_after,
        tall.at[pl.ds(lines + 3, 3), :, :, inner],
        tall.at[pl.ds(0, 3), :, :, inner],
    )
    center = pltpu.make_async_copy(
        tall.at[pl.ds(3, lines), :, :, inner], start_ref, own.at[pieces + 1]
    )
    center.start()
    copies = []
    for i in range(pieces):
        take(i).wait()
        for t in range(lanes // 128):
            at = slice(t * 128, (t + 1) * 128)
            wide[t] = taken[i, :, :, at].astype(F32).reshape(rows * chans, 128)
            for c in range(chans):
                turned[i, c, :, at] = wide[t, pl.ds(c, rows, stride=chans), :].astype(BF16)
        columns = pl.ds(i * lanes, lanes)
        for k, where in enumerate(others):
            copy = pltpu.make_async_remote_copy(
                turned.at[i, pl.ds(where[0] * part, part)],
                out_ref.at[band, :, :, columns],
                send.at[i, k],
                recv.at[i, k],
                device_id=where,
                device_id_type=MESH,
            )
            copy.start()
            copies.append(copy)
        copy = pltpu.make_async_copy(
            turned.at[i, pl.ds(band * part, part)],
            out_ref.at[band, :, :, columns],
            own.at[i + 1],
        )
        copy.start()
        copies.append(copy)
    center.wait()
    finish_rows()
    finish_columns = start_edges(
        tall.at[:, :, :, pl.ds(128, 128)],
        tall.at[:, :, :, pl.ds(cols, 128)],
        edge.at[1],
        chan_before,
        chan_after,
        tall.at[:, :, :, pl.ds(128 + cols, 128)],
        tall.at[:, :, :, pl.ds(0, 128)],
    )
    finish_columns()
    store = pltpu.make_async_copy(tall, around_ref, own.at[0])
    store.start()
    for copy in copies:
        copy.wait()
    store.wait()


def open_exchange(probe, ocean, mask, bands, blocks):
    rows, chans, lons = probe.shape
    probes, fine, lines, cols = ocean.shape
    pieces, lanes = 4, lons // 4
    any_spec = pl.BlockSpec(memory_space=pl.ANY)
    tall = (lines + 6, probes, fine, cols + 256)
    return pl.pallas_call(
        functools.partial(open_kernel, blocks),
        in_specs=[any_spec, whole(ocean.shape), whole(mask.shape)],
        out_specs=[any_spec, any_spec, any_spec],
        out_shape=[
            jax.ShapeDtypeStruct((bands, chans // bands, rows, lons), BF16),
            jax.ShapeDtypeStruct(tall, BF16),
            jax.ShapeDtypeStruct((lines, probes, fine, cols), BF16),
        ],
        scratch_shapes=[
            pltpu.VMEM((pieces, rows, chans, lanes), BF16),
            pltpu.VMEM((lanes // 128, rows * chans, 128), F32),
            pltpu.VMEM((pieces, chans, rows, lanes), BF16),
            pltpu.VMEM(tall, BF16),
            [
                pltpu.SemaphoreType.DMA((pieces, bands - 1)),
                pltpu.SemaphoreType.DMA((pieces, bands - 1)),
                pltpu.SemaphoreType.DMA((pieces,)),
            ],
            pltpu.SemaphoreType.DMA((pieces + 2,)),
            pltpu.SemaphoreType.DMA((2, 4)),
        ],
        compiler_params=params(collective_id=3, has_side_effects=True),
        cost_estimate=cost(0, 4 * probe.size),
        name="open_exchange",
    )(probe, ocean, mask)


def probe_flux_kernel(probe_ref, weight_ref, out_ref):
    weight = weight_ref[...]
    rows = probe_ref.shape[1]
    for n in range(0, rows, 2):
        pair = [
            mm(weight, jnp.concatenate([probe_ref[0, m], probe_ref[1, m]], axis=0))
            for m in (n, n + 1)
        ]
        both = jnp.concatenate(pair, axis=0).astype(BF16)
        for j in range(out_ref.shape[0]):
            out_ref[j, n * 8 : n * 8 + 16, :] = both[:, j * 128 : (j + 1) * 128]


def probe_flux(probe, weight):
    probes, rows, chans, lons = probe.shape
    blocks = lons // 128
    step = 4
    return pl.pallas_call(
        probe_flux_kernel,
        grid=(rows // step,),
        in_specs=[
            pl.BlockSpec((probes, step, chans, lons), lambda i: (0, i, 0, 0)),
            whole(weight.shape),
        ],
        out_specs=pl.BlockSpec((blocks, step * 8, 128), lambda i: (0, i, 0)),
        out_shape=jax.ShapeDtypeStruct((blocks, rows * 8, 128), BF16),
        compiler_params=params(),
        cost_estimate=cost(2 * 8 * probe.size, 2 * probe.size),
        name="probe_flux",
    )(probe, weight)


def filter_kernel(in_ref, fwd_ref, inv_ref, filt_ref, diff_ref, out_ref, wide, back):
    bands, _, pair, lons = in_ref.shape
    rows = pair // 2
    which = lax.broadcasted_iota(jnp.int32, filt_ref.shape, 1)
    filt = jnp.sum(
        jnp.where(which == pl.program_id(0), filt_ref[...], 0.0), axis=1, keepdims=True
    )
    for b in range(bands):
        piece = in_ref[b, 0].astype(F32)
        wide[b * rows : (b + 1) * rows, 0:lons] = piece[0:rows]
        wide[b * rows : (b + 1) * rows, lons : 2 * lons] = piece[rows:pair]
    for t in range(2):
        at = slice(t * lons, (t + 1) * lons)
        value = wide[:, at]
        filtered = (mm(fwd_ref[...], value.astype(BF16)) * filt).astype(BF16)
        returned = mm(inv_ref[...], filtered)
        back[:, at] = returned.astype(BF16)
        wide[:, at] = value + returned
    for t in range(lons // 256):
        cols = slice(t * 256, (t + 1) * 256)
        mixed = [
            wide[:, p * lons + t * 256 : p * lons + (t + 1) * 256]
            + mm(back[:, p * lons : (p + 1) * lons], diff_ref[:, cols])
            for p in range(2)
        ]
        for b in range(bands):
            at = slice(b * rows, (b + 1) * rows)
            both = jnp.concatenate([mixed[0][at], mixed[1][at]], axis=0).astype(BF16)
            for j in range(2):
                out_ref[b, 2 * t + j, 0] = both[:, j * 128 : (j + 1) * 128]


def lat_filter(received, fwd, inv, filt, diff):
    bands, chans, pair, lons = received.shape
    lats = fwd.shape[0]
    blocks = lons // 128
    return pl.pallas_call(
        filter_kernel,
        grid=(chans,),
        in_specs=[
            pl.BlockSpec((bands, 1, pair, lons), lambda i: (0, i, 0, 0)),
            whole(fwd.shape),
            whole(inv.shape),
            whole(filt.shape),
            whole(diff.shape),
        ],
        out_specs=pl.BlockSpec((bands, blocks, 1, pair, 128), lambda i: (0, 0, i, 0, 0)),
        out_shape=jax.ShapeDtypeStruct((bands, blocks, chans, pair, 128), BF16),
        scratch_shapes=[pltpu.VMEM((lats, 2 * lons), F32), pltpu.VMEM((lats, 2 * lons), BF16)],
        compiler_params=params(),
        cost_estimate=cost(8.4e9, 4 * received.size),
        name="lat_filter",
    )(received, fwd, inv, filt, diff)


GROUP = 4


def point_kernel(
    sent,
    mixed_ref,
    slope_ref,
    win_ref,
    wout_ref,
    pflux_ref,
    cells_ref,
    out_ref,
    picked_ref,
    *rest,
):
    back_refs = rest[:sent]
    wide, flux, ship, home_sems = rest[sent:]
    chans, pair, lanes = mixed_ref.shape
    rows = pair // 2
    step = pl.program_id(0)
    send, recv, own = home_sems
    blocks = out_ref.shape[0]
    block = lax.axis_index("chan")
    peers = chan_peers(blocks)

    def homeward_group(i):
        copies = [
            pltpu.make_async_remote_copy(
                ship.at[i, where[1]],
                back_refs[i].at[block],
                send.at[i, k],
                recv.at[i, k],
                device_id=where,
                device_id_type=MESH,
            )
            for k, where in enumerate(peers)
        ]
        return copies + [
            pltpu.make_async_copy(ship.at[i, block], back_refs[i].at[block], own.at[i])
        ]

    @pl.when(step == 0)
    def _():
        greet((), peers)

        def load(i, carry):
            at = pl.ds(pl.multiple_of(i * 8, 8), 8)
            wide[pl.ds(pl.multiple_of(i * 8 * pair, 8), 8 * pair), :] = (
                mixed_ref[at].astype(F32).reshape(8 * pair, lanes)
            )
            return carry

        lax.fori_loop(0, chans // 8, load, 0)

    which = lax.broadcasted_iota(jnp.int32, (8, lanes), 0)
    width = out_ref.shape[3]
    gated = []
    for g in range(GROUP):
        value = jnp.concatenate(
            [
                wide[pl.ds(step * GROUP + g + p * rows, chans, stride=pair), :]
                for p in range(2)
            ],
            axis=1,
        ).astype(BF16)
        slope = slope_ref[g].astype(F32)
        hidden = mm(win_ref[...], value)
        gated.append((jnp.concatenate([slope, slope], axis=1) * hidden).astype(BF16))
    for g in range(GROUP):
        update = mm(wout_ref[...], gated[g])
        for j in range(blocks):
            piece = update[j * width : (j + 1) * width].astype(BF16)
            out_ref[j, 0, g] = piece[:, 0:lanes]
            out_ref[j, 1, g] = piece[:, lanes : 2 * lanes]
        terms = update[chans : chans + 8]
        flux[pl.ds(pl.multiple_of((step * GROUP + g) * 8, 8), 8), :] = jnp.where(
            which < 4, terms[:, 0:lanes], terms[:, lanes : 2 * lanes]
        )

    for i in range(sent):

        @pl.when(step == i)
        def _(i=i):
            ship[i] = out_ref[...]
            for copy in homeward_group(i):
                copy.start()

    @pl.when(step == rows // GROUP - 1)
    def _():
        total = flux[...]
        for j in range(pflux_ref.shape[0]):
            total = total + pflux_ref[j].astype(F32)
        total = total.astype(BF16)
        place = lax.broadcasted_iota(jnp.int32, (lanes, lanes), 0)
        for r in range(cells_ref.shape[0]):
            cells = cells_ref[r : r + 1, :]
            row = cells // lanes
            hot = jnp.where(place == cells - row * lanes, 1.0, 0.0).astype(BF16)
            found = mm(total, hot)
            picked = jnp.zeros((8, lanes), F32)
            for n in range(rows):
                picked = picked + jnp.where(row == n, found[n * 8 : (n + 1) * 8], 0.0)
            picked_ref[r] = picked
        for i in range(sent):
            for copy in homeward_group(i):
                copy.wait()


def pointwise(mixed, slope, win, wout, pflux, cells, blocks, sent):
    chans, pair, lanes = mixed.shape
    rows, hid, _ = slope.shape
    width = chans // blocks
    shipped = (sent, blocks, 2, GROUP, width, lanes)
    return pl.pallas_call(
        functools.partial(point_kernel, sent),
        grid=(rows // GROUP,),
        in_specs=[
            whole(mixed.shape),
            pl.BlockSpec((GROUP, hid, lanes), lambda i: (i, 0, 0)),
            whole(win.shape),
            whole(wout.shape),
            whole(pflux.shape),
            whole(cells.shape),
        ],
        out_specs=[
            pl.BlockSpec((blocks, 2, GROUP, width, lanes), lambda i: (0, 0, i, 0, 0)),
            whole((cells.shape[0], 8, lanes)),
        ]
        + [ANYWHERE] * sent,
        out_shape=[
            jax.ShapeDtypeStruct((blocks, 2, rows, width, lanes), BF16),
            jax.ShapeDtypeStruct((cells.shape[0], 8, lanes), F32),
        ]
        + [jax.ShapeDtypeStruct(shipped[1:], BF16)] * sent,
        scratch_shapes=[
            pltpu.VMEM((chans * pair, lanes), F32),
            pltpu.VMEM((rows * 8, lanes), F32),
            pltpu.VMEM(shipped, BF16),
            [
                pltpu.SemaphoreType.DMA((sent, blocks - 1)),
                pltpu.SemaphoreType.DMA((sent, blocks - 1)),
                pltpu.SemaphoreType.DMA((sent,)),
            ],
        ],
        compiler_params=params(collective_id=6, has_side_effects=True),
        cost_estimate=cost(7.3e9, 4 * mixed.size + 2 * slope.size),
        name="pointwise",
    )(mixed, slope, win, wout, pflux, cells)


def add_kernel(starts, probe_ref, *refs):
    out_ref = refs[-1]
    step = pl.program_id(0)
    for k, update_ref in enumerate(refs[:-1]):

        @pl.when((step >= starts[k]) & (step < starts[k + 1]))
        def _(update_ref=update_ref):
            for j in range(update_ref.shape[0]):
                cols = slice(j * 128, (j + 1) * 128)
                out_ref[:, :, :, cols] = probe_ref[:, :, :, cols] + update_ref[j]


def add_update(probe, parts):
    probes, rows, chans, lons = probe.shape
    blocks = parts[0].shape[0]
    step = 4
    counts = [a.shape[2] // step for a in parts]
    starts = [sum(counts[:k]) for k in range(len(counts) + 1)]

    def spec(k):
        return pl.BlockSpec(
            (blocks, probes, step, chans, 128),
            lambda i: (0, 0, jnp.clip(i - starts[k], 0, counts[k] - 1), 0, 0),
        )

    field = pl.BlockSpec((probes, step, chans, lons), lambda i: (0, i, 0, 0))
    return pl.pallas_call(
        functools.partial(add_kernel, starts),
        grid=(rows // step,),
        in_specs=[field] + [spec(k) for k in range(len(parts))],
        out_specs=field,
        out_shape=jax.ShapeDtypeStruct(probe.shape, BF16),
        compiler_params=params(),
        cost_estimate=cost(probe.size, 6 * probe.size),
        name="add_update",
    )(probe, *parts)


def depth_sum(first, taps_ref, wide, done):
    halves, high = wide.shape[0], wide.shape[1]
    rows, cols = done.shape[0], done.shape[1]

    def tile(i, carry):
        at = pl.multiple_of(i * 8, 8)
        for h in range(halves):
            lanes = slice(h * 128, (h + 1) * 128)
            total = [jnp.zeros((8, 128), F32) for _ in range(rows)]
            for b in range(7):
                taps = [taps_ref[(7 * a + b) * 8 : (7 * a + b + 1) * 8, lanes] for a in range(7)]
                for y in range(high):
                    moved = wide[h, y, pl.ds(at + (first + b), 8), :]
                    for a in range(7):
                        if 0 <= y - a < rows:
                            total[y - a] = total[y - a] + moved * taps[a]
            for y in range(rows):
                done[y, pl.ds(at, 8), lanes] = total[y]
        return carry

    lax.fori_loop(0, cols // 8, tile, 0)


def depth_kernel(in_ref, taps_ref, out_ref, wide, done):
    high, _, chans, broad = in_ref.shape
    for y in range(high):
        value = in_ref[y, 0].astype(F32)
        for h in range(wide.shape[0]):
            top = min(128, chans - h * 128)
            part = value[h * 128 : h * 128 + top]
            wide[h, y, :, 0:top] = part.T
    depth_sum(125, taps_ref, wide, done)
    for y in range(done.shape[0]):
        out_ref[y] = done[y].T[0:chans]


def tap_rows(kernel):
    chans = kernel.shape[0]
    full = -(-chans // 128) * 128
    return jnp.repeat(jnp.pad(kernel.T, ((0, 0), (0, full - chans))), 8, axis=0)


def depthwise(around, kernel):
    high, probes, chans, broad = around.shape
    rows, cols = high - 6, broad - 256
    halves = -(-chans // 128)
    taps = tap_rows(kernel)
    return pl.pallas_call(
        depth_kernel,
        grid=(probes,),
        in_specs=[
            pl.BlockSpec((high, 1, chans, broad), lambda p: (0, p, 0, 0)),
            whole(taps.shape),
        ],
        out_specs=pl.BlockSpec((rows, chans, cols), lambda p: (0, 0, p)),
        out_shape=jax.ShapeDtypeStruct((rows, chans, probes * cols), F32),
        scratch_shapes=[
            pltpu.VMEM((halves, high, broad, 128), F32),
            pltpu.VMEM((rows, cols, halves * 128), F32),
        ],
        compiler_params=params(),
        cost_estimate=cost(200 * rows * cols * chans * probes, 4 * around.size),
        name="depthwise",
    )(around, taps)


def normed_step(spread, base, sigma, gain):
    chans = spread.shape[0]
    wide_base = jnp.concatenate([base, base], axis=1)
    center = jnp.sum(spread, axis=0, keepdims=True) * (1.0 / chans)
    along = jnp.sum(wide_base * spread, axis=0, keepdims=True) * (1.0 / chans)
    scale = jnp.concatenate([sigma, sigma], axis=1)
    return (gain * scale * (spread - center - wide_base * along)).astype(BF16)


def row_edges(bands, blocks, line, lines, around, inner, sems):
    before, after, _, _ = neighbours(bands, blocks)
    pairs = []
    if line < 3:
        pairs.append((before, lines + 3 + line, 3 + line, after))
    if line >= lines - 3:
        pairs.append((after, line - (lines - 3), line - (lines - 3), before))
    return [
        (
            there,
            comes[0],
            pltpu.make_async_remote_copy(
                around.at[3 + line, :, inner, :],
                around.at[to, :, inner, :],
                sems.at[0, slot],
                sems.at[1, slot],
                device_id=where,
                device_id_type=MESH,
            ),
        )
        for (there, where), to, slot, comes in pairs
    ]


def ocean_kernel(
    bands,
    rows_sent,
    picked_ref,
    slots_ref,
    weights_ref,
    mask_ref,
    spread_ref,
    probe_ref,
    sigma_ref,
    base_ref,
    slope_ref,
    gain_ref,
    mix_ref,
    couple_ref,
    expand_ref,
    shrink_ref,
    pool_ref,
    down_ref,
    turn_ref,
    taps_ref,
    sigma_two_ref,
    base_two_ref,
    slope_two_ref,
    gain_two_ref,
    expand_two_ref,
    shrink_two_ref,
    spreadout_ref,
    up_ref,
    update_ref,
    out_ref,
    *rest,
):
    stages = len(rows_sent)
    back_refs = rest[:stages]
    (pool, flux, columns, one, coarse, around, wide, tall, done, spread_two) = rest[
        stages : stages + 10
    ]
    send, recv, flux_sems, row_sems, column_sems = rest[stages + 10 : stages + 15]
    home_sems = rest[stages + 15]
    step = pl.program_id(0)
    blocks = update_ref.shape[0]
    probes, fine, rows, cols = out_ref.shape
    lines = rows // 2
    half = cols // 2
    fields = picked_ref.shape[1]
    cap = picked_ref.shape[2]
    band, block = lax.axis_index("lat"), lax.axis_index("chan")
    before, after, chan_before, chan_after = neighbours(bands, blocks)
    inner = pl.ds(16, half)
    homes = [
        homeward(update_ref, back_refs[k], rows_sent[k][0], home_sems[k]) for k in range(stages)
    ]

    def start_home(k):
        for copy in homes[k]:
            copy.start()

    @pl.when(step == 0)
    def _():
        flux[...] = jnp.zeros_like(flux)
        around[...] = jnp.zeros_like(around)
        pool[pl.ds(band, 1)] = picked_ref[pl.ds(band, 1)]
        others = [(lax.rem(band + k, bands), block) for k in range(1, bands)]
        greet((), others + chan_peers(blocks))
        copies = []
        for k, where in enumerate(others):
            copy = pltpu.make_async_remote_copy(
                picked_ref.at[where[0]],
                pool.at[band],
                send.at[k],
                recv.at[k],
                device_id=where,
                device_id_type=MESH,
            )
            copy.start()
            copies.append(copy)
        start_home(0)
        for copy in copies:
            copy.wait()

        values = pool[...].reshape(bands * fields, cap).astype(BF16)
        place = lax.broadcasted_iota(jnp.int32, (cap, cols), 0)
        for y in range(rows):
            at = slice(y * cols, (y + 1) * cols)
            total = jnp.zeros((fields, cols), F32)
            for k in range(slots_ref.shape[0]):
                slots = slots_ref[k : k + 1, at]
                weights = weights_ref[k : k + 1, at]
                source = slots // cap
                hot = jnp.where(place == slots - source * cap, 1.0, 0.0).astype(BF16)
                found = mm(values, hot)
                for b in range(bands):
                    total = total + found[b * fields : (b + 1) * fields] * jnp.where(
                        source == b, weights, 0.0
                    )
            flux[3 + y, :, 128 : 128 + cols] = total * mask_ref[y : y + 1, :]

        center = pl.ds(128, cols)
        swap_edges(
            flux.at[pl.ds(3, 3), :, center],
            flux.at[pl.ds(rows, 3), :, center],
            flux_sems.at[0],
            before,
            after,
            flux.at[pl.ds(rows + 3, 3), :, center],
            flux.at[pl.ds(0, 3), :, center],
        )
        swap_edges(
            flux.at[:, :, pl.ds(128, 128)],
            flux.at[:, :, pl.ds(cols, 128)],
            flux_sems.at[1],
            chan_before,
            chan_after,
            flux.at[:, :, pl.ds(128 + cols, 128)],
            flux.at[:, :, pl.ds(0, 128)],
        )
        start_home(1)
        for y in range(rows + 6):
            row = flux[y]
            for b in range(7):
                columns[(y * 7 + b) * 8 : (y * 7 + b + 1) * 8, :] = row[:, 125 + b : 125 + b + cols]

    pooled = []
    for h in range(2):
        y = step * 2 + h
        near = columns[pl.ds(pl.multiple_of(y * 56, 8), 392), :].astype(BF16)
        center = columns[pl.ds(pl.multiple_of((y + 3) * 56 + 24, 8), 8), :].astype(BF16)
        spread = spread_ref[h] + jnp.concatenate(
            [mm(mix_ref[p], near) for p in range(2)], axis=1
        )
        forcing = jnp.concatenate([mm(couple_ref[p], center) for p in range(2)], axis=1)
        probe = jnp.concatenate([probe_ref[h, 0], probe_ref[h, 1]], axis=1).astype(F32)
        start = (probe + forcing).astype(BF16).astype(F32)
        at = pl.ds(y, 1)
        tangent = normed_step(spread, base_ref[h].astype(F32), sigma_ref[at, :], gain_ref[...])
        slope = slope_ref[h].astype(F32)
        hidden = mm(expand_ref[...], tangent)
        gated = (hidden * jnp.concatenate([slope, slope], axis=1)).astype(BF16)
        mask = mask_ref[at, :]
        level = (
            (start + mm(shrink_ref[...], gated)) * jnp.concatenate([mask, mask], axis=1)
        ).astype(BF16)
        one[y] = level
        pooled.append(mm(level, pool_ref[...]))

    both = (pooled[0] + pooled[1]).astype(BF16)
    coarse[step] = mm(down_ref[...], both).astype(BF16)
    turned = mm(both.T, turn_ref[...]).astype(BF16)
    for line in range(lines):

        @pl.when(step == line)
        def _(line=line):
            around[3 + line, 0, 16 : 16 + half, :] = turned[0:half]
            around[3 + line, 1, 16 : 16 + half, :] = turned[half : 2 * half]
            for there, _, copy in row_edges(bands, blocks, line, lines, around, inner, row_sems):

                @pl.when(there)
                def _(copy=copy):
                    copy.start()

    @pl.when(step == lines - 1)
    def _():
        for line in range(lines):
            for there, comes, copy in row_edges(
                bands, blocks, line, lines, around, inner, row_sems
            ):

                @pl.when(there)
                def _(copy=copy):
                    copy.wait_send()

                @pl.when(comes)
                def _(copy=copy):
                    copy.wait_recv()

        finish = start_edges(
            around.at[:, :, pl.ds(16, 16), :],
            around.at[:, :, pl.ds(half, 16), :],
            column_sems,
            chan_before,
            chan_after,
            around.at[:, :, pl.ds(16 + half, 16), :],
            around.at[:, :, pl.ds(0, 16), :],
        )
        start_home(2)
        finish()
        chans = coarse.shape[1]
        for p in range(probes):
            for y in range(tall.shape[1]):
                for h in range(tall.shape[0]):
                    tall[h, y] = around[y, p, :, h * 128 : (h + 1) * 128].astype(F32)
            depth_sum(13, taps_ref, tall, done)
            for y in range(lines):
                spread_two[y, :, p * half : (p + 1) * half] = done[y].T[0:chans]

        acts = []
        for y in range(lines):
            tangent = normed_step(
                spread_two[y],
                base_two_ref[y].astype(F32),
                sigma_two_ref[y : y + 1, :],
                gain_two_ref[...],
            )
            slope = slope_two_ref[y].astype(F32)
            hidden = mm(expand_two_ref[...], tangent)
            acts.append((hidden * jnp.concatenate([slope, slope], axis=1)).astype(BF16))
        for y in range(lines):
            two = (coarse[y].astype(F32) + mm(shrink_two_ref[...], acts[y])).astype(BF16)
            raised = mm(up_ref[...], mm(two, spreadout_ref[...]).astype(BF16))
            for h in range(2):
                line = y * 2 + h
                mask = mask_ref[line : line + 1, :]
                for p in range(probes):
                    for t in range(cols // 128):
                        lanes = slice(p * cols + t * 128, p * cols + (t + 1) * 128)
                        wide[p, t, pl.ds(line, fine, stride=rows), :] = (
                            one[line, :, lanes].astype(F32) + raised[:, lanes]
                        ) * mask[:, t * 128 : (t + 1) * 128]
        for p in range(probes):
            for t in range(cols // 128):
                out_ref[p, :, :, t * 128 : (t + 1) * 128] = (
                    wide[p, t].reshape(fine, rows, 128).astype(BF16)
                )
        for home in homes:
            for copy in home:
                copy.wait()


def ocean_levels(routed, fine_args, coarse_args, update, bands, rows_sent):
    picked, slots, weights, mask = routed
    spread, probe, sigma, base, slope = fine_args[:5]
    taps = coarse_args[0]
    down = fine_args[11]
    rows, chans, double = spread.shape
    cols = double // 2
    lines, half = rows // 2, cols // 2
    high = lines + 6
    fields = picked.shape[1]
    blocks = update.shape[0]
    row = lambda i: (i, 0, 0)
    streamed = [
        pl.BlockSpec((2, chans, double), row),
        pl.BlockSpec((2,) + probe.shape[1:], lambda i: (i, 0, 0, 0)),
        whole(sigma.shape),
        pl.BlockSpec((2, chans, cols), row),
        pl.BlockSpec((2, slope.shape[1], cols), row),
    ]
    return pl.pallas_call(
        functools.partial(ocean_kernel, bands, rows_sent),
        grid=(lines,),
        in_specs=[whole(a.shape) for a in routed]
        + streamed
        + [whole(a.shape) for a in fine_args[5:] + coarse_args]
        + [ANYWHERE],
        out_specs=[whole((2, chans, rows, cols))] + [ANYWHERE] * len(rows_sent),
        out_shape=[jax.ShapeDtypeStruct((2, chans, rows, cols), BF16)]
        + [homeward_shape(update, count) for _, count in rows_sent],
        scratch_shapes=[
            pltpu.VMEM(picked.shape, F32),
            pltpu.VMEM((rows + 6, fields, cols + 256), F32),
            pltpu.VMEM(((rows + 6) * 56, cols), F32),
            pltpu.VMEM((rows, chans, double), BF16),
            pltpu.VMEM((lines, down.shape[0], cols), BF16),
            pltpu.VMEM((high, 2, half + 32, taps.shape[1]), BF16),
            pltpu.VMEM((2, cols // 128, chans * rows, 128), F32),
            pltpu.VMEM((taps.shape[1] // 128, high, half + 32, 128), F32),
            pltpu.VMEM((lines, half, taps.shape[1]), F32),
            pltpu.VMEM((lines, down.shape[0], cols), F32),
            pltpu.SemaphoreType.DMA((bands - 1,)),
            pltpu.SemaphoreType.DMA((bands - 1,)),
            pltpu.SemaphoreType.DMA((2, 4)),
            pltpu.SemaphoreType.DMA((2, 6)),
            pltpu.SemaphoreType.DMA((4,)),
            [homeward_sems(blocks) for _ in rows_sent],
        ],
        compiler_params=params(collective_id=1, has_side_effects=True),
        cost_estimate=cost(5e9, 2e7),
        name="ocean_levels",
    )(*routed, *fine_args, *coarse_args, update)


def local(
    probe_field,
    gate_slope,
    spectral_filter,
    weight_in,
    weight_out,
    weight_flux,
    send_cells,
    recv_slots,
    recv_weights,
    ocean_probe,
    ocean_mask,
    coupling,
    base_fine,
    sigma_fine,
    slope_fine,
    gain_fine,
    kernel_fine,
    expand_fine,
    shrink_fine,
    down_proj,
    base_coarse,
    sigma_coarse,
    slope_coarse,
    gain_coarse,
    kernel_coarse,
    expand_coarse,
    shrink_coarse,
    up_proj,
):
    probes, rows, width, lons = probe_field.shape
    bands = lax.axis_size("lat")
    blocks = lax.axis_size("chan")
    part = width // bands
    pair = probes * rows
    lats = rows * bands
    chans = width * blocks
    fields = weight_flux.shape[1]

    flat_probe = probe_field.reshape(pair, width, lons)

    flux_rows = lax.dynamic_slice_in_dim(
        weight_flux, lax.axis_index("chan") * width, width, 0
    ).T
    none = jnp.zeros_like(flux_rows)
    flux_pair = jnp.concatenate(
        [
            jnp.concatenate([flux_rows, none], axis=1),
            jnp.concatenate([none, flux_rows], axis=1),
        ],
        axis=0,
    )
    terms = probe_flux(probe_field, flux_pair)

    tile_rows, tile_cols = ocean_mask.shape
    fine = ocean_probe.shape[1]
    mask = ocean_mask.astype(F32)
    base_rows = base_fine.transpose(1, 0, 2)
    slope_rows = slope_fine.transpose(1, 0, 2)
    base_lines = base_coarse.transpose(1, 0, 2)
    slope_lines = slope_coarse.transpose(1, 0, 2)
    couple_t = coupling.T
    no_couple = jnp.zeros_like(couple_t)
    couple = jnp.stack(
        [
            jnp.concatenate([couple_t, no_couple], axis=1),
            jnp.concatenate([no_couple, couple_t], axis=1),
        ]
    )
    mix = (kernel_fine[None, :, :, None] * couple.astype(F32)[:, :, None, :]).astype(BF16)
    mix = mix.reshape(probes, fine, 49 * probes * fields)
    lane = jnp.arange(probes * tile_cols, dtype=jnp.int32)
    meets = lane[:, None] // 2 == jnp.arange(probes * tile_cols // 2, dtype=jnp.int32)[None, :]
    pool = jnp.where(meets, 0.25, 0.0).astype(BF16)
    spreadout = jnp.where(meets.T, 1.0, 0.0).astype(BF16)

    gathered, around, start = open_exchange(
        flat_probe, ocean_probe, ocean_mask, bands, blocks
    )

    fwd_lat, inv_lat = cosine_tables(lats)
    diff = jnp.asarray(fourier_product(lons))
    filt = lax.dynamic_slice_in_dim(spectral_filter, lax.axis_index("lat") * part, part, 1)
    gathered, filt = lax.optimization_barrier((gathered, filt))
    mixed = lat_filter(gathered, jnp.asarray(fwd_lat.T), jnp.asarray(inv_lat.T), filt, diff)
    regrouped = lax.all_to_all(
        mixed.reshape(bands * blocks, part, pair, 128),
        ("lat", "chan"),
        split_axis=0,
        concat_axis=0,
        tiled=True,
    ).reshape(chans, pair, 128)

    win = (
        weight_in.reshape(blocks, bands, part, -1).transpose(1, 0, 2, 3).reshape(chans, -1).T
    )
    folded = mm(weight_out, weight_flux).astype(BF16)
    wout = jnp.concatenate([weight_out, folded, folded], axis=1).T
    probe_terms = lax.psum_scatter(terms, "chan", scatter_dimension=0, tiled=True)
    spread = depthwise(around, kernel_fine)
    early = (
        spread,
        start,
        mask,
        win,
        wout,
        probe_terms,
        base_rows,
        slope_rows,
        base_lines,
        slope_lines,
        gain_fine[:, None],
        mix,
        couple,
        expand_fine.T,
        shrink_fine.T,
        pool,
        down_proj.T,
        jnp.pad(down_proj, ((0, 0), (0, 256 - down_proj.shape[1]))),
        tap_rows(kernel_coarse),
        gain_coarse[:, None],
        expand_coarse.T,
        shrink_coarse.T,
        spreadout,
        up_proj.T,
        send_cells[0],
        recv_slots[0],
        recv_weights[0],
    )
    regrouped, early = lax.optimization_barrier((regrouped, early))
    (
        spread,
        start,
        mask,
        win,
        wout,
        probe_terms,
        base_rows,
        slope_rows,
        base_lines,
        slope_lines,
        gain_one,
        mix,
        couple,
        expand_one,
        shrink_one,
        pool,
        down,
        turn,
        taps,
        gain_two,
        expand_two,
        shrink_two,
        spreadout,
        raise_two,
        cells,
        slots,
        weights,
    ) = early
    update, picked, *shipped = pointwise(
        regrouped, gate_slope, win, wout, probe_terms, cells, blocks, SENT_GROUPS
    )

    ocean_out, *backs = ocean_levels(
        (picked, slots, weights, mask),
        (spread, start, sigma_fine, base_rows, slope_rows, gain_one, mix, couple)
        + (expand_one, shrink_one, pool, down, turn),
        (taps, sigma_coarse, base_lines, slope_lines, gain_two, expand_two, shrink_two)
        + (spreadout, raise_two),
        update,
        bands,
        SENT,
    )
    parts = (*shipped, *backs)
    atmos_out = add_update(probe_field, parts)
    return (atmos_out, ocean_out)


def solution(mesh):
    tile = P(("lat", "chan"), None, None)
    rows_cols = P(None, "lat", "chan")
    return jax.shard_map(
        local,
        mesh=mesh,
        in_specs=(
            P(None, "lat", "chan", None),
            P("lat", None, "chan"),
            P(None, "chan"),
            P(),
            P(),
            P(),
            tile,
            tile,
            tile,
            P(None, None, "lat", "chan"),
            P("lat", "chan"),
            P(),
            rows_cols,
            P("lat", "chan"),
            rows_cols,
            P(),
            P(),
            P(),
            P(),
            P(),
            rows_cols,
            P("lat", "chan"),
            rows_cols,
            P(),
            P(),
            P(),
            P(),
            P(),
        ),
        out_specs=(P(None, "lat", "chan", None), P(None, None, "lat", "chan")),
        check_vma=False,
    )
```
